32 devices in a mesh: dp: 8 (over z, x), emb: 4 (over y, core).
Axes of the slice: x: 2, y: 2, z: 4, core: 2. Of those that a mesh axis runs over, the one named last changes fastest.
Arguments:
- stem_rows: bfloat16 [1024, 4, 64, 128], P(('dp', 'emb')), may hold values from -6 to 6
- emb_ids: int32 [1024, 1], P(('dp', 'emb')), may hold values from 0 to 3; in each aligned block of 32 rows (0 to 31, 32 to 63, ...) at most 16 rows name the same one
- segments: int32 [1024, 4], P(('dp', 'emb')), may hold values from 0 to 3, as said below
- cotangent: bfloat16 [1024, 128, 128], P(('dp', 'emb')), may hold values from -6 to 6
- trunk_mats: float32 [128, 1024], replicated
- mats_momentum: float32 [128, 1024], replicated
- mats_average: float32 [128, 1024], replicated, may hold values from -0.5 to 0.5
- trunk_down: float32 [512, 128], replicated, may hold values from -0.25 to 0.25
- down_momentum: float32 [512, 128], replicated
- down_average: float32 [512, 128], replicated, may hold values from -0.25 to 0.25
- trunk_vectors: float32 [9, 128], replicated
- vectors_momentum: float32 [9, 128], replicated
- vectors_average: float32 [9, 128], replicated
- stem_mats: float32 [4, 128, 384], P('emb')
- stem_momentum: float32 [4, 128, 384], P('emb')
- stem_average: float32 [4, 128, 384], P('emb'), may hold values from -0.5 to 0.5
- stem_queries: float32 [4, 32, 128], P('emb'), may hold values from -6 to 6
- queries_momentum: float32 [4, 32, 128], P('emb')
- queries_average: float32 [4, 32, 128], P('emb'), may hold values from -6 to 6
Outputs:
- trunk_out: bfloat16 [1024, 128, 128], P(('dp', 'emb'))
- rows_grad: bfloat16 [1024, 4, 64, 128], P(('dp', 'emb'))
- mats_moment: float32 [128, 1024], replicated
- mats_mean: float32 [128, 1024], replicated
- mats_new: float32 [128, 1024], replicated
- mats_copy: bfloat16 [128, 1024], replicated
- down_moment: float32 [512, 128], replicated
- down_mean: float32 [512, 128], replicated
- down_new: float32 [512, 128], replicated
- down_copy: bfloat16 [512, 128], replicated
- vectors_moment: float32 [9, 128], replicated
- vectors_mean: float32 [9, 128], replicated
- vectors_new: float32 [9, 128], replicated
- stem_moment: float32 [4, 128, 384], P('emb')
- stem_mean: float32 [4, 128, 384], P('emb')
- stem_new: float32 [4, 128, 384], P('emb')
- stem_copy: bfloat16 [4, 128, 384], P('emb')
- queries_moment: float32 [4, 32, 128], P('emb')
- queries_mean: float32 [4, 32, 128], P('emb')
- queries_new: float32 [4, 32, 128], P('emb')
- queries_copy: bfloat16 [4, 32, 128], P('emb')
- action_stats: float32 [2, 128], replicated
The draws below stay inside these ranges and needn't reach their ends.
Inputs may be any that keep to these rules, and one draw needn't show every extreme that they name: `emb_ids`: among the 32 sequences of one device at most 16 have the same embodiment. `segments`: each row starts at 0 and rises by 0 or 1 from one step to the next; a sample is the run of steps with one id.
All inputs are finite; a program needn't handle non-finite values.
Results may differ from the reference program's by a relative error of at most 0.017.
Values may be sent and summed in bfloat16 or wider, within the bound.
No kernel may reach another device: no remote copies, remote signals or barrier semaphores. Data moves between devices by JAX's collectives and lax.ppermute only.
A program may use at most 256 MiB of HBM per device.

```python
import math
import jax
import jax.numpy as jnp
import numpy as np
from jax import lax

D = 128
FF = 512
HEADS = 8
HEAD_DIM = 16
QUERIES = 32
IN_ROWS = 64
STEPS_SEQ = 4
STEP = 4
SEQ_DEV = 32
CAP = 16
EMBODIMENTS = 4
TOK_SEQ = 128
SEQS = 1024
TOKENS = 131072
MATW = 1024
VROWS = 9


def column_scaled(key, shape, fan_in, start, stop, factor):
    base = jax.random.normal(key, shape, jnp.float32) / jnp.sqrt(jnp.float32(fan_in))
    column = jnp.arange(shape[-1])
    boost = jnp.where((column >= start) & (column < stop), factor, 1.0)
    return base * boost


def vector_rows(key):
    noise = jax.random.normal(key, (VROWS, D), jnp.float32)
    row = jnp.arange(VROWS)[:, None]
    is_gain = (row == 0) | (row == 2)
    return jnp.where(is_gain, 1.0 + 0.2 * noise, 0.3 * noise)


def state_normal(key, shape, scale):
    return jax.random.normal(key, shape, jnp.float32) * scale


def draw_segments(key, part):
    key = jax.random.fold_in(key, 1)
    starts = jax.random.randint(key, (SEQS, STEPS_SEQ - 1), 0, 2).astype(jnp.int32)
    starts = starts.at[0].set(1)
    return jnp.concatenate([jnp.zeros((SEQS, 1), jnp.int32), jnp.cumsum(starts, axis=1).astype(jnp.int32)], axis=1)


def draw_trunk_mats(key, part):
    key = jax.random.fold_in(key, 2)
    return column_scaled(key, (D, MATW), D, 3 * D, 4 * D, 4.0)


def draw_stem_mats(key, part):
    key = jax.random.fold_in(key, 3)
    return column_scaled(key, (EMBODIMENTS, D, 3 * D), D, 2 * D, 3 * D, 4.0)


def draw_trunk_vectors(key, part):
    key = jax.random.fold_in(key, 4)
    return vector_rows(key)


def draw_vectors_average(key, part):
    key = jax.random.fold_in(key, 5)
    return vector_rows(key)


def draw_mats_momentum(key, part):
    key = jax.random.fold_in(key, 6)
    return state_normal(key, (D, MATW), 0.5 * jnp.sqrt(jnp.float32(TOKENS)))


def draw_down_momentum(key, part):
    key = jax.random.fold_in(key, 7)
    return state_normal(key, (FF, D), 0.5 * jnp.sqrt(jnp.float32(TOKENS)))


def draw_vectors_momentum(key, part):
    key = jax.random.fold_in(key, 8)
    return state_normal(key, (VROWS, D), jnp.sqrt(jnp.float32(TOKENS)))


def draw_stem_momentum(key, part):
    key = jax.random.fold_in(key, 9)
    return state_normal(key, (EMBODIMENTS, D, 3 * D), 0.3 * jnp.sqrt(jnp.float32(TOKENS // EMBODIMENTS)))


def draw_queries_momentum(key, part):
    key = jax.random.fold_in(key, 10)
    return state_normal(key, (EMBODIMENTS, QUERIES, D), 2.8 * jnp.sqrt(jnp.float32(TOKENS // EMBODIMENTS)))


def levels(key, shape, shards, low, high):
    def one(position, blocks):
        steps = jax.random.uniform(jax.random.fold_in(jax.random.fold_in(key, 6), position), (blocks,), jnp.float32, low / len(shards), high / len(shards))
        return jnp.repeat(jnp.exp(steps), shape[position] // blocks).reshape((-1,) + (1,) * (len(shape) - position - 1))

    loudness = one(*shards[0])
    for cut in shards[1:]:
        loudness = loudness * one(*cut)
    return loudness


def shared_out(own_key, own, number, rows, count, top, most, lean):
    order = jax.random.permutation(own_key, count)
    heavy_load, usual = portions_of(count, rows * top, most, lean, True), portions_of(count, rows * top, most, lean, False)
    places = jnp.arange(count)

    def named(tallies, rotation):
        used = int((tallies > 0).sum())
        fixed = max(1, used // 4)
        shifted = fixed + (places - fixed + rotation * (used - fixed)) % max(1, count - fixed)
        return jnp.zeros((count,), jnp.int32).at[order[jnp.where(places < fixed, places, shifted)]].set(jnp.asarray(tallies, jnp.int32))

    tallies = jnp.where(number % 4 == 0, named(heavy_load, number // 4), named(usual, number - number // 4 - 1))
    mixed = jax.random.permutation(jax.random.fold_in(own, 3), count)
    donor, taker = mixed[0:count // 2 * 2:2], mixed[1:count // 2 * 2:2]
    margin = jnp.minimum(tallies[donor] - 1, most - tallies[taker]) // 2
    margin = jnp.where((donor == order[0]) | (taker == order[0]) | (tallies[taker] == 0), 0, jnp.maximum(margin, 0))
    shifted = jax.random.randint(jax.random.fold_in(own, 4), (count // 2,), 0, 1 << 20) % (margin + 1)
    tallies = tallies.at[donor].add(-shifted).at[taker].add(shifted)
    items = jnp.searchsorted(jnp.cumsum(tallies), jnp.arange(rows * top), side="right").astype(jnp.int32)
    grid = items.reshape(top, rows).T
    grid = grid[jax.random.permutation(jax.random.fold_in(own, 1), rows)]
    rotation = jax.random.randint(jax.random.fold_in(own, 2), (rows, 1), 0, top)
    return jnp.take_along_axis(grid, (jnp.arange(top)[None, :] + rotation) % top, axis=1)


def portions_of(amount, total, limit, skew, full):
    portions = [(1 << 20) // math.isqrt(grade ** skew) + 1 for grade in range(1, amount + 1)]
    largest = limit if full else min(limit, max(-(-total // amount), total * portions[0] // sum(portions)))
    least = 1 if total - largest >= amount - 1 else 0
    given, surplus = [largest] + [least] * (amount - 1), total - largest - least * (amount - 1)
    while surplus > 0:
        candidates = [i for i in range(1, amount) if given[i] < largest] or [i for i in range(1, amount) if given[i] < limit]
        mass, left = sum([portions[i] for i in candidates]), surplus
        for i in candidates:
            addition = min(limit - given[i], max(1, left * portions[i] // mass), surplus)
            given[i] = given[i] + addition
            surplus = surplus - addition
    return np.array(given)


def centred(own_key, extent, spread, bound, cuts=(), dtype=jnp.bfloat16):
    drawn = jax.random.normal(own_key, extent, jnp.float32) * spread
    if len(cuts) > 0:
        drawn = levels(own_key, extent, cuts, -0.22, 0.18) * drawn
    return jnp.clip(drawn, min=-bound, max=bound).astype(dtype)


def setup_inputs(seed: int = 0) -> dict:
    key_list = jax.random.split(jax.random.key(seed), 20)
    stem_rows = centred(key_list[0], (SEQS, STEPS_SEQ, IN_ROWS, D), 1.0, 6.0, ((0, 32),))
    emb_ids_keys = jax.random.split(jax.random.fold_in(key_list[1], 1), SEQS // SEQ_DEV)
    emb_ids_turns = jax.random.permutation(jax.random.fold_in(key_list[1], 3), SEQS // SEQ_DEV)
    emb_ids = jax.vmap(lambda own, number: shared_out(jax.random.fold_in(key_list[1], 2), own, number, SEQ_DEV, EMBODIMENTS, 1, CAP, 2))(emb_ids_keys, emb_ids_turns).reshape((SEQS, 1))
    segments = draw_segments(jax.random.fold_in(key_list[19], 71), 0)
    cotangent = centred(key_list[3], (SEQS, TOK_SEQ, D), 1.0, 6.0, ((0, 32),))
    trunk_mats = draw_trunk_mats(jax.random.fold_in(key_list[19], 71), 0)
    mats_momentum = draw_mats_momentum(jax.random.fold_in(key_list[19], 71), 0)
    mats_average = centred(key_list[6], (D, MATW), D ** -0.5, 0.5, (), jnp.float32)
    trunk_down = centred(key_list[7], (FF, D), FF ** -0.5, 0.25, (), jnp.float32)
    down_momentum = draw_down_momentum(jax.random.fold_in(key_list[19], 71), 0)
    down_average = centred(key_list[9], (FF, D), FF ** -0.5, 0.25, (), jnp.float32)
    trunk_vectors = draw_trunk_vectors(jax.random.fold_in(key_list[19], 71), 0)
    vectors_momentum = draw_vectors_momentum(jax.random.fold_in(key_list[19], 71), 0)
    vectors_average = draw_vectors_average(jax.random.fold_in(key_list[19], 71), 0)
    stem_mats = draw_stem_mats(jax.random.fold_in(key_list[19], 71), 0)
    stem_momentum = draw_stem_momentum(jax.random.fold_in(key_list[19], 71), 0)
    stem_average = centred(key_list[15], (EMBODIMENTS, D, 3 * D), D ** -0.5, 0.5, ((0, 4),), jnp.float32)
    stem_queries = centred(key_list[16], (EMBODIMENTS, QUERIES, D), 1.0, 6.0, ((0, 4),), jnp.float32)
    queries_momentum = draw_queries_momentum(jax.random.fold_in(key_list[19], 71), 0)
    queries_average = centred(key_list[18], (EMBODIMENTS, QUERIES, D), 1.0, 6.0, ((0, 4),), jnp.float32)
    return dict(stem_rows=stem_rows, emb_ids=emb_ids, segments=segments, cotangent=cotangent, trunk_mats=trunk_mats, mats_momentum=mats_momentum, mats_average=mats_average, trunk_down=trunk_down, down_momentum=down_momentum, down_average=down_average, trunk_vectors=trunk_vectors, vectors_momentum=vectors_momentum, vectors_average=vectors_average, stem_mats=stem_mats, stem_momentum=stem_momentum, stem_average=stem_average, stem_queries=stem_queries, queries_momentum=queries_momentum, queries_average=queries_average)


@jax.custom_vjp
def low(v):
    return lax.optimization_barrier(v.astype(jnp.bfloat16)).astype(jnp.float32)

@jax.custom_vjp
def low_back(v):
    return v

def low_keep(v):
    return (low(v), None)

def low_pass(kept, grad):
    return (grad,)

def back_keep(v):
    return (v, None)

def back_low(kept, grad):
    return (low(grad),)
low.defvjp(low_keep, low_pass)
low_back.defvjp(back_keep, back_low)
NORM_EPSILON = 1e-05
MOMENTUM_DECAY = 0.9
BASE_RATE = 0.1
MASKED_SCORE = -1000000000.0
HIGHEST_PRECISION = lax.Precision.HIGHEST

def split_heads(value):
    return value.reshape(value.shape[:-1] + (HEADS, HEAD_DIM))

def layer_norm(value, gain, bias):
    row_mean = lax.optimization_barrier(jnp.mean(value, axis=-1, keepdims=True))
    centered = value - row_mean
    variance = lax.optimization_barrier(jnp.mean(centered * centered, axis=-1, keepdims=True))
    return centered * lax.rsqrt(variance + NORM_EPSILON) * gain + bias

def stem_forward(step_rows, kv_weight, out_weight, queries):
    seq_count = step_rows.shape[0]
    score_scale = 1.0 / math.sqrt(HEAD_DIM)
    key_value = low(low_back(jnp.einsum('bsrd,bde->bsre', step_rows, kv_weight, precision=HIGHEST_PRECISION)))
    key_heads = split_heads(key_value[..., :D])
    value_heads = split_heads(key_value[..., D:])
    query_heads = split_heads(queries)
    scores = low_back(jnp.einsum('bqhc,bsrhc->bshqr', query_heads, key_heads, precision=HIGHEST_PRECISION) * score_scale)
    attend = low(jax.nn.softmax(scores, axis=-1))
    mixed_heads = jnp.einsum('bshqr,bsrhc->bsqhc', attend, value_heads, precision=HIGHEST_PRECISION)
    mixed_low = low(low_back(mixed_heads.reshape(seq_count, STEPS_SEQ, QUERIES, D)))
    result = jnp.einsum('bsqd,bde->bsqe', mixed_low, out_weight, precision=HIGHEST_PRECISION)
    return low(low_back(result)).reshape(seq_count, TOK_SEQ, D)

def trunk_forward(tokens, mats_low, down_low, vectors, seg_tokens):
    seq_count = tokens.shape[0]
    score_scale = 1.0 / math.sqrt(HEAD_DIM)
    normed = low(layer_norm(tokens, vectors[0], vectors[1]))
    projected = low(low_back(jnp.einsum('btd,de->bte', normed, mats_low[:, :3 * D], precision=HIGHEST_PRECISION)))
    query_heads = split_heads(projected[..., :D])
    key_heads = split_heads(projected[..., D:2 * D])
    value_heads = split_heads(projected[..., 2 * D:])
    scores = low_back(jnp.einsum('bqhc,bkhc->bhqk', query_heads, key_heads, precision=HIGHEST_PRECISION) * score_scale)
    visible = (seg_tokens[:, :, None] == seg_tokens[:, None, :])[:, None]
    scores = jnp.where(visible, scores, MASKED_SCORE)
    attend = low(jax.nn.softmax(scores, axis=-1))
    mixed_heads = jnp.einsum('bhqk,bkhc->bqhc', attend, value_heads, precision=HIGHEST_PRECISION)
    mixed_low = low(low_back(mixed_heads.reshape(seq_count, TOK_SEQ, D)))
    hidden = tokens + low_back(jnp.einsum('btd,de->bte', mixed_low, mats_low[:, 3 * D:4 * D], precision=HIGHEST_PRECISION))
    normed_two = low(layer_norm(hidden, vectors[2], vectors[3]))
    inner_act = low_back(jnp.einsum('btd,df->btf', normed_two, mats_low[:, 4 * D:], precision=HIGHEST_PRECISION) + vectors[5:].reshape(FF))
    active = low(jax.nn.gelu(inner_act, approximate=True))
    return hidden + low_back(jnp.einsum('btf,fd->btd', active, down_low, precision=HIGHEST_PRECISION)) + vectors[4]

def forward(params, step_rows, embodiment, seg_tokens):
    trunk_mats, trunk_down, trunk_vectors, stem_mats, stem_queries = params
    mats_low = low(trunk_mats)
    down_low = low(trunk_down)
    stem_low = low(stem_mats)
    queries_low = low(stem_queries)

    def one_block(pieces):
        rows_block, ids_block, seg_block = pieces
        chosen = stem_low[ids_block]
        tokens = stem_forward(rows_block, chosen[:, :, :2 * D], chosen[:, :, 2 * D:], queries_low[ids_block])
        return trunk_forward(tokens, mats_low, down_low, trunk_vectors, seg_block)
    block_size = min(32, SEQS)
    blocks = SEQS // block_size
    shaped = (step_rows.reshape((blocks, block_size) + step_rows.shape[1:]), embodiment.reshape(blocks, block_size), seg_tokens.reshape(blocks, block_size, TOK_SEQ))
    outputs = lax.map(jax.checkpoint(one_block), shaped)
    return outputs.reshape(SEQS, TOK_SEQ, D)

def renew(weight, moment, average, gradient, step_rate):
    new_moment = MOMENTUM_DECAY * moment + gradient
    new_weight = weight - step_rate * (gradient + MOMENTUM_DECAY * new_moment)
    new_average = average + (new_weight - average) / (STEP + 1)
    return (new_moment, new_average, new_weight)

def reference(stem_rows, emb_ids, segments, cotangent, trunk_mats, mats_momentum, mats_average, trunk_down, down_momentum, down_average, trunk_vectors, vectors_momentum, vectors_average, stem_mats, stem_momentum, stem_average, stem_queries, queries_momentum, queries_average):
    seg_tokens = jnp.repeat(segments, QUERIES, axis=1)
    embodiment = emb_ids[:, 0]
    params = (trunk_mats, trunk_down, trunk_vectors, stem_mats, stem_queries)

    def run_layers(weights, inputs):
        return forward(weights, inputs, embodiment, seg_tokens)
    outputs, pullback = jax.vjp(run_layers, params, stem_rows.astype(jnp.float32))
    weight_grads, input_grads = pullback(cotangent.astype(jnp.float32))
    out_low = outputs.astype(jnp.bfloat16)
    out_values = out_low.astype(jnp.float32).reshape(-1, D)
    feature_mean = lax.optimization_barrier(jnp.mean(out_values, axis=0))
    feature_var = lax.optimization_barrier(jnp.mean(out_values * out_values, axis=0)) - feature_mean * feature_mean
    action_stats = jnp.stack([feature_mean, feature_var])
    step_rate = BASE_RATE / math.sqrt(TOKENS)
    mats_moment, mats_mean, mats_new = renew(trunk_mats, mats_momentum, mats_average, weight_grads[0], step_rate)
    down_moment, down_mean, down_new = renew(trunk_down, down_momentum, down_average, weight_grads[1], step_rate)
    vectors_moment, vectors_mean, vectors_new = renew(trunk_vectors, vectors_momentum, vectors_average, weight_grads[2], step_rate)
    stem_moment, stem_mean, stem_new = renew(stem_mats, stem_momentum, stem_average, weight_grads[3], step_rate)
    queries_moment, queries_mean, queries_new = renew(stem_queries, queries_momentum, queries_average, weight_grads[4], step_rate)
    return (out_low, input_grads.astype(jnp.bfloat16), mats_moment, mats_mean, mats_new, mats_new.astype(jnp.bfloat16), down_moment, down_mean, down_new, down_new.astype(jnp.bfloat16), vectors_moment, vectors_mean, vectors_new, stem_moment, stem_mean, stem_new, stem_new.astype(jnp.bfloat16), queries_moment, queries_mean, queries_new, queries_new.astype(jnp.bfloat16), action_stats)
```

```python
import functools
import math

import jax
import jax.numpy as jnp
from jax import lax
from jax.experimental import pallas as pl
from jax.experimental.pallas import tpu as pltpu
from jax.sharding import PartitionSpec as P

D = 128
FF = 512
HEADS = 8
HEAD_DIM = 16
QUERIES = 32
STEPS = 4
STEP = 4
TOK_SEQ = 128
ROWS_SEQ = 256
PAIRS = HEADS // 2

NORM_EPSILON = 1e-05
MOMENTUM_DECAY = 0.9
BASE_RATE = 0.1
HIDDEN_SCORE = -1e30
SCALE = 1.0 / math.sqrt(HEAD_DIM)

TRUNK_ROWS = 384
STEM_ROWS = 416
VEC_ROWS = 32
SEND_ROWS = TRUNK_ROWS + STEM_ROWS + VEC_ROWS

BF = jnp.bfloat16
F32 = jnp.float32
VMEM_LIMIT = 56 * 1024 * 1024


def mm(a, b):
    return lax.dot_general(a, b, (((1,), (0,)), ((), ())), preferred_element_type=F32)


def mm_nt(a, b):
    return lax.dot_general(a, b, (((1,), (1,)), ((), ())), preferred_element_type=F32)


def norm_ahead(value, gain, bias):
    centered = value - jnp.mean(value, axis=0, keepdims=True)
    inverse = lax.rsqrt(jnp.mean(centered * centered, axis=0, keepdims=True) + NORM_EPSILON)
    unit = centered * inverse
    return unit * gain + bias, unit, inverse


def norm_back(gradient, gain, unit, inverse):
    grad_unit = gradient * gain
    mean_one = jnp.mean(grad_unit, axis=0, keepdims=True)
    mean_two = jnp.mean(grad_unit * unit, axis=0, keepdims=True)
    return inverse * (grad_unit - mean_one - unit * mean_two)


def softmax_rows(scores, axis):
    top = jnp.max(scores, axis=axis, keepdims=True)
    raised = jnp.exp(scores - top)
    return raised * (1.0 / jnp.sum(raised, axis=axis, keepdims=True))


def scores_back(probs, grad, axis):
    product = probs * grad
    return (product - probs * jnp.sum(product, axis=axis, keepdims=True)).astype(BF)


def head_pair(source, j):
    pieces = []
    if j:
        pieces.append(jnp.zeros((32 * j, 256), BF))
    zero = jnp.zeros((16, 128), BF)
    one = source[32 * j : 32 * j + 16]
    two = source[32 * j + 16 : 32 * j + 32]
    pieces.append(jnp.concatenate([one, zero], axis=1))
    pieces.append(jnp.concatenate([zero, two], axis=1))
    if j < PAIRS - 1:
        pieces.append(jnp.zeros((128 - 32 * j - 32, 256), BF))
    return jnp.concatenate(pieces, axis=0)


def pair_rows(source, j):
    zero = jnp.zeros((16, 128), BF)
    one = source[32 * j : 32 * j + 16]
    two = source[32 * j + 16 : 32 * j + 32]
    return jnp.concatenate(
        [jnp.concatenate([one, zero], axis=1), jnp.concatenate([zero, two], axis=1)], axis=0
    )


def pair_pick(both):
    return jnp.concatenate([both[:16, :128], both[16:, 128:]], axis=0)


def fold_lanes(value, group):
    total = value[:, :128]
    for b in range(1, group):
        total = total + value[:, 128 * b : 128 * b + 128]
    return total


def main_kernel(
    group,
    rel_ref,
    seg_ref,
    pos_ref,
    rows_ref,
    cot_ref,
    own_ref,
    one_ref,
    two_ref,
    three_ref,
    mats_ref,
    down_ref,
    vec_ref,
    out_ref,
    rgrad_ref,
    send_ref,
    vsend_ref,
    s_kv,
    s_kvT,
    s_out,
    s_outT,
    s_qb,
    t_qkvT,
    t_qkv,
    t_o,
    t_oT,
    t_in,
    t_inT,
    t_dn,
    t_dnT,
    bias_in,
    vecs,
    a_qkv,
    a_o,
    a_in,
    a_dn,
    a_bin,
    a_vec,
    a_kv,
    a_out,
    a_q,
):
    step = pl.program_id(0)

    @pl.when(step == 0)
    def _():
        head_mask = (
            lax.broadcasted_iota(jnp.int32, (256, 128), 0) // 32
            == lax.broadcasted_iota(jnp.int32, (256, 128), 1) // 16
        )
        for k, ref in enumerate((own_ref, one_ref, two_ref, three_ref)):
            wk, wv, wo = ref[0:128], ref[128:256], ref[256:384]
            s_kv[k] = jnp.concatenate([wk, wv], axis=1)
            s_kvT[k] = jnp.concatenate([wk.T, wv.T], axis=0)
            s_out[k] = wo
            s_outT[k] = wo.T
            queries = ref[384:416].astype(F32) * SCALE
            tiled = jnp.where(head_mask, jnp.concatenate([queries] * HEADS, axis=0), 0.0)
            s_qb[k] = tiled.T.astype(BF)
        mats = mats_ref[...].astype(BF)
        t_qkv[...] = mats[:, :384]
        t_qkvT[0:128] = (mats[:, 0:128].astype(F32) * SCALE).astype(BF).T
        t_qkvT[128:256] = mats[:, 128:256].T
        t_qkvT[256:384] = mats[:, 256:384].T
        t_o[...] = mats[:, 384:512]
        t_oT[...] = mats[:, 384:512].T
        t_in[...] = mats[:, 512:]
        down = down_ref[...].astype(BF)
        t_dn[...] = down
        for c in range(4):
            t_inT[128 * c : 128 * c + 128] = mats[:, 512 + 128 * c : 640 + 128 * c].T
            t_dnT[:, 128 * c : 128 * c + 128] = down[128 * c : 128 * c + 128].T
            bias_in[128 * c : 128 * c + 128] = jnp.broadcast_to(
                vec_ref[5 + c : 6 + c], (128, 128)
            ).T
        for c in range(5):
            vecs[c] = jnp.broadcast_to(vec_ref[c : c + 1], (128, 128)).T
        for ref in (a_qkv, a_o, a_in, a_dn, a_bin, a_vec, a_kv, a_out, a_q):
            ref[...] = jnp.zeros_like(ref)

    lane_block = lax.broadcasted_iota(jnp.int32, (1, 128), 1) // 32
    rels = [rel_ref[step * group + b] for b in range(group)]

    kept = []
    token_list = []
    for b in range(group):
        e = rels[b]
        rows = rows_ref[b]
        rows_T = rows.T
        kv = mm(rows, s_kv[e]).astype(BF)
        kv_T = mm(s_kvT[e], rows_T).astype(BF)
        query_block = s_qb[e]
        scores = mm(kv[:, :128], query_block)
        probs = softmax_rows(scores.reshape(STEPS, 64, 256), 1)
        probs_low = probs.astype(BF).reshape(256, 256)
        value_T = kv_T[128:]
        mixed = [jnp.zeros((16, 128), F32)] * HEADS
        half = (lax.broadcasted_iota(jnp.int32, (1, 128), 1) < 64).astype(BF)
        for t in range(2):
            both = value_T[:, 128 * t : 128 * t + 128]
            left = both * half
            made = mm(
                jnp.concatenate([left, both - left], axis=0), probs_low[128 * t : 128 * t + 128]
            )
            for u in range(2):
                s = 2 * t + u
                for h in range(HEADS):
                    c = h % 4
                    piece = made[
                        128 * u + 16 * h : 128 * u + 16 * h + 16,
                        128 * (h // 4) : 128 * (h // 4) + 128,
                    ]
                    turn = (s - c) % 4
                    if turn:
                        piece = pltpu.roll(piece, 32 * turn, 1)
                    mixed[h] = jnp.where(lane_block == s, piece, mixed[h])
        mixed_T = jnp.concatenate(mixed, axis=0).astype(BF)
        token_list.append(mm(s_outT[e], mixed_T).astype(BF))
        kept.append((rows_T, kv, kv_T, query_block, probs, probs_low, mixed_T))

    def wide(index):
        return jnp.concatenate([vecs[index]] * group, axis=1)

    residual = jnp.concatenate(token_list, axis=1).astype(F32)
    gain_one, gain_two = wide(0), wide(2)
    normed, unit_one, inverse_one = norm_ahead(residual, gain_one, wide(1))
    normed = normed.astype(BF)
    projected = mm(t_qkvT[...], normed).astype(BF)
    mixed_list, trunk_kept = [], []
    for b in range(group):
        lanes = slice(128 * b, 128 * b + 128)
        normed_tok = normed[:, lanes].T
        key_value = mm(normed_tok, t_qkv[:, 128:]).astype(BF)
        keys, values = key_value[:, :128], key_value[:, 128:]
        query_T = projected[:128, lanes]
        key_T = projected[128:256, lanes]
        value_T = projected[256:, lanes]
        base = (step * group + b) * STEPS
        marks = [seg_ref[base + s] for s in range(STEPS)]
        lane_marks = jnp.where(
            lane_block == 0,
            marks[0],
            jnp.where(
                lane_block == 1, marks[1], jnp.where(lane_block == 2, marks[2], marks[3])
            ),
        )
        lane_marks = jnp.concatenate([lane_marks] * 2, axis=1)
        hide = jnp.stack([jnp.where(lane_marks == marks[s], 0.0, HIDDEN_SCORE) for s in range(STEPS)])
        probs_list, made_list = [], []
        for j in range(PAIRS):
            scores = mm(keys, head_pair(query_T, j))
            scores = (scores.reshape(STEPS, 32, 256) + hide).reshape(128, 256)
            probs = softmax_rows(scores, 0)
            probs_low = probs.astype(BF)
            made_list.append(pair_pick(mm(value_T[32 * j : 32 * j + 32], probs_low)))
            probs_list.append((probs, probs_low))
        mixed_list.append(jnp.concatenate(made_list, axis=0).astype(BF))
        trunk_kept.append((query_T, key_T, values, probs_list))
    mixed = jnp.concatenate(mixed_list, axis=1)
    hidden = residual + mm(t_oT[...], mixed)
    normed_two, unit_two, inverse_two = norm_ahead(hidden, gain_two, wide(3))
    normed_two = normed_two.astype(BF)
    cot = jnp.concatenate([cot_ref[b].T for b in range(group)], axis=1)
    output = hidden + wide(4)
    grad_normed = jnp.zeros((128, 128 * group), F32)
    inner_const = math.sqrt(2.0 / math.pi)
    for c in range(4):
        part = slice(128 * c, 128 * c + 128)
        bias = jnp.concatenate([bias_in[part]] * group, axis=1)
        inner = mm(t_inT[part], normed_two) + bias
        square = inner * inner
        bend = jnp.tanh(inner * (inner_const + (inner_const * 0.044715) * square))
        rise = 0.5 + 0.5 * bend
        active = (inner * rise).astype(BF)
        slope = rise + (0.5 * inner) * (1.0 - bend * bend) * (
            inner_const + (3.0 * inner_const * 0.044715) * square
        )
        output = output + mm(t_dnT[:, part], active)
        a_dn[:, part] += mm_nt(cot, active)
        grad_inner = mm(t_dn[part], cot) * slope
        a_bin[part] += fold_lanes(grad_inner, group)
        grad_inner = grad_inner.astype(BF)
        a_in[:, part] += mm_nt(normed_two, grad_inner)
        grad_normed = grad_normed + mm(t_in[:, part], grad_inner)
    output = output.astype(BF)
    for b in range(group):
        out_ref[b] = output[:, 128 * b : 128 * b + 128].T
    output = output.astype(F32)
    a_vec[5] += fold_lanes(output, group)
    a_vec[6] += fold_lanes(output * output, group)

    grad_out = cot.astype(F32)
    a_vec[4] += fold_lanes(grad_out, group)
    a_vec[2] += fold_lanes(grad_normed * unit_two, group)
    a_vec[3] += fold_lanes(grad_normed, group)
    grad_hidden = grad_out + norm_back(grad_normed, gain_two, unit_two, inverse_two)
    grad_branch = grad_hidden.astype(BF)
    a_o[...] += mm_nt(mixed, grad_branch)
    grad_mixed = mm(t_o[...], grad_branch).astype(BF)
    grad_list = []
    for b in range(group):
        query_T, key_T, values, probs_list = trunk_kept[b]
        grad_T = grad_mixed[:, 128 * b : 128 * b + 128]
        grad_queries, grad_keys, grad_values = [], [], []
        for j in range(PAIRS):
            probs, probs_low = probs_list[j]
            grad_probs = mm(values, head_pair(grad_T, j))
            grad_scores = scores_back(probs, grad_probs, 0)
            grad_queries.append(pair_pick(mm(key_T[32 * j : 32 * j + 32], grad_scores)))
            grad_keys.append(mm_nt(pair_rows(query_T, j), grad_scores))
            grad_values.append(mm_nt(pair_rows(grad_T, j), probs_low))
        grad_queries = jnp.concatenate(grad_queries, axis=0) * SCALE
        grad_list.append(
            jnp.concatenate([grad_queries] + grad_keys + grad_values, axis=0).astype(BF)
        )
    grad_projected = jnp.concatenate(grad_list, axis=1)
    a_qkv[...] += mm_nt(normed, grad_projected)
    grad_normed = mm(t_qkv[...], grad_projected)
    a_vec[0] += fold_lanes(grad_normed * unit_one, group)
    a_vec[1] += fold_lanes(grad_normed, group)
    grad_tokens = (grad_hidden + norm_back(grad_normed, gain_one, unit_one, inverse_one)).astype(BF)

    for b in range(group):
        e = rels[b]
        rows_T, kv, kv_T, query_block, probs, probs_low, mixed_T = kept[b]
        grad_T = grad_tokens[:, 128 * b : 128 * b + 128]
        a_out[e] += mm_nt(mixed_T, grad_T)
        grad_mixed = mm(s_out[e], grad_T)
        turned = [grad_mixed.astype(BF)] + [
            pltpu.roll(grad_mixed, 32 * k, 1).astype(BF) for k in range(1, 4)
        ]
        masks = [(lane_block == c).astype(BF) for c in range(4)]
        zero = jnp.zeros((16, 128), BF)
        grad_values, grad_scores = [], []
        for s in range(STEPS):
            pieces = []
            for h in range(HEADS):
                c = h % 4
                piece = turned[(c - s) % 4][16 * h : 16 * h + 16] * masks[c]
                pieces.append(
                    jnp.concatenate([piece, zero] if h < 4 else [zero, piece], axis=1)
                )
            spread = jnp.concatenate(pieces, axis=0)
            here = slice(64 * s, 64 * s + 64)
            grad_probs = mm(kv[here, 128:], spread)
            grad_scores.append(scores_back(probs[s], grad_probs, 0))
            grad_values.append(mm_nt(probs_low[here], spread))
        grad_scores = jnp.concatenate(grad_scores, axis=0)
        grad_values = jnp.concatenate(grad_values, axis=0).astype(BF)
        grad_keys = mm_nt(grad_scores, query_block).astype(BF)
        a_q[e] += mm(kv_T[:128], grad_scores)
        grad_kv = jnp.concatenate([grad_keys, grad_values], axis=1)
        a_kv[e] += mm(rows_T, grad_kv)
        rgrad_ref[b] = mm_nt(grad_kv, s_kv[e]).astype(BF)

    @pl.when(step == pl.num_programs(0) - 1)
    def _():
        me = pos_ref[0]
        count = send_ref.shape[0]
        blocks = [a_qkv[:, 128 * c : 128 * c + 128] for c in range(3)]
        blocks.append(a_o[...])
        blocks += [a_in[:, 128 * c : 128 * c + 128] for c in range(4)]
        blocks += [a_dn[:, 128 * c : 128 * c + 128].T for c in range(4)]
        per = len(blocks) // count
        for j in range(count):
            place = lax.rem(j - me + count, count)
            for i in range(per):
                send_ref[place, 128 * i : 128 * i + 128] = blocks[per * j + i].astype(BF)
        head_mask = (
            lax.broadcasted_iota(jnp.int32, (256, 128), 0) // 32
            == lax.broadcasted_iota(jnp.int32, (256, 128), 1) // 16
        )
        sums = [jnp.sum(a_vec[c].T, axis=0, keepdims=True) for c in range(5)]
        sums += [
            jnp.sum(a_bin[128 * c : 128 * c + 128].T, axis=0, keepdims=True) for c in range(4)
        ]
        sums += [jnp.sum(a_vec[c].T, axis=0, keepdims=True) for c in (5, 6)]
        sums.append(jnp.zeros((5, 128), F32))
        sums = jnp.concatenate(sums, axis=0)
        high = sums.astype(BF)
        low = (sums - high.astype(F32)).astype(BF)
        vsend_ref[...] = sums
        for k in range(count):
            send_ref[k, 384:512] = a_kv[k, :, :128].astype(BF)
            send_ref[k, 512:640] = a_kv[k, :, 128:].astype(BF)
            send_ref[k, 640:768] = a_out[k].astype(BF)
            spread = jnp.where(head_mask, a_q[k].T, 0.0)
            query = spread[0:32]
            for h in range(1, HEADS):
                query = query + spread[32 * h : 32 * h + 32]
            send_ref[k, 768:800] = (query * SCALE).astype(BF)
            send_ref[k, 800:816] = high
            send_ref[k, 816:832] = low


def split_sum(sums):
    high = sums.astype(BF)
    return high, (sums - high.astype(F32)).astype(BF)


def owner_kernel(shards, pos_ref, *refs):
    out_ref, scratch = refs[-2], refs[-1]
    total = refs[0][0].astype(F32)
    for ref in refs[1:-2]:
        total = total + ref[...].astype(F32)
    scratch[...] = total
    rows = SEND_ROWS // shards
    sums = scratch[800:816] + scratch[816:832]
    high, low = split_sum(sums)
    me = pos_ref[1]
    for j in range(shards):
        place = lax.rem(j - me + shards, shards)
        out_ref[place, 32 : 32 + rows] = scratch[rows * j : rows * j + rows].astype(BF)
        out_ref[place, 0:16] = high
        out_ref[place, 16:32] = low


def shard_kernel(*refs):
    own_ref, vec_ref = refs[-2:]
    total = refs[0][0].astype(F32)
    for ref in refs[1:-2]:
        total = total + ref[...].astype(F32)
    own_ref[...] = total[32:].astype(BF)
    vec_ref[...] = total[0:16] + total[16:32]


def place_kernel(pos_ref, *refs):
    out_ref = refs[-1]
    shards = len(refs) - 1
    me = pos_ref[1]
    for k, ref in enumerate(refs[:-1]):
        out_ref[lax.rem(me - k + shards, shards)] = ref[...]


def renew(weight, moment, average, gradient, step_rate):
    new_moment = MOMENTUM_DECAY * moment + gradient
    new_weight = weight - step_rate * (gradient + MOMENTUM_DECAY * new_moment)
    new_average = average + (new_weight - average) / (STEP + 1)
    return (new_moment, new_average, new_weight)


def renew_kernel(token_total, pos_ref, *refs):
    trunk_refs, stem_ref, sums_ref = refs[0:4], refs[4], refs[5]
    groups = [refs[6 + 3 * i : 9 + 3 * i] for i in range(5)]
    outs = refs[21:41]
    pieces = refs[41]
    mats_o, down_o, vec_o, stem_o, quer_o = outs[0:4], outs[4:8], outs[8:11], outs[11:15], outs[15:19]
    stats_o = outs[19]
    rate = BASE_RATE / math.sqrt(token_total)
    me = pos_ref[0]
    count = len(trunk_refs)
    for k, ref in enumerate(trunk_refs):
        pieces[lax.rem(me - k + count, count)] = ref[...].astype(F32)

    def block(i):
        return pieces[i // 3, 128 * (i % 3) : 128 * (i % 3) + 128]

    def put(out, where, made):
        out[0][where], out[1][where], out[2][where] = made
        if len(out) > 3:
            out[3][where] = made[2].astype(BF)

    def take(ins, where):
        return [ref[where] for ref in ins]

    for i in range(8):
        where = (slice(None), slice(128 * i, 128 * i + 128))
        put(mats_o, where, renew(*take(groups[0], where), block(i), rate))
    for i in range(4):
        where = (slice(128 * i, 128 * i + 128), slice(None))
        put(down_o, where, renew(*take(groups[1], where), block(8 + i), rate))
    where = (slice(None), slice(None))
    put(vec_o, where, renew(*take(groups[2], where), sums_ref[0:9], rate))
    for i in range(3):
        where = (slice(None), slice(128 * i, 128 * i + 128))
        grad = stem_ref[128 * i : 128 * i + 128].astype(F32)
        put(stem_o, where, renew(*take(groups[3], where), grad, rate))
    where = (slice(None), slice(None))
    put(quer_o, where, renew(*take(groups[4], where), stem_ref[384:416].astype(F32), rate))
    mean = sums_ref[9:10] / token_total
    stats_o[0:1] = mean
    stats_o[1:2] = sums_ref[10:11] / token_total - mean * mean


def vmem_call(kernel, outs, scratch=(), scalars=1):
    in_vmem = pl.BlockSpec(memory_space=pltpu.VMEM)

    def call(*args):
        return pl.pallas_call(
            kernel,
            out_shape=outs,
            in_specs=[pl.BlockSpec(memory_space=pltpu.SMEM)] * scalars
            + [in_vmem] * (len(args) - scalars),
            out_specs=jax.tree.map(lambda _: in_vmem, outs),
            scratch_shapes=list(scratch),
            compiler_params=pltpu.CompilerParams(vmem_limit_bytes=VMEM_LIMIT),
        )(*args)

    return call


def local(
    stem_rows,
    emb_ids,
    segments,
    cotangent,
    trunk_mats,
    mats_momentum,
    mats_average,
    trunk_down,
    down_momentum,
    down_average,
    trunk_vectors,
    vectors_momentum,
    vectors_average,
    stem_mats,
    stem_momentum,
    stem_average,
    stem_queries,
    queries_momentum,
    queries_average,
):
    seqs = stem_rows.shape[0]
    emb_count, dp_count = lax.axis_size("emb"), lax.axis_size("dp")
    emb_me, dp_me = lax.axis_index("emb"), lax.axis_index("dp")
    pos = jnp.stack([emb_me, dp_me]).astype(jnp.int32)
    rel = lax.rem(emb_ids[:, 0] - emb_me + emb_count, emb_count)
    token_total = seqs * TOK_SEQ * dp_count * emb_count

    def shift(value, axis, count, by):
        return lax.ppermute(value, axis, [(i, (i + by) % count) for i in range(count)])

    low = stem_mats[0].astype(BF)
    own = jnp.concatenate(
        [low[:, :D], low[:, D : 2 * D], low[:, 2 * D :], stem_queries[0].astype(BF)], axis=0
    )
    stems = [own] + [shift(own, "emb", emb_count, -k) for k in range(1, emb_count)]

    group = 2
    grid = seqs // group

    def whole(shape):
        return pl.BlockSpec(shape, lambda i, *_: (0,) * len(shape))

    scratch = [
        ((4, 128, 256), BF),
        ((4, 256, 128), BF),
        ((4, 128, 128), BF),
        ((4, 128, 128), BF),
        ((4, 128, 256), BF),
        ((384, 128), BF),
        ((128, 384), BF),
        ((128, 128), BF),
        ((128, 128), BF),
        ((128, 512), BF),
        ((512, 128), BF),
        ((512, 128), BF),
        ((128, 512), BF),
        ((512, 128), F32),
        ((5, 128, 128), F32),
        ((128, 384), F32),
        ((128, 128), F32),
        ((128, 512), F32),
        ((128, 512), F32),
        ((512, 128), F32),
        ((7, 128, 128), F32),
        ((4, 128, 256), F32),
        ((4, 128, 128), F32),
        ((4, 128, 256), F32),
    ]
    output, rows_grad, send, _ = pl.pallas_call(
        functools.partial(main_kernel, group),
        out_shape=(
            jax.ShapeDtypeStruct((seqs, TOK_SEQ, D), BF),
            jax.ShapeDtypeStruct((seqs, ROWS_SEQ, D), BF),
            jax.ShapeDtypeStruct((emb_count, SEND_ROWS, D), BF),
            jax.ShapeDtypeStruct((16, D), F32),
        ),
        grid_spec=pltpu.PrefetchScalarGridSpec(
            num_scalar_prefetch=3,
            grid=(grid,),
            in_specs=[
                pl.BlockSpec((group, ROWS_SEQ, D), lambda i, *_: (i, 0, 0)),
                pl.BlockSpec((group, TOK_SEQ, D), lambda i, *_: (i, 0, 0)),
            ]
            + [whole((STEM_ROWS, D))] * 4
            + [whole((D, 1024)), whole((FF, D)), whole((9, D))],
            out_specs=(
                pl.BlockSpec((group, TOK_SEQ, D), lambda i, *_: (i, 0, 0)),
                pl.BlockSpec((group, ROWS_SEQ, D), lambda i, *_: (i, 0, 0)),
                whole((emb_count, SEND_ROWS, D)),
                whole((16, D)),
            ),
            scratch_shapes=[pltpu.VMEM(shape, dtype) for shape, dtype in scratch],
        ),
        compiler_params=pltpu.CompilerParams(
            vmem_limit_bytes=VMEM_LIMIT, dimension_semantics=("arbitrary",)
        ),
    )(
        rel,
        segments.reshape(-1),
        pos,
        stem_rows.reshape(seqs, ROWS_SEQ, D),
        cotangent,
        *stems,
        trunk_mats,
        trunk_down,
        trunk_vectors,
    )

    shard_rows = SEND_ROWS // dp_count
    arrived = [shift(send[k], "emb", emb_count, k) for k in range(1, emb_count)]
    first = pl.BlockSpec((1, SEND_ROWS, D), lambda i: (0, 0, 0))
    in_vmem = pl.BlockSpec(memory_space=pltpu.VMEM)
    shards = pl.pallas_call(
        functools.partial(owner_kernel, dp_count),
        grid=(1,),
        out_shape=jax.ShapeDtypeStruct((dp_count, 32 + shard_rows, D), BF),
        in_specs=[pl.BlockSpec(memory_space=pltpu.SMEM), first] + [in_vmem] * len(arrived),
        out_specs=in_vmem,
        scratch_shapes=[pltpu.VMEM((SEND_ROWS, D), F32)],
        compiler_params=pltpu.CompilerParams(vmem_limit_bytes=VMEM_LIMIT),
    )(pos, send, *arrived)
    arrived = [shift(shards[k], "dp", dp_count, k) for k in range(1, dp_count)]
    first = pl.BlockSpec((1, 32 + shard_rows, D), lambda i: (0, 0, 0))
    shard, sums = pl.pallas_call(
        shard_kernel,
        grid=(1,),
        out_shape=(
            jax.ShapeDtypeStruct((shard_rows, D), BF),
            jax.ShapeDtypeStruct((16, D), F32),
        ),
        in_specs=[first] + [in_vmem] * len(arrived),
        out_specs=(in_vmem, in_vmem),
        compiler_params=pltpu.CompilerParams(vmem_limit_bytes=VMEM_LIMIT),
    )(shards, *arrived)
    all_shards = [shard] + [shift(shard, "dp", dp_count, k) for k in range(1, dp_count)]
    placed = vmem_call(
        place_kernel, jax.ShapeDtypeStruct((dp_count, shard_rows, D), BF)
    )(pos, *all_shards).reshape(SEND_ROWS, D)
    trunk = placed[:TRUNK_ROWS]
    trunks = [trunk] + [shift(trunk, "emb", emb_count, k) for k in range(1, emb_count)]
    stem = placed[TRUNK_ROWS : TRUNK_ROWS + STEM_ROWS]

    def like(array, copy):
        made = [jax.ShapeDtypeStruct(array.shape, F32)] * 3
        return made + ([jax.ShapeDtypeStruct(array.shape, BF)] if copy else [])

    outs = (
        like(trunk_mats, True)
        + like(trunk_down, True)
        + like(trunk_vectors, False)
        + like(stem_mats[0], True)
        + like(stem_queries[0], True)
        + [jax.ShapeDtypeStruct((2, D), F32)]
    )
    made = vmem_call(
        functools.partial(renew_kernel, token_total),
        outs,
        [pltpu.VMEM((emb_count, TRUNK_ROWS, D), F32)],
    )(
        pos,
        *trunks,
        stem,
        sums,
        trunk_mats,
        mats_momentum,
        mats_average,
        trunk_down,
        down_momentum,
        down_average,
        trunk_vectors,
        vectors_momentum,
        vectors_average,
        stem_mats[0],
        stem_momentum[0],
        stem_average[0],
        stem_queries[0],
        queries_momentum[0],
        queries_average[0],
    )
    made = list(made[:11]) + [part[None] for part in made[11:19]] + [made[19]]
    return (output, rows_grad.reshape(stem_rows.shape), *made)


def solution(mesh):
    split = P(("dp", "emb"))
    stem = P("emb")
    in_specs = (split,) * 4 + (P(),) * 9 + (stem,) * 6
    out_specs = (split,) * 2 + (P(),) * 11 + (stem,) * 8 + (P(),)
    return jax.shard_map(local, mesh=mesh, in_specs=in_specs, out_specs=out_specs, check_vma=False)
```

```python
import functools
import math

import jax
import jax.numpy as jnp
from jax import lax
from jax.experimental import pallas as pl
from jax.experimental.pallas import tpu as pltpu
from jax.sharding import PartitionSpec as P

D = 128
FF = 512
HEADS = 8
HEAD_DIM = 16
QUERIES = 32
STEPS = 4
STEP = 4
TOK_SEQ = 128
ROWS_SEQ = 256
PAIRS = HEADS // 2

NORM_EPSILON = 1e-05
MOMENTUM_DECAY = 0.9
BASE_RATE = 0.1
HIDDEN_SCORE = -1e30
SCALE = 1.0 / math.sqrt(HEAD_DIM)
LOG2E = math.log2(math.e)

TRUNK_ROWS = 384
STEM_ROWS = 416
VEC_ROWS = 32
SEND_ROWS = TRUNK_ROWS + STEM_ROWS + VEC_ROWS

BF = jnp.bfloat16
F32 = jnp.float32
VMEM_LIMIT = 56 * 1024 * 1024


def mm(a, b):
    return lax.dot_general(a, b, (((1,), (0,)), ((), ())), preferred_element_type=F32)


def mm_nt(a, b):
    return lax.dot_general(a, b, (((1,), (1,)), ((), ())), preferred_element_type=F32)


def norm_ahead(value, gain, bias):
    centered = value - jnp.mean(value, axis=0, keepdims=True)
    inverse = lax.rsqrt(jnp.mean(centered * centered, axis=0, keepdims=True) + NORM_EPSILON)
    unit = centered * inverse
    return unit * gain + bias, unit, inverse


def norm_back(gradient, gain, unit, inverse):
    grad_unit = gradient * gain
    mean_one = jnp.mean(grad_unit, axis=0, keepdims=True)
    mean_two = jnp.mean(grad_unit * unit, axis=0, keepdims=True)
    return inverse * (grad_unit - mean_one - unit * mean_two)


def softmax_rows(scores, axis):
    top = jnp.max(scores, axis=axis, keepdims=True)
    raised = jnp.exp(scores - top)
    return raised * (1.0 / jnp.sum(raised, axis=axis, keepdims=True))


def scores_back(probs, grad, axis):
    product = probs * grad
    return (product - probs * jnp.sum(product, axis=axis, keepdims=True)).astype(BF)


def head_pair(source, j):
    pieces = []
    if j:
        pieces.append(jnp.zeros((32 * j, 256), BF))
    zero = jnp.zeros((16, 128), BF)
    one = source[32 * j : 32 * j + 16]
    two = source[32 * j + 16 : 32 * j + 32]
    pieces.append(jnp.concatenate([one, zero], axis=1))
    pieces.append(jnp.concatenate([zero, two], axis=1))
    if j < PAIRS - 1:
        pieces.append(jnp.zeros((128 - 32 * j - 32, 256), BF))
    return jnp.concatenate(pieces, axis=0)


def pair_rows(source, j):
    zero = jnp.zeros((16, 128), BF)
    one = source[32 * j : 32 * j + 16]
    two = source[32 * j + 16 : 32 * j + 32]
    return jnp.concatenate(
        [jnp.concatenate([one, zero], axis=1), jnp.concatenate([zero, two], axis=1)], axis=0
    )


def pair_pick(both):
    return jnp.concatenate([both[:16, :128], both[16:, 128:]], axis=0)


def fold_lanes(value, group):
    total = value[:, :128]
    for b in range(1, group):
        total = total + value[:, 128 * b : 128 * b + 128]
    return total


def main_kernel(
    group,
    rel_ref,
    seg_ref,
    pos_ref,
    rows_ref,
    cot_ref,
    own_ref,
    one_ref,
    two_ref,
    three_ref,
    mats_ref,
    down_ref,
    vec_ref,
    out_ref,
    rgrad_ref,
    send_ref,
    vsend_ref,
    s_kv,
    s_out,
    s_outT,
    s_qb,
    t_qkvT,
    t_qkv,
    t_o,
    t_oT,
    t_in,
    t_inT,
    t_dn,
    t_dnT,
    bias_in,
    vecs,
    a_qkv,
    a_o,
    a_in,
    a_dn,
    a_vec,
    a_kv,
    a_out,
    a_q,
):
    step = pl.program_id(0)

    @pl.when(step == 0)
    def _():
        head_mask = (
            lax.broadcasted_iota(jnp.int32, (256, 128), 0) // 32
            == lax.broadcasted_iota(jnp.int32, (256, 128), 1) // 16
        )
        for k, ref in enumerate((own_ref, one_ref, two_ref, three_ref)):
            wk, wv, wo = ref[0:128], ref[128:256], ref[256:384]
            s_kv[k] = jnp.concatenate([wk, wv], axis=1)
            s_out[k] = wo
            s_outT[k] = wo.T
            queries = ref[384:416].astype(F32) * (SCALE * LOG2E)
            tiled = jnp.where(head_mask, jnp.concatenate([queries] * HEADS, axis=0), 0.0)
            s_qb[k] = tiled.T.astype(BF)
        mats = mats_ref[...].astype(BF)
        t_qkv[...] = mats[:, :384]
        for c in range(3):
            t_qkvT[128 * c : 128 * c + 128] = mats[:, 128 * c : 128 * c + 128].T
        t_o[...] = mats[:, 384:512]
        t_oT[...] = mats[:, 384:512].T
        t_in[...] = mats[:, 512:]
        down = down_ref[...].astype(BF)
        t_dn[...] = down
        for c in range(4):
            t_inT[128 * c : 128 * c + 128] = mats[:, 512 + 128 * c : 640 + 128 * c].T
            t_dnT[:, 128 * c : 128 * c + 128] = down[128 * c : 128 * c + 128].T
            bias_in[128 * c : 128 * c + 128] = jnp.broadcast_to(
                vec_ref[5 + c : 6 + c], (128, 128)
            ).T
        for c in range(5):
            vecs[c] = jnp.broadcast_to(vec_ref[c : c + 1], (128, 128)).T
        for ref in (a_qkv, a_o, a_in, a_dn, a_vec, a_kv, a_out, a_q):
            ref[...] = jnp.zeros_like(ref)

    lane_block = lax.broadcasted_iota(jnp.int32, (1, 128), 1) // 32
    rels = [rel_ref[step * group + b] for b in range(group)]
    ones = jnp.ones((16, 128), BF)

    every = range(group)
    kv = [mm(rows_ref[b], s_kv[rels[b]]).astype(BF) for b in every]
    scores = [
        [mm(kv[b][64 * s : 64 * s + 64, :128], s_qb[rels[b]]) for s in range(STEPS)] for b in every
    ]
    half = (lax.broadcasted_iota(jnp.int32, (1, 128), 1) < 64).astype(BF)
    value_T = [kv[b][:, 128:].T for b in every]
    probs, probs_low = [], []
    for b in every:
        probs.append([])
        probs_low.append([])
        for s in range(STEPS):
            halves = []
            for u in range(2):
                tile = scores[b][s][:, 128 * u : 128 * u + 128]
                raised = jnp.exp2(tile - jnp.max(tile, axis=0, keepdims=True))
                halves.append(raised * (1.0 / jnp.sum(raised, axis=0, keepdims=True)))
            probs[b].append(halves)
            probs_low[b].append(jnp.concatenate([half.astype(BF) for half in halves], axis=1))
    made = []
    for b in every:
        made.append([])
        for t in range(2):
            both = value_T[b][:, 128 * t : 128 * t + 128]
            left = both * half
            made[b].append(
                mm(
                    jnp.concatenate([left, both - left], axis=0),
                    jnp.concatenate(probs_low[b][2 * t : 2 * t + 2], axis=0),
                )
            )
    stem_mixed = []
    for b in every:
        rows = []
        for h in range(HEADS):
            c = h % 4
            row = jnp.zeros((16, 128), F32)
            for s in range(STEPS):
                start = 128 * (s % 2) + 16 * h
                piece = made[b][s // 2][start : start + 16, 128 * (h // 4) : 128 * (h // 4) + 128]
                turn = (s - c) % 4
                if turn:
                    piece = pltpu.roll(piece, 32 * turn, 1)
                row = jnp.where(lane_block == s, piece, row)
            rows.append(row)
        stem_mixed.append(jnp.concatenate(rows, axis=0).astype(BF))
    tokens = [mm(s_outT[rels[b]], stem_mixed[b]).astype(BF) for b in every]

    residual, normed_list, unit_one, inverse_one = [], [], [], []
    for b in every:
        residual.append(tokens[b].astype(F32))
        ahead, unit, inverse = norm_ahead(residual[b], vecs[0], vecs[1])
        normed_list.append(ahead.astype(BF))
        unit_one.append(unit)
        inverse_one.append(inverse)
    normed = jnp.concatenate(normed_list, axis=1)
    projected = mm(t_qkvT[...], normed)
    lanes = [slice(128 * b, 128 * b + 128) for b in every]
    query_T = [(projected[:128, lanes[b]] * (LOG2E * SCALE)).astype(BF) for b in every]
    key_T = [projected[128:256, lanes[b]].astype(BF) for b in every]
    value_T = [projected[256:, lanes[b]].astype(BF) for b in every]
    keys = [key_T[b].T for b in every]
    values = [value_T[b].T for b in every]
    hide = []
    for b in every:
        base = (step * group + b) * STEPS
        marks = [seg_ref[base + s] for s in range(STEPS)]
        lane_marks = jnp.where(
            lane_block == 0,
            marks[0],
            jnp.where(
                lane_block == 1, marks[1], jnp.where(lane_block == 2, marks[2], marks[3])
            ),
        )
        hide.append([jnp.where(lane_marks == marks[s], 0.0, HIDDEN_SCORE) for s in range(STEPS)])
    scores = [[mm(keys[b], head_pair(query_T[b], j)) for j in range(PAIRS)] for b in every]
    cot_list = [cot_ref[b].T for b in every]
    raised = []
    for b in every:
        raised.append([])
        for j in range(PAIRS):
            halves = []
            for u in range(2):
                tile = scores[b][j][:, 128 * u : 128 * u + 128]
                tile = jnp.concatenate(
                    [tile[32 * s : 32 * s + 32] + hide[b][s] for s in range(STEPS)], axis=0
                )
                halves.append(
                    jnp.exp2(tile - jnp.max(tile, axis=0, keepdims=True)).astype(BF)
                )
            raised[b].append(jnp.concatenate(halves, axis=1))
    made = [
        [
            mm(jnp.concatenate([value_T[b][32 * j : 32 * j + 32], ones], axis=0), raised[b][j])
            for j in range(PAIRS)
        ]
        for b in every
    ]
    head_mixed, head_inverse, mixed_list = [], [], []
    for b in every:
        head_mixed.append([])
        head_inverse.append([])
        for h in range(HEADS):
            j, u = divmod(h, 2)
            here = slice(128 * u, 128 * u + 128)
            inverse = 1.0 / made[b][j][32:40, here]
            part = made[b][j][16 * u : 16 * u + 16, here]
            head_inverse[b].append(inverse)
            head_mixed[b].append(
                jnp.concatenate([part[:8] * inverse, part[8:] * inverse], axis=0)
            )
        mixed_list.append(jnp.concatenate(head_mixed[b], axis=0).astype(BF))
    mixed = jnp.concatenate(mixed_list, axis=1)
    branch = mm(t_oT[...], mixed)
    hidden, normed_list, unit_two, inverse_two = [], [], [], []
    for b in every:
        hidden.append(residual[b] + branch[:, lanes[b]])
        ahead, unit, inverse = norm_ahead(hidden[b], vecs[2], vecs[3])
        normed_list.append(ahead.astype(BF))
        unit_two.append(unit)
        inverse_two.append(inverse)
    normed_two = jnp.concatenate(
        [jnp.concatenate(normed_list, axis=1), jnp.ones((16, 128 * group), BF)], axis=0
    )
    cot = jnp.concatenate(cot_list, axis=1)
    c0 = math.sqrt(2.0 / math.pi)
    c1 = c0 * 0.044715
    inner_all = mm(t_inT[...], normed_two[:128])
    grad_all = mm(t_dn[...], cot)
    active_rows, grad_rows = [], []
    for r in range(0, FF, 16):
        bias = bias_in[r : r + 16]
        active_cols, grad_cols = [], []
        for b in every:
            inner = inner_all[r : r + 16, lanes[b]] + bias
            square = inner * inner
            bend = jnp.tanh(inner * (c0 + c1 * square))
            rise = 0.5 + 0.5 * bend
            active = inner * rise
            slope = rise + (active - active * rise) * (2.0 * c0 + (6.0 * c1) * square)
            active_cols.append(active.astype(BF))
            grad_cols.append((grad_all[r : r + 16, lanes[b]] * slope).astype(BF))
        active_rows.append(jnp.concatenate(active_cols, axis=1))
        grad_rows.append(jnp.concatenate(grad_cols, axis=1))
    active = jnp.concatenate(active_rows, axis=0)
    grad_inner = jnp.concatenate(grad_rows, axis=0)
    grad_all = mm(t_in[...], grad_inner)
    output_all = mm(t_dnT[...], active)
    a_dn[...] += mm_nt(cot, active)
    a_in[...] += mm_nt(normed_two, grad_inner)

    grad_hidden = []
    for b in every:
        grad_out = cot_list[b].astype(F32)
        grad_normed = grad_all[:, lanes[b]]
        a_vec[4] += grad_out
        a_vec[2] += grad_normed * unit_two[b]
        a_vec[3] += grad_normed
        grad_hidden.append(
            grad_out + norm_back(grad_normed, vecs[2], unit_two[b], inverse_two[b])
        )
    grad_branch = jnp.concatenate([part.astype(BF) for part in grad_hidden], axis=1)
    grad_mixed = mm(t_o[...], grad_branch)
    a_o[...] += mm_nt(mixed, grad_branch)
    for b in every:
        output = (hidden[b] + output_all[:, lanes[b]] + vecs[4]).astype(BF)
        out_ref[b] = output.T
        output = output.astype(F32)
        a_vec[5] += output
        a_vec[6] += output * output
    grad_T, drops = [], []
    for b in every:
        scaled = []
        drops.append([])
        for h in range(HEADS):
            inverse = head_inverse[b][h]
            part = grad_mixed[16 * h : 16 * h + 16, lanes[b]]
            part = jnp.concatenate([part[:8] * inverse, part[8:] * inverse], axis=0).astype(BF)
            scaled.append(part)
            drops[b].append(jnp.sum(part.astype(F32) * head_mixed[b][h], axis=0, keepdims=True))
        grad_T.append(jnp.concatenate(scaled, axis=0))
    grad_probs = [[mm(values[b], head_pair(grad_T[b], j)) for j in range(PAIRS)] for b in every]
    grad_values = [
        [mm_nt(pair_rows(grad_T[b], j), raised[b][j]) for j in range(PAIRS)] for b in every
    ]
    grad_scores = []
    for b in every:
        grad_scores.append([])
        for j in range(PAIRS):
            halves = []
            for u in range(2):
                here = slice(128 * u, 128 * u + 128)
                tile = grad_probs[b][j][:, here] - drops[b][2 * j + u]
                halves.append(tile.astype(BF) * raised[b][j][:, here])
            grad_scores[b].append(jnp.concatenate(halves, axis=1))
    grad_queries = [
        [pair_pick(mm(key_T[b][32 * j : 32 * j + 32], grad_scores[b][j])) for j in range(PAIRS)]
        for b in every
    ]
    grad_keys = [
        [mm_nt(pair_rows(query_T[b], j), grad_scores[b][j]) for j in range(PAIRS)] for b in every
    ]
    grad_list = []
    for b in every:
        grad_list.append(
            jnp.concatenate(
                [
                    (jnp.concatenate(grad_queries[b], axis=0) * SCALE).astype(BF),
                    (jnp.concatenate(grad_keys[b], axis=0) * (1.0 / LOG2E)).astype(BF),
                    jnp.concatenate(grad_values[b], axis=0).astype(BF),
                ],
                axis=0,
            )
        )
    grad_projected = jnp.concatenate(grad_list, axis=1)
    grad_all = mm(t_qkv[...], grad_projected)
    a_qkv[...] += mm_nt(normed, grad_projected)
    grad_tokens = []
    for b in every:
        grad_normed = grad_all[:, lanes[b]]
        a_vec[0] += grad_normed * unit_one[b]
        a_vec[1] += grad_normed
        grad_tokens.append(
            (grad_hidden[b] + norm_back(grad_normed, vecs[0], unit_one[b], inverse_one[b])).astype(BF)
        )

    grad_mixed = [mm(s_out[rels[b]], grad_tokens[b]) for b in every]
    for b in every:
        a_out[rels[b]] += mm_nt(stem_mixed[b], grad_tokens[b])
    masks = [(lane_block == c).astype(BF) for c in range(4)]
    zero = jnp.zeros((16, 128), BF)
    spread = []
    for b in every:
        spread.append([])
        turned = [grad_mixed[b].astype(BF)] + [
            pltpu.roll(grad_mixed[b], 32 * k, 1).astype(BF) for k in range(1, 4)
        ]
        for s in range(STEPS):
            pieces = []
            for h in range(HEADS):
                c = h % 4
                piece = turned[(c - s) % 4][16 * h : 16 * h + 16] * masks[c]
                pieces.append(
                    jnp.concatenate([piece, zero] if h < 4 else [zero, piece], axis=1)
                )
            spread[b].append(jnp.concatenate(pieces, axis=0))
    grad_probs = [
        [mm(kv[b][64 * s : 64 * s + 64, 128:], spread[b][s]) for s in range(STEPS)] for b in every
    ]
    grad_values = [
        jnp.concatenate(
            [mm_nt(probs_low[b][s], spread[b][s]).astype(BF) for s in range(STEPS)], axis=0
        )
        for b in every
    ]
    grad_scores = []
    for b in every:
        steps = []
        for s in range(STEPS):
            steps.append(
                jnp.concatenate(
                    [
                        scores_back(probs[b][s][u], grad_probs[b][s][:, 128 * u : 128 * u + 128], 0)
                        for u in range(2)
                    ],
                    axis=1,
                )
            )
        grad_scores.append(jnp.concatenate(steps, axis=0))
    grad_keys = [
        (mm_nt(grad_scores[b], s_qb[rels[b]]) * (1.0 / LOG2E)).astype(BF) for b in every
    ]
    keys_T = [kv[b][:, :128].T for b in every]
    rows_T = [rows_ref[b].T for b in every]
    for b in every:
        a_q[rels[b]] += mm(keys_T[b], grad_scores[b])
    grad_kv = [jnp.concatenate([grad_keys[b], grad_values[b]], axis=1) for b in every]
    for b in every:
        rgrad_ref[b] = mm_nt(grad_kv[b], s_kv[rels[b]]).astype(BF)
    for b in every:
        a_kv[rels[b]] += mm(rows_T[b], grad_kv[b])

    @pl.when(step == pl.num_programs(0) - 1)
    def _():
        me = pos_ref[0]
        count = send_ref.shape[0]
        blocks = [a_qkv[:, 128 * c : 128 * c + 128] for c in range(3)]
        blocks.append(a_o[...])
        blocks += [a_in[0:128, 128 * c : 128 * c + 128] for c in range(4)]
        blocks += [a_dn[:, 128 * c : 128 * c + 128].T for c in range(4)]
        per = len(blocks) // count
        for j in range(count):
            place = lax.rem(j - me + count, count)
            for i in range(per):
                send_ref[place, 128 * i : 128 * i + 128] = blocks[per * j + i].astype(BF)
        head_mask = (
            lax.broadcasted_iota(jnp.int32, (256, 128), 0) // 32
            == lax.broadcasted_iota(jnp.int32, (256, 128), 1) // 16
        )
        sums = [jnp.sum(a_vec[c].T, axis=0, keepdims=True) for c in range(5)]
        sums += [a_in[128:129, 128 * c : 128 * c + 128] for c in range(4)]
        sums += [jnp.sum(a_vec[c].T, axis=0, keepdims=True) for c in (5, 6)]
        sums.append(jnp.zeros((5, 128), F32))
        sums = jnp.concatenate(sums, axis=0)
        high = sums.astype(BF)
        low = (sums - high.astype(F32)).astype(BF)
        vsend_ref[...] = sums
        for k in range(count):
            send_ref[k, 384:512] = a_kv[k, :, :128].astype(BF)
            send_ref[k, 512:640] = a_kv[k, :, 128:].astype(BF)
            send_ref[k, 640:768] = a_out[k].astype(BF)
            spread = jnp.where(head_mask, a_q[k].T, 0.0)
            query = spread[0:32]
            for h in range(1, HEADS):
                query = query + spread[32 * h : 32 * h + 32]
            send_ref[k, 768:800] = (query * SCALE).astype(BF)
            send_ref[k, 800:816] = high
            send_ref[k, 816:832] = low


def split_sum(sums):
    high = sums.astype(BF)
    return high, (sums - high.astype(F32)).astype(BF)


def owner_kernel(shards, pos_ref, *refs):
    out_ref, scratch = refs[-2], refs[-1]
    total = refs[0][0].astype(F32)
    for ref in refs[1:-2]:
        total = total + ref[...].astype(F32)
    scratch[...] = total
    rows = SEND_ROWS // shards
    sums = scratch[800:816] + scratch[816:832]
    high, low = split_sum(sums)
    me = pos_ref[1]
    for j in range(shards):
        place = lax.rem(j - me + shards, shards)
        out_ref[place, 32 : 32 + rows] = scratch[rows * j : rows * j + rows].astype(BF)
        out_ref[place, 0:16] = high
        out_ref[place, 16:32] = low


def shard_kernel(*refs):
    own_ref, vec_ref = refs[-2:]
    total = refs[0][0].astype(F32)
    for ref in refs[1:-2]:
        total = total + ref[...].astype(F32)
    own_ref[...] = total[32:].astype(BF)
    vec_ref[...] = total[0:16] + total[16:32]


def place_kernel(pos_ref, *refs):
    out_ref = refs[-1]
    shards = len(refs) - 1
    me = pos_ref[1]
    for k, ref in enumerate(refs[:-1]):
        out_ref[lax.rem(me - k + shards, shards)] = ref[...]


def renew(weight, moment, average, gradient, step_rate):
    new_moment = MOMENTUM_DECAY * moment + gradient
    new_weight = weight - step_rate * (gradient + MOMENTUM_DECAY * new_moment)
    new_average = average + (new_weight - average) / (STEP + 1)
    return (new_moment, new_average, new_weight)


def renew_kernel(token_total, pos_ref, *refs):
    trunk_refs, stem_ref, sums_ref = refs[0:4], refs[4], refs[5]
    groups = [refs[6 + 3 * i : 9 + 3 * i] for i in range(5)]
    outs = refs[21:41]
    pieces = refs[41]
    mats_o, down_o, vec_o, stem_o, quer_o = outs[0:4], outs[4:8], outs[8:11], outs[11:15], outs[15:19]
    stats_o = outs[19]
    rate = BASE_RATE / math.sqrt(token_total)
    me = pos_ref[0]
    count = len(trunk_refs)
    for k, ref in enumerate(trunk_refs):
        pieces[lax.rem(me - k + count, count)] = ref[...].astype(F32)

    def block(i):
        return pieces[i // 3, 128 * (i % 3) : 128 * (i % 3) + 128]

    def put(out, where, made):
        out[0][where], out[1][where], out[2][where] = made
        if len(out) > 3:
            out[3][where] = made[2].astype(BF)

    def take(ins, where):
        return [ref[where] for ref in ins]

    for i in range(8):
        where = (slice(None), slice(128 * i, 128 * i + 128))
        put(mats_o, where, renew(*take(groups[0], where), block(i), rate))
    for i in range(4):
        where = (slice(128 * i, 128 * i + 128), slice(None))
        put(down_o, where, renew(*take(groups[1], where), block(8 + i), rate))
    where = (slice(None), slice(None))
    put(vec_o, where, renew(*take(groups[2], where), sums_ref[0:9], rate))
    for i in range(3):
        where = (slice(None), slice(128 * i, 128 * i + 128))
        grad = stem_ref[128 * i : 128 * i + 128].astype(F32)
        put(stem_o, where, renew(*take(groups[3], where), grad, rate))
    where = (slice(None), slice(None))
    put(quer_o, where, renew(*take(groups[4], where), stem_ref[384:416].astype(F32), rate))
    mean = sums_ref[9:10] / token_total
    stats_o[0:1] = mean
    stats_o[1:2] = sums_ref[10:11] / token_total - mean * mean


def vmem_call(kernel, outs, scratch=(), scalars=1):
    in_vmem = pl.BlockSpec(memory_space=pltpu.VMEM)

    def call(*args):
        return pl.pallas_call(
            kernel,
            out_shape=outs,
            in_specs=[pl.BlockSpec(memory_space=pltpu.SMEM)] * scalars
            + [in_vmem] * (len(args) - scalars),
            out_specs=jax.tree.map(lambda _: in_vmem, outs),
            scratch_shapes=list(scratch),
            compiler_params=pltpu.CompilerParams(vmem_limit_bytes=VMEM_LIMIT),
        )(*args)

    return call


def local(
    stem_rows,
    emb_ids,
    segments,
    cotangent,
    trunk_mats,
    mats_momentum,
    mats_average,
    trunk_down,
    down_momentum,
    down_average,
    trunk_vectors,
    vectors_momentum,
    vectors_average,
    stem_mats,
    stem_momentum,
    stem_average,
    stem_queries,
    queries_momentum,
    queries_average,
):
    seqs = stem_rows.shape[0]
    emb_count, dp_count = lax.axis_size("emb"), lax.axis_size("dp")
    emb_me, dp_me = lax.axis_index("emb"), lax.axis_index("dp")
    pos = jnp.stack([emb_me, dp_me]).astype(jnp.int32)
    rel = lax.rem(emb_ids[:, 0] - emb_me + emb_count, emb_count)
    token_total = seqs * TOK_SEQ * dp_count * emb_count

    def shift(value, axis, count, by):
        return lax.ppermute(value, axis, [(i, (i + by) % count) for i in range(count)])

    low = stem_mats[0].astype(BF)
    own = jnp.concatenate(
        [low[:, :D], low[:, D : 2 * D], low[:, 2 * D :], stem_queries[0].astype(BF)], axis=0
    )
    stems = [own] + [shift(own, "emb", emb_count, -k) for k in range(1, emb_count)]

    group = 4
    grid = seqs // group

    def whole(shape):
        return pl.BlockSpec(shape, lambda i, *_: (0,) * len(shape))

    scratch = [
        ((4, 128, 256), BF),
        ((4, 128, 128), BF),
        ((4, 128, 128), BF),
        ((4, 128, 256), BF),
        ((384, 128), BF),
        ((128, 384), BF),
        ((128, 128), BF),
        ((128, 128), BF),
        ((128, 512), BF),
        ((512, 128), BF),
        ((512, 128), BF),
        ((128, 512), BF),
        ((512, 128), F32),
        ((5, 128, 128), F32),
        ((128, 384), F32),
        ((128, 128), F32),
        ((144, 512), F32),
        ((128, 512), F32),
        ((7, 128, 128), F32),
        ((4, 128, 256), F32),
        ((4, 128, 128), F32),
        ((4, 128, 256), F32),
    ]
    output, rows_grad, send, _ = pl.pallas_call(
        functools.partial(main_kernel, group),
        out_shape=(
            jax.ShapeDtypeStruct((seqs, TOK_SEQ, D), BF),
            jax.ShapeDtypeStruct((seqs, ROWS_SEQ, D), BF),
            jax.ShapeDtypeStruct((emb_count, SEND_ROWS, D), BF),
            jax.ShapeDtypeStruct((16, D), F32),
        ),
        grid_spec=pltpu.PrefetchScalarGridSpec(
            num_scalar_prefetch=3,
            grid=(grid,),
            in_specs=[
                pl.BlockSpec((group, ROWS_SEQ, D), lambda i, *_: (i, 0, 0)),
                pl.BlockSpec((group, TOK_SEQ, D), lambda i, *_: (i, 0, 0)),
            ]
            + [whole((STEM_ROWS, D))] * 4
            + [whole((D, 1024)), whole((FF, D)), whole((9, D))],
            out_specs=(
                pl.BlockSpec((group, TOK_SEQ, D), lambda i, *_: (i, 0, 0)),
                pl.BlockSpec((group, ROWS_SEQ, D), lambda i, *_: (i, 0, 0)),
                whole((emb_count, SEND_ROWS, D)),
                whole((16, D)),
            ),
            scratch_shapes=[pltpu.VMEM(shape, dtype) for shape, dtype in scratch],
        ),
        compiler_params=pltpu.CompilerParams(
            vmem_limit_bytes=VMEM_LIMIT, dimension_semantics=("arbitrary",)
        ),
    )(
        rel,
        segments.reshape(-1),
        pos,
        stem_rows.reshape(seqs, ROWS_SEQ, D),
        cotangent,
        *stems,
        trunk_mats,
        trunk_down,
        trunk_vectors,
    )

    shard_rows = SEND_ROWS // dp_count
    arrived = [shift(send[k], "emb", emb_count, k) for k in range(1, emb_count)]
    first = pl.BlockSpec((1, SEND_ROWS, D), lambda i: (0, 0, 0))
    in_vmem = pl.BlockSpec(memory_space=pltpu.VMEM)
    shards = pl.pallas_call(
        functools.partial(owner_kernel, dp_count),
        grid=(1,),
        out_shape=jax.ShapeDtypeStruct((dp_count, 32 + shard_rows, D), BF),
        in_specs=[pl.BlockSpec(memory_space=pltpu.SMEM), first] + [in_vmem] * len(arrived),
        out_specs=in_vmem,
        scratch_shapes=[pltpu.VMEM((SEND_ROWS, D), F32)],
        compiler_params=pltpu.CompilerParams(vmem_limit_bytes=VMEM_LIMIT),
    )(pos, send, *arrived)
    arrived = [shift(shards[k], "dp", dp_count, k) for k in range(1, dp_count)]
    first = pl.BlockSpec((1, 32 + shard_rows, D), lambda i: (0, 0, 0))
    shard, sums = pl.pallas_call(
        shard_kernel,
        grid=(1,),
        out_shape=(
            jax.ShapeDtypeStruct((shard_rows, D), BF),
            jax.ShapeDtypeStruct((16, D), F32),
        ),
        in_specs=[first] + [in_vmem] * len(arrived),
        out_specs=(in_vmem, in_vmem),
        compiler_params=pltpu.CompilerParams(vmem_limit_bytes=VMEM_LIMIT),
    )(shards, *arrived)
    all_shards = [shard] + [shift(shard, "dp", dp_count, k) for k in range(1, dp_count)]
    placed = vmem_call(
        place_kernel, jax.ShapeDtypeStruct((dp_count, shard_rows, D), BF)
    )(pos, *all_shards).reshape(SEND_ROWS, D)
    trunk = placed[:TRUNK_ROWS]
    trunks = [trunk] + [shift(trunk, "emb", emb_count, k) for k in range(1, emb_count)]
    stem = placed[TRUNK_ROWS : TRUNK_ROWS + STEM_ROWS]

    def like(array, copy):
        made = [jax.ShapeDtypeStruct(array.shape, F32)] * 3
        return made + ([jax.ShapeDtypeStruct(array.shape, BF)] if copy else [])

    outs = (
        like(trunk_mats, True)
        + like(trunk_down, True)
        + like(trunk_vectors, False)
        + like(stem_mats[0], True)
        + like(stem_queries[0], True)
        + [jax.ShapeDtypeStruct((2, D), F32)]
    )
    made = vmem_call(
        functools.partial(renew_kernel, token_total),
        outs,
        [pltpu.VMEM((emb_count, TRUNK_ROWS, D), F32)],
    )(
        pos,
        *trunks,
        stem,
        sums,
        trunk_mats,
        mats_momentum,
        mats_average,
        trunk_down,
        down_momentum,
        down_average,
        trunk_vectors,
        vectors_momentum,
        vectors_average,
        stem_mats[0],
        stem_momentum[0],
        stem_average[0],
        stem_queries[0],
        queries_momentum[0],
        queries_average[0],
    )
    made = list(made[:11]) + [part[None] for part in made[11:19]] + [made[19]]
    return (output, rows_grad.reshape(stem_rows.shape), *made)


def solution(mesh):
    split = P(("dp", "emb"))
    stem = P("emb")
    in_specs = (split,) * 4 + (P(),) * 9 + (stem,) * 6
    out_specs = (split,) * 2 + (P(),) * 11 + (stem,) * 8 + (P(),)
    return jax.shard_map(local, mesh=mesh, in_specs=in_specs, out_specs=out_specs, check_vma=False)
```

```python
import functools
import math

import jax
import jax.numpy as jnp
from jax import lax
from jax.experimental import pallas as pl
from jax.experimental.pallas import tpu as pltpu
from jax.sharding import PartitionSpec as P

D = 128
FF = 512
HEADS = 8
HEAD_DIM = 16
QUERIES = 32
STEPS = 4
STEP = 4
TOK_SEQ = 128
ROWS_SEQ = 256
PAIRS = HEADS // 2

NORM_EPSILON = 1e-05
MOMENTUM_DECAY = 0.9
BASE_RATE = 0.1
HIDDEN_SCORE = -1e30
LAG = 1
SCALE = 1.0 / math.sqrt(HEAD_DIM)
LOG2E = math.log2(math.e)

TRUNK_ROWS = 384
STEM_ROWS = 416
VEC_ROWS = 32
PIECE_ROWS = TRUNK_ROWS + STEM_ROWS

BF = jnp.bfloat16
F32 = jnp.float32
VMEM_LIMIT = 56 * 1024 * 1024


def mm(a, b):
    return lax.dot_general(a, b, (((1,), (0,)), ((), ())), preferred_element_type=F32)


def mm_nt(a, b):
    return lax.dot_general(a, b, (((1,), (1,)), ((), ())), preferred_element_type=F32)


def scores_back(probs, grad, axis):
    product = probs * grad
    return (product - probs * jnp.sum(product, axis=axis, keepdims=True)).astype(BF)


def head_pair(source, j):
    pieces = []
    if j:
        pieces.append(jnp.zeros((32 * j, 256), BF))
    zero = jnp.zeros((16, 128), BF)
    one = source[32 * j : 32 * j + 16]
    two = source[32 * j + 16 : 32 * j + 32]
    pieces.append(jnp.concatenate([one, zero], axis=1))
    pieces.append(jnp.concatenate([zero, two], axis=1))
    if j < PAIRS - 1:
        pieces.append(jnp.zeros((128 - 32 * j - 32, 256), BF))
    return jnp.concatenate(pieces, axis=0)


def pair_rows(source, j):
    zero = jnp.zeros((16, 128), BF)
    one = source[32 * j : 32 * j + 16]
    two = source[32 * j + 16 : 32 * j + 32]
    return jnp.concatenate(
        [jnp.concatenate([one, zero], axis=1), jnp.concatenate([zero, two], axis=1)], axis=0
    )


def pair_pick(both):
    return jnp.concatenate([both[:16, :128], both[16:, 128:]], axis=0)


def main_kernel(
    group,
    rel_ref,
    seg_ref,
    pos_ref,
    rows_ref,
    cot_ref,
    own_ref,
    one_ref,
    two_ref,
    three_ref,
    mats_ref,
    down_ref,
    vec_ref,
    out_ref,
    rgrad_ref,
    keep_ref,
    give_ref,
    sums_ref,
    s_k,
    s_qb,
    s_a,
    s_a2,
    s_v,
    s_vT,
    s_out,
    s_outT,
    t_qkvT,
    t_qkv,
    t_o,
    t_oT,
    t_in,
    t_inT,
    t_dn,
    t_dnT,
    vecs,
    a_qkv,
    a_o,
    a_in,
    a_dn,
    a_vec,
    a_a,
    a_v,
    a_out,
):
    step = pl.program_id(0)

    head_mask = (
        lax.broadcasted_iota(jnp.int32, (256, 128), 0) // 32
        == lax.broadcasted_iota(jnp.int32, (256, 128), 1) // 16
    )

    @pl.when(step == 0)
    def _():
        for k, ref in enumerate((own_ref, one_ref, two_ref, three_ref)):
            wk, wv, wo = ref[0:128], ref[128:256], ref[256:384]
            queries = ref[384:416].astype(F32)
            tiled = jnp.where(head_mask, jnp.concatenate([queries] * HEADS, axis=0), 0.0)
            block = tiled.T.astype(BF)
            both = mm(wk, block) * SCALE
            s_k[k] = wk
            s_qb[k] = block
            s_a[k] = both.astype(BF)
            s_a2[k] = (both * LOG2E).astype(BF)
            s_v[k] = wv
            s_vT[k] = wv.T
            s_out[k] = wo
            s_outT[k] = wo.T
        mats = mats_ref[...].astype(BF)
        for c in range(5):
            vecs[c] = jnp.broadcast_to(vec_ref[c : c + 1], (128, 128)).T
        corner = lax.broadcasted_iota(jnp.int32, (128, 16), 1)

        def beside(column):
            column = jnp.broadcast_to(column, (128, 16))
            high = column.astype(BF).astype(F32)
            return jnp.where(corner == 0, high, jnp.where(corner == 1, column - high, 0.0)).astype(BF)

        for c in range(7):
            where = 128 * c if c < 3 else 128 * (c + 1)
            block = mats[:, where : where + 128].astype(F32)
            gain, bias = (vecs[0], vecs[1]) if c < 3 else (vecs[2], vecs[3])
            scaled = (block * gain).astype(BF)
            shift = jnp.sum((block * bias).T, axis=1, keepdims=True)
            if c < 3:
                t_qkv[:, 128 * c : 128 * c + 128] = scaled
                t_qkvT[128 * c : 128 * c + 128, 0:128] = scaled.T
                t_qkvT[128 * c : 128 * c + 128, 128:144] = beside(shift)
            else:
                d = c - 3
                shift = shift + jnp.broadcast_to(vec_ref[5 + d : 6 + d], (128, 128)).T[:, 0:1]
                t_in[:, 128 * d : 128 * d + 128] = scaled
                t_inT[128 * d : 128 * d + 128, 0:128] = scaled.T
                t_inT[128 * d : 128 * d + 128, 128:144] = beside(shift)
        t_o[...] = mats[:, 384:512]
        t_oT[...] = mats[:, 384:512].T
        down = down_ref[...].astype(BF)
        t_dn[...] = down
        for c in range(4):
            t_dnT[:, 128 * c : 128 * c + 128] = down[128 * c : 128 * c + 128].T
        for ref in (a_qkv, a_o, a_in, a_dn, a_vec, a_a, a_v, a_out):
            ref[...] = jnp.zeros_like(ref)

    lane_block = lax.broadcasted_iota(jnp.int32, (1, 128), 1) // 32
    ones = jnp.ones((16, 128), BF)
    zero = jnp.zeros((16, 128), BF)
    c0 = math.sqrt(2.0 / math.pi)
    c1 = c0 * 0.044715
    masks = [(lane_block == c).astype(BF) for c in range(4)]
    at_block = [lane_block == c for c in range(4)]
    kept = {name: [] for name in ("normed", "gradp", "mixed", "branch", "normed2", "inner", "cot", "active", "sums")}

    def flow(seqs):
        every = range(len(seqs))
        rels = [rel_ref[step * group + b] for b in seqs]
        lanes = [slice(128 * b, 128 * b + 128) for b in every]
        scores = [mm(rows_ref[b], s_a2[e]) for b, e in zip(seqs, rels)]
        rows_T = [rows_ref[b].T for b in seqs]
        value_T = [mm(s_vT[e], rows_T[i]).astype(BF) for i, e in enumerate(rels)]
        yield
        probs, probs_low = [], []
        for b in every:
            probs.append([])
            probs_low.append([])
            for s in range(STEPS):
                halves = []
                for u in range(2):
                    tile = scores[b][64 * s : 64 * s + 64, 128 * u : 128 * u + 128]
                    raised = jnp.exp2(tile - jnp.max(tile, axis=0, keepdims=True))
                    halves.append(raised * (1.0 / jnp.sum(raised, axis=0, keepdims=True)))
                probs[b].append(halves)
                probs_low[b].append([half.astype(BF) for half in halves])
        stem_values = [value_T[b].T for b in every]
        yield
        made = []
        gap = jnp.zeros((64, 128), BF)
        for b in every:
            made.append([])
            for t in range(2):
                made[b].append([])
                for u in range(2):
                    block = jnp.concatenate(
                        [
                            jnp.concatenate([probs_low[b][2 * t][u], gap], axis=1),
                            jnp.concatenate([gap, probs_low[b][2 * t + 1][u]], axis=1),
                        ],
                        axis=0,
                    )
                    made[b][t].append(
                        mm(value_T[b][64 * u : 64 * u + 64, 128 * t : 128 * t + 128], block)
                    )
        stem_mixed = []
        for b in every:
            rows = []
            for h in range(HEADS):
                u, c = divmod(h, 4)
                row = None
                for s in range(STEPS):
                    piece = made[b][s // 2][u][
                        16 * c : 16 * c + 16, 128 * (s % 2) : 128 * (s % 2) + 128
                    ]
                    turn = (s - c) % 4
                    if turn:
                        piece = pltpu.roll(piece, 32 * turn, 1)
                    row = piece if row is None else jnp.where(at_block[s], piece, row)
                rows.append(row)
            stem_mixed.append(jnp.concatenate(rows, axis=0).astype(BF))
        yield
        residual = [mm(s_outT[rels[b]], stem_mixed[b]) for b in every]
        yield

        def norm(values):
            units, inverses = [], []
            for value in values:
                centered = value - jnp.mean(value, axis=0, keepdims=True)
                inverse = lax.rsqrt(
                    jnp.mean(centered * centered, axis=0, keepdims=True) + NORM_EPSILON
                )
                units.append(centered * inverse)
                inverses.append(inverse)
            low = jnp.concatenate([unit.astype(BF) for unit in units], axis=1)
            return units, inverses, jnp.concatenate([low, jnp.ones((16, low.shape[1]), BF)], axis=0)

        def norm_back(gradient, unit, inverse):
            mean_one = jnp.mean(gradient, axis=0, keepdims=True)
            mean_two = jnp.mean(gradient * unit, axis=0, keepdims=True)
            return inverse * (gradient - mean_one - unit * mean_two)

        unit_one, inverse_one, normed = norm(residual)
        yield
        projected = mm(t_qkvT[...], normed)
        query_T = [(projected[:128, lanes[b]] * (LOG2E * SCALE)).astype(BF) for b in every]
        key_T = [projected[128:256, lanes[b]].astype(BF) for b in every]
        value_T = [projected[256:, lanes[b]].astype(BF) for b in every]
        keys = [key_T[b].T for b in every]
        values = [value_T[b].T for b in every]
        hide = []
        for b in seqs:
            base = (step * group + b) * STEPS
            marks = [seg_ref[base + s] for s in range(STEPS)]
            lane_marks = jnp.where(
                at_block[0],
                marks[0],
                jnp.where(at_block[1], marks[1], jnp.where(at_block[2], marks[2], marks[3])),
            )
            hide.append([jnp.where(lane_marks == marks[s], 0.0, HIDDEN_SCORE) for s in range(STEPS)])
        yield
        scores = [[mm(keys[b], head_pair(query_T[b], j)) for j in range(PAIRS)] for b in every]
        cot_list = [cot_ref[b].T for b in seqs]
        yield
        raised = []
        for b in every:
            raised.append([])
            for j in range(PAIRS):
                halves = []
                for u in range(2):
                    tile = scores[b][j][:, 128 * u : 128 * u + 128]
                    tile = jnp.concatenate(
                        [tile[32 * s : 32 * s + 32] + hide[b][s] for s in range(STEPS)], axis=0
                    )
                    halves.append(
                        jnp.exp2(tile - jnp.max(tile, axis=0, keepdims=True)).astype(BF)
                    )
                raised[b].append(jnp.concatenate(halves, axis=1))
        yield
        made = [
            [
                mm(jnp.concatenate([value_T[b][32 * j : 32 * j + 32], ones], axis=0), raised[b][j])
                for j in range(PAIRS)
            ]
            for b in every
        ]
        head_mixed, head_inverse, mixed_list = [], [], []
        for b in every:
            head_mixed.append([])
            head_inverse.append([])
            for h in range(HEADS):
                j, u = divmod(h, 2)
                here = slice(128 * u, 128 * u + 128)
                inverse = 1.0 / made[b][j][32:40, here]
                part = made[b][j][16 * u : 16 * u + 16, here]
                head_inverse[b].append(inverse)
                head_mixed[b].append(
                    jnp.concatenate([part[:8] * inverse, part[8:] * inverse], axis=0)
                )
            mixed_list.append(jnp.concatenate(head_mixed[b], axis=0).astype(BF))
        mixed = jnp.concatenate(mixed_list, axis=1)
        yield
        branch = mm(t_oT[...], mixed)
        hidden = [residual[b] + branch[:, lanes[b]] for b in every]
        yield
        unit_two, inverse_two, normed_two = norm(hidden)
        cot = jnp.concatenate(cot_list, axis=1)
        yield
        inner_all = mm(t_inT[...], normed_two)
        grad_all = mm(t_dn[...], cot)
        yield
        active_rows, grad_rows = [], []
        for r in range(0, FF, 16):
            active_cols, grad_cols = [], []
            for b in every:
                inner = inner_all[r : r + 16, lanes[b]]
                square = inner * inner
                bend = jnp.tanh(inner * (c0 + c1 * square))
                rise = 0.5 + 0.5 * bend
                active = inner * rise
                slope = rise + (active - active * rise) * (2.0 * c0 + (6.0 * c1) * square)
                active_cols.append(active.astype(BF))
                grad_cols.append((grad_all[r : r + 16, lanes[b]] * slope).astype(BF))
            active_rows.append(jnp.concatenate(active_cols, axis=1))
            grad_rows.append(jnp.concatenate(grad_cols, axis=1))
        active = jnp.concatenate(active_rows, axis=0)
        grad_inner = jnp.concatenate(grad_rows, axis=0)
        yield
        grad_all = mm(t_in[...], grad_inner)
        output_all = mm(t_dnT[...], active)
        yield

        grad_hidden = []
        for b in every:
            grad_hidden.append(
                cot_list[b].astype(F32)
                + norm_back(grad_all[:, lanes[b]], unit_two[b], inverse_two[b])
            )
        grad_branch = jnp.concatenate([part.astype(BF) for part in grad_hidden], axis=1)
        yield
        grad_mixed = mm(t_o[...], grad_branch)
        sums = [jnp.zeros((128, 128), F32)] * 3
        for i, b in enumerate(seqs):
            output = hidden[i] + output_all[:, lanes[i]] + vecs[4]
            out_ref[b] = output.astype(BF).T
            sums = [
                sums[0] + cot_list[i].astype(F32),
                sums[1] + output,
                sums[2] + output * output,
            ]
        kept["sums"].append(sums)
        grad_T, drops = [], []
        for b in every:
            scaled = []
            drops.append([])
            for h in range(HEADS):
                inverse = head_inverse[b][h]
                part = grad_mixed[16 * h : 16 * h + 16, lanes[b]]
                part = jnp.concatenate([part[:8] * inverse, part[8:] * inverse], axis=0)
                scaled.append(part.astype(BF))
                drops[b].append(jnp.sum(part * head_mixed[b][h], axis=0, keepdims=True))
            grad_T.append(jnp.concatenate(scaled, axis=0))
        yield
        grad_probs = [[mm(values[b], head_pair(grad_T[b], j)) for j in range(PAIRS)] for b in every]
        grad_values = [
            [mm_nt(pair_rows(grad_T[b], j), raised[b][j]) for j in range(PAIRS)] for b in every
        ]
        yield
        grad_scores = []
        for b in every:
            grad_scores.append([])
            for j in range(PAIRS):
                halves = []
                for u in range(2):
                    here = slice(128 * u, 128 * u + 128)
                    tile = grad_probs[b][j][:, here] - drops[b][2 * j + u]
                    halves.append(tile.astype(BF) * raised[b][j][:, here])
                grad_scores[b].append(jnp.concatenate(halves, axis=1))
        yield
        grad_queries = [
            [pair_pick(mm(key_T[b][32 * j : 32 * j + 32], grad_scores[b][j])) for j in range(PAIRS)]
            for b in every
        ]
        grad_keys = [
            [mm_nt(pair_rows(query_T[b], j), grad_scores[b][j]) for j in range(PAIRS)] for b in every
        ]
        grad_list = []
        for b in every:
            grad_list.append(
                jnp.concatenate(
                    [
                        (jnp.concatenate(grad_queries[b], axis=0) * SCALE).astype(BF),
                        (jnp.concatenate(grad_keys[b], axis=0) * (1.0 / LOG2E)).astype(BF),
                        jnp.concatenate(grad_values[b], axis=0).astype(BF),
                    ],
                    axis=0,
                )
            )
        grad_projected = jnp.concatenate(grad_list, axis=1)
        yield
        grad_all = mm(t_qkv[...], grad_projected)
        for name, value in (
            ("normed", normed),
            ("gradp", grad_projected),
            ("mixed", mixed),
            ("branch", grad_branch),
            ("normed2", normed_two),
            ("inner", grad_inner),
            ("cot", cot),
            ("active", active),
        ):
            kept[name].append(value)
        yield
        grad_tokens = [
            (grad_hidden[b] + norm_back(grad_all[:, lanes[b]], unit_one[b], inverse_one[b])).astype(BF)
            for b in every
        ]
        yield

        grad_mixed = [mm(s_out[rels[b]], grad_tokens[b]) for b in every]
        for b in every:
            a_out[rels[b]] += mm_nt(stem_mixed[b], grad_tokens[b])
        yield
        spread = []
        for b in every:
            spread.append([])
            turned = [grad_mixed[b].astype(BF)] + [
                pltpu.roll(grad_mixed[b], 32 * k, 1).astype(BF) for k in range(1, 4)
            ]
            for s in range(STEPS):
                pieces = []
                for h in range(HEADS):
                    c = h % 4
                    piece = turned[(c - s) % 4][16 * h : 16 * h + 16] * masks[c]
                    pieces.append(
                        jnp.concatenate([piece, zero] if h < 4 else [zero, piece], axis=1)
                    )
                spread[b].append(jnp.concatenate(pieces, axis=0))
        yield
        grad_probs = [
            [mm(stem_values[b][64 * s : 64 * s + 64], spread[b][s]) for s in range(STEPS)]
            for b in every
        ]
        grad_values = [
            jnp.concatenate(
                [
                    mm_nt(jnp.concatenate(probs_low[b][s], axis=1), spread[b][s]).astype(BF)
                    for s in range(STEPS)
                ],
                axis=0,
            )
            for b in every
        ]
        yield
        grad_scores = []
        for b in every:
            steps = []
            for s in range(STEPS):
                steps.append(
                    jnp.concatenate(
                        [
                            scores_back(probs[b][s][u], grad_probs[b][s][:, 128 * u : 128 * u + 128], 0)
                            for u in range(2)
                        ],
                        axis=1,
                    )
                )
            grad_scores.append(jnp.concatenate(steps, axis=0))
        yield
        for i, b in enumerate(seqs):
            e = rels[i]
            made = mm_nt(s_a[e], grad_scores[i]) + mm_nt(s_v[e], grad_values[i])
            rgrad_ref[b] = made.astype(BF).T
        yield
        for i, b in enumerate(seqs):
            e = rels[i]
            rows_T = rows_ref[b].T
            a_a[e] += mm(rows_T, grad_scores[i])
            a_v[e] += mm(rows_T, grad_values[i])

    part = 2
    flows = [flow(range(part * g, part * g + part)) for g in range(group // part)]
    live, wave = len(flows), 0
    while live:
        live = 0
        for g, one in enumerate(flows):
            if wave < LAG * g:
                live += 1
                continue
            try:
                next(one)
                live += 1
            except StopIteration:
                pass
        wave += 1

    def side(name):
        return jnp.concatenate(kept[name], axis=1)

    a_dn[...] += mm_nt(side("cot"), side("active"))
    a_in[...] += mm_nt(side("normed2"), side("inner"))
    a_o[...] += mm_nt(side("mixed"), side("branch"))
    a_qkv[...] += mm_nt(side("normed"), side("gradp"))
    for c in range(3):
        total = kept["sums"][0][c]
        for sums in kept["sums"][1:]:
            total = total + sums[c]
        a_vec[c] += total

    @pl.when(step == pl.num_programs(0) - 1)
    def _():
        me = pos_ref[0]

        def exact(left, right):
            high = left.astype(BF)
            return mm(high, right) + mm((left - high.astype(F32)).astype(BF), right)

        mats = mats_ref[...].astype(BF).astype(F32)
        blocks, gains, biases = [], [None, None], [None, None]
        for c in range(8):
            if c == 3:
                blocks.append(a_o[...])
                continue
            n = 0 if c < 3 else 1
            ref, where = (a_qkv, 128 * c) if c < 3 else (a_in, 128 * (c - 4))
            summed = ref[0:128, where : where + 128]
            ones_row = jnp.broadcast_to(ref[128:129, where : where + 128], (128, 128))
            weight = mats[:, 128 * c : 128 * c + 128]
            blocks.append(summed * vecs[2 * n] + ones_row * vecs[2 * n + 1])
            gain, bias = weight * summed, weight * ones_row
            gains[n] = gain if gains[n] is None else gains[n] + gain
            biases[n] = bias if biases[n] is None else biases[n] + bias
        blocks += [a_dn[:, 128 * c : 128 * c + 128].T for c in range(4)]
        count, per = 4, len(blocks) // 4

        def put(place, where, value):
            rows = value.shape[0]
            base = PIECE_ROWS * lax.div(place, 2)

            @pl.when(lax.rem(place, 2) == 0)
            def _():
                keep_ref[pl.ds(base + where, rows)] = value

            @pl.when(lax.rem(place, 2) == 1)
            def _():
                give_ref[pl.ds(base + where, rows)] = value.astype(BF)

        for j in range(count):
            place = jnp.bitwise_xor(me, j)
            for i in range(per):
                put(place, 128 * i, blocks[per * j + i])
        columns = [gains[0], biases[0], gains[1], biases[1], a_vec[0]]
        sums = [jnp.sum(column.T, axis=0, keepdims=True) for column in columns]
        sums += [a_in[128:129, 128 * c : 128 * c + 128] for c in range(4)]
        sums += [jnp.sum(a_vec[c].T, axis=0, keepdims=True) for c in (1, 2)]
        sums.append(jnp.zeros((5, 128), F32))
        sums = jnp.concatenate(sums, axis=0)
        high, low = split_sum(sums)
        sums_ref[...] = sums
        give_ref[2 * PIECE_ROWS : 2 * PIECE_ROWS + 16] = high
        give_ref[2 * PIECE_ROWS + 16 : 2 * PIECE_ROWS + 32] = low
        for k in range(count):
            grad = a_a[k] * SCALE
            grad_high = grad.astype(BF)
            grad_low = (grad - grad_high.astype(F32)).astype(BF)
            key_T = s_k[k].T
            spread = (mm(key_T, grad_high) + mm(key_T, grad_low)).T
            spread = jnp.where(head_mask, spread, 0.0)
            query = spread[0:32]
            for h in range(1, HEADS):
                query = query + spread[32 * h : 32 * h + 32]
            parts = [
                mm_nt(grad_high, s_qb[k]) + mm_nt(grad_low, s_qb[k]),
                a_v[k],
                a_out[k],
                query,
            ]
            base = PIECE_ROWS * (k // 2) + TRUNK_ROWS
            for i, value in enumerate(parts):
                here = slice(base + 128 * i, base + 128 * i + value.shape[0])
                if k % 2:
                    give_ref[here] = value.astype(BF)
                else:
                    keep_ref[here] = value


def split_sum(sums):
    high = sums.astype(BF)
    return high, (sums - high.astype(F32)).astype(BF)


def add_sums(sums_ref, got_ref, start, next_ref, give_ref, give_start):
    total = sums_ref[...] + (
        got_ref[start : start + 16].astype(F32) + got_ref[start + 16 : start + 32].astype(F32)
    )
    next_ref[...] = total
    if give_ref is not None:
        high, low = split_sum(total)
        give_ref[give_start : give_start + 16] = high
        give_ref[give_start + 16 : give_start + 32] = low


def core_kernel(keep_ref, got_ref, sums_ref, own_ref, give_ref, next_ref):
    own_ref[...] = keep_ref[0:PIECE_ROWS] + got_ref[0:PIECE_ROWS].astype(F32)
    give_ref[0:PIECE_ROWS] = (
        keep_ref[PIECE_ROWS : 2 * PIECE_ROWS] + got_ref[PIECE_ROWS : 2 * PIECE_ROWS].astype(F32)
    ).astype(BF)
    add_sums(sums_ref, got_ref, 2 * PIECE_ROWS, next_ref, give_ref, PIECE_ROWS)


def halve_kernel(pos_ref, keep_ref, got_ref, sums_ref, own_ref, give_ref, next_ref):
    odd = lax.rem(pos_ref[1], 2)
    trunk = keep_ref[0:TRUNK_ROWS] + got_ref[0:TRUNK_ROWS].astype(F32)
    stem = keep_ref[TRUNK_ROWS:] + got_ref[TRUNK_ROWS:PIECE_ROWS].astype(F32)
    rest = jnp.zeros((STEM_ROWS - TRUNK_ROWS, D), F32)
    trunk = jnp.concatenate([trunk, rest], axis=0)
    own_ref[...] = jnp.where(odd == 0, trunk, stem)
    give_ref[0:STEM_ROWS] = jnp.where(odd == 0, stem, trunk).astype(BF)
    add_sums(sums_ref, got_ref, PIECE_ROWS, next_ref, give_ref, STEM_ROWS)


def level_kernel(keep_ref, got_ref, sums_ref, own_ref, give_ref, next_ref):
    total = keep_ref[...] + got_ref[0:STEM_ROWS].astype(F32)
    own_ref[...] = total
    give_ref[0:STEM_ROWS] = total.astype(BF)
    add_sums(sums_ref, got_ref, STEM_ROWS, next_ref, give_ref, STEM_ROWS)


def last_kernel(keep_ref, got_ref, sums_ref, own_ref, next_ref):
    own_ref[...] = (keep_ref[...] + got_ref[0:STEM_ROWS].astype(F32)).astype(BF)
    add_sums(sums_ref, got_ref, STEM_ROWS, next_ref, None, 0)


def renew(weight, moment, average, gradient, step_rate):
    new_moment = MOMENTUM_DECAY * moment + gradient
    new_weight = weight - step_rate * (gradient + MOMENTUM_DECAY * new_moment)
    new_average = average + (new_weight - average) / (STEP + 1)
    return (new_moment, new_average, new_weight)


def put_new(outs, where, made):
    outs[0][where], outs[1][where], outs[2][where] = made
    if len(outs) > 3:
        outs[3][where] = made[2].astype(BF)


def renew_stem(token_total, pos_ref, own_ref, got_ref, sums_ref, *refs):
    stem_in, quer_in, vec_in = refs[0:3], refs[3:6], refs[6:9]
    stem_o, quer_o, vec_o, stats_o = refs[9:13], refs[13:17], refs[17:20], refs[20]
    rate = BASE_RATE / math.sqrt(token_total)
    odd = lax.rem(pos_ref[1], 2) == 1
    full = (slice(None), slice(None))
    for i in range(3):
        where = (slice(None), slice(128 * i, 128 * i + 128))
        rows = slice(128 * i, 128 * i + 128)
        grad = jnp.where(odd, own_ref[rows].astype(F32), got_ref[rows].astype(F32))
        put_new(stem_o, where, renew(*[ref[where] for ref in stem_in], grad, rate))
    grad = jnp.where(odd, own_ref[384:416].astype(F32), got_ref[384:416].astype(F32))
    put_new(quer_o, full, renew(*[ref[...] for ref in quer_in], grad, rate))
    put_new(vec_o, full, renew(*[ref[...] for ref in vec_in], sums_ref[0:9], rate))
    mean = sums_ref[9:10] / token_total
    stats_o[0:1] = mean
    stats_o[1:2] = sums_ref[10:11] / token_total - mean * mean


def renew_trunk(token_total, pos_ref, *refs):
    trunk_refs, mats_in, down_in = refs[0:4], refs[4:7], refs[7:10]
    mats_o, down_o, pieces = refs[10:14], refs[14:18], refs[18]
    rate = BASE_RATE / math.sqrt(token_total)
    for k, ref in enumerate(trunk_refs):
        pieces[jnp.bitwise_xor(pos_ref[0], k)] = ref[...].astype(F32)

    def block(i):
        return pieces[i // 3, 128 * (i % 3) : 128 * (i % 3) + 128]

    for i in range(8):
        where = (slice(None), slice(128 * i, 128 * i + 128))
        put_new(mats_o, where, renew(*[ref[where] for ref in mats_in], block(i), rate))
    for i in range(4):
        where = (slice(128 * i, 128 * i + 128), slice(None))
        put_new(down_o, where, renew(*[ref[where] for ref in down_in], block(8 + i), rate))


def vmem_call(kernel, outs, scratch=(), scalars=0):
    in_vmem = pl.BlockSpec(memory_space=pltpu.VMEM)

    def call(*args):
        return pl.pallas_call(
            kernel,
            out_shape=outs,
            in_specs=[pl.BlockSpec(memory_space=pltpu.SMEM)] * scalars
            + [in_vmem] * (len(args) - scalars),
            out_specs=jax.tree.map(lambda _: in_vmem, outs),
            scratch_shapes=list(scratch),
            compiler_params=pltpu.CompilerParams(vmem_limit_bytes=VMEM_LIMIT),
        )(*args)

    return call


def run_main(rel, segments, pos, rows, cot, stems, mats, down, vectors, emb_count):
    seqs = rows.shape[0]
    group = 8
    grid = seqs // group

    def whole(shape):
        return pl.BlockSpec(shape, lambda i, *_: (0,) * len(shape))

    scratch = [
        ((4, 128, 128), BF),
        ((4, 128, 256), BF),
        ((4, 128, 256), BF),
        ((4, 128, 256), BF),
        ((4, 128, 128), BF),
        ((4, 128, 128), BF),
        ((4, 128, 128), BF),
        ((4, 128, 128), BF),
        ((384, 144), BF),
        ((128, 384), BF),
        ((128, 128), BF),
        ((128, 128), BF),
        ((128, 512), BF),
        ((512, 144), BF),
        ((512, 128), BF),
        ((128, 512), BF),
        ((5, 128, 128), F32),
        ((144, 384), F32),
        ((128, 128), F32),
        ((144, 512), F32),
        ((128, 512), F32),
        ((3, 128, 128), F32),
        ((4, 128, 256), F32),
        ((4, 128, 128), F32),
        ((4, 128, 128), F32),
    ]
    return pl.pallas_call(
        functools.partial(main_kernel, group),
        out_shape=(
            jax.ShapeDtypeStruct((seqs, TOK_SEQ, D), BF),
            jax.ShapeDtypeStruct((seqs, ROWS_SEQ, D), BF),
            jax.ShapeDtypeStruct((2 * PIECE_ROWS, D), F32),
            jax.ShapeDtypeStruct((2 * PIECE_ROWS + VEC_ROWS, D), BF),
            jax.ShapeDtypeStruct((16, D), F32),
        ),
        grid_spec=pltpu.PrefetchScalarGridSpec(
            num_scalar_prefetch=3,
            grid=(grid,),
            in_specs=[
                pl.BlockSpec((group, ROWS_SEQ, D), lambda i, *_: (i, 0, 0)),
                pl.BlockSpec((group, TOK_SEQ, D), lambda i, *_: (i, 0, 0)),
            ]
            + [whole((STEM_ROWS, D))] * 4
            + [whole((D, 1024)), whole((FF, D)), whole((9, D))],
            out_specs=(
                pl.BlockSpec((group, TOK_SEQ, D), lambda i, *_: (i, 0, 0)),
                pl.BlockSpec((group, ROWS_SEQ, D), lambda i, *_: (i, 0, 0)),
                whole((2 * PIECE_ROWS, D)),
                whole((2 * PIECE_ROWS + VEC_ROWS, D)),
                whole((16, D)),
            ),
            scratch_shapes=[pltpu.VMEM(shape, dtype) for shape, dtype in scratch],
        ),
        compiler_params=pltpu.CompilerParams(
            vmem_limit_bytes=VMEM_LIMIT, dimension_semantics=("arbitrary",)
        ),
    )(rel, segments, pos, rows, cot, *stems, mats, down, vectors)


def local(
    stem_rows,
    emb_ids,
    segments,
    cotangent,
    trunk_mats,
    mats_momentum,
    mats_average,
    trunk_down,
    down_momentum,
    down_average,
    trunk_vectors,
    vectors_momentum,
    vectors_average,
    stem_mats,
    stem_momentum,
    stem_average,
    stem_queries,
    queries_momentum,
    queries_average,
):
    seqs = stem_rows.shape[0]
    emb_count, dp_count = lax.axis_size("emb"), lax.axis_size("dp")
    emb_me, dp_me = lax.axis_index("emb"), lax.axis_index("dp")
    pos = jnp.stack([emb_me, dp_me]).astype(jnp.int32)
    rel = emb_ids[:, 0] ^ emb_me
    token_total = seqs * TOK_SEQ * dp_count * emb_count

    def swap(value, axis, count, mask):
        return lax.ppermute(value, axis, [(i, i ^ mask) for i in range(count)])

    def spread(value):
        far = swap(value, "emb", emb_count, 2)
        return [value, swap(value, "emb", emb_count, 1), far, swap(far, "emb", emb_count, 1)]

    low = stem_mats[0].astype(BF)
    own = jnp.concatenate(
        [low[:, :D], low[:, D : 2 * D], low[:, 2 * D :], stem_queries[0].astype(BF)], axis=0
    )
    stems = spread(own)

    output, rows_grad, keep, give, sums = run_main(
        rel,
        segments.reshape(-1),
        pos,
        stem_rows.reshape(seqs, ROWS_SEQ, D),
        cotangent,
        stems,
        trunk_mats,
        trunk_down,
        trunk_vectors,
        emb_count,
    )

    f32, bf16 = F32, BF

    def shape(rows, dtype):
        return jax.ShapeDtypeStruct((rows, D), dtype)

    got = swap(give, "emb", emb_count, 1)
    own, give, sums = vmem_call(
        core_kernel, (shape(PIECE_ROWS, f32), shape(PIECE_ROWS + VEC_ROWS, bf16), shape(16, f32))
    )(keep, got, sums)
    got = swap(give, "emb", emb_count, 2)
    half = (shape(STEM_ROWS, f32), shape(STEM_ROWS + VEC_ROWS, bf16), shape(16, f32))
    own, give, sums = vmem_call(halve_kernel, half, scalars=1)(pos, own, got, sums)
    got = swap(give, "dp", dp_count, 1)
    bits = [1 << i for i in range(1, dp_count.bit_length() - 1)]
    if len(bits) == 2:
        bits[1] = bits[0] | bits[1]
    for mask in bits:
        own, give, sums = vmem_call(level_kernel, half)(own, got, sums)
        got = swap(give, "dp", dp_count, mask)
    own, sums = vmem_call(last_kernel, (shape(STEM_ROWS, bf16), shape(16, f32)))(own, got, sums)
    other = swap(own, "dp", dp_count, 1)
    trunk = jnp.where(dp_me % 2 == 0, own[:TRUNK_ROWS], other[:TRUNK_ROWS])
    trunks = spread(trunk)

    def like(array, copy):
        made = [jax.ShapeDtypeStruct(array.shape, F32)] * 3
        return made + ([jax.ShapeDtypeStruct(array.shape, BF)] if copy else [])

    stem_made = vmem_call(
        functools.partial(renew_stem, token_total),
        like(stem_mats[0], True)
        + like(stem_queries[0], True)
        + like(trunk_vectors, False)
        + [jax.ShapeDtypeStruct((2, D), F32)],
        scalars=1,
    )(
        pos,
        own,
        other,
        sums,
        stem_mats[0],
        stem_momentum[0],
        stem_average[0],
        stem_queries[0],
        queries_momentum[0],
        queries_average[0],
        trunk_vectors,
        vectors_momentum,
        vectors_average,
    )
    trunk_made = vmem_call(
        functools.partial(renew_trunk, token_total),
        like(trunk_mats, True) + like(trunk_down, True),
        [pltpu.VMEM((emb_count, TRUNK_ROWS, D), F32)],
        scalars=1,
    )(
        pos,
        *trunks,
        trunk_mats,
        mats_momentum,
        mats_average,
        trunk_down,
        down_momentum,
        down_average,
    )
    stems_new = [part[None] for part in stem_made[:8]]
    return (
        output,
        rows_grad.reshape(stem_rows.shape),
        *trunk_made,
        *stem_made[8:11],
        *stems_new,
        stem_made[11],
    )


def solution(mesh):
    split = P(("dp", "emb"))
    stem = P("emb")
    in_specs = (split,) * 4 + (P(),) * 9 + (stem,) * 6
    out_specs = (split,) * 2 + (P(),) * 11 + (stem,) * 8 + (P(),)
    return jax.shard_map(local, mesh=mesh, in_specs=in_specs, out_specs=out_specs, check_vma=False)
```

```python
import functools
import math

import jax
import jax.numpy as jnp
from jax import lax
from jax.experimental import pallas as pl
from jax.experimental.pallas import tpu as pltpu
from jax.sharding import PartitionSpec as P

D = 128
FF = 512
HEADS = 8
HEAD_DIM = 16
QUERIES = 32
STEPS = 4
STEP = 4
TOK_SEQ = 128
ROWS_SEQ = 256
PAIRS = HEADS // 2

NORM_EPSILON = 1e-05
MOMENTUM_DECAY = 0.9
BASE_RATE = 0.1
HIDDEN_SCORE = -1e30
LAG = 1
SCALE = 1.0 / math.sqrt(HEAD_DIM)
LOG2E = math.log2(math.e)

TRUNK_ROWS = 384
STEM_ROWS = 416
VEC_ROWS = 32
PIECE_ROWS = TRUNK_ROWS + STEM_ROWS

BF = jnp.bfloat16
F32 = jnp.float32
VMEM_LIMIT = 54 * 1024 * 1024


def mm(a, b):
    return lax.dot_general(a, b, (((1,), (0,)), ((), ())), preferred_element_type=F32)


def mm_nt(a, b):
    return lax.dot_general(a, b, (((1,), (1,)), ((), ())), preferred_element_type=F32)


def scores_back(probs, grad, axis):
    product = probs * grad
    return (product - probs * jnp.sum(product, axis=axis, keepdims=True)).astype(BF)


def head_pair(source, j):
    pieces = []
    if j:
        pieces.append(jnp.zeros((32 * j, 256), BF))
    zero = jnp.zeros((16, 128), BF)
    one = source[32 * j : 32 * j + 16]
    two = source[32 * j + 16 : 32 * j + 32]
    pieces.append(jnp.concatenate([one, zero], axis=1))
    pieces.append(jnp.concatenate([zero, two], axis=1))
    if j < PAIRS - 1:
        pieces.append(jnp.zeros((128 - 32 * j - 32, 256), BF))
    return jnp.concatenate(pieces, axis=0)


def pair_rows(source, j):
    zero = jnp.zeros((16, 128), BF)
    one = source[32 * j : 32 * j + 16]
    two = source[32 * j + 16 : 32 * j + 32]
    return jnp.concatenate(
        [jnp.concatenate([one, zero], axis=1), jnp.concatenate([zero, two], axis=1)], axis=0
    )


def turn_pair(both):
    return jnp.concatenate([both[:, :128].T, both[:, 128:].T], axis=0)


def turn_square(square):
    return jnp.concatenate(
        [jnp.concatenate([square[:128, c : c + 128].T, square[128:, c : c + 128].T], axis=1) for c in (0, 128)],
        axis=0,
    )


def turn_all(wide):
    return jnp.concatenate(
        [turn_rows(wide[:, c : c + 128]) for c in range(0, wide.shape[1], 128)], axis=0
    )


def turn_rows(tall):
    return jnp.concatenate(
        [tall[i : i + 128].T for i in range(0, tall.shape[0], 128)], axis=1
    )


def pair_pick(both):
    return jnp.concatenate([both[:16, :128], both[16:, 128:]], axis=0)


def main_kernel(
    group,
    rel_ref,
    seg_ref,
    pos_ref,
    rows_ref,
    cot_ref,
    own_ref,
    one_ref,
    two_ref,
    three_ref,
    mats_ref,
    down_ref,
    vec_ref,
    out_ref,
    rgrad_ref,
    keep_ref,
    give_ref,
    sums_ref,
    s_k,
    s_qb,
    s_a,
    s_a2,
    s_v,
    s_vT,
    s_out,
    s_outT,
    t_qkvT,
    t_qkv,
    t_o,
    t_oT,
    t_in,
    t_inT,
    t_dn,
    t_dnT,
    vecs,
    a_qkv,
    a_o,
    a_in,
    a_dn,
    a_vec,
    a_a,
    a_v,
    a_out,
):
    step = pl.program_id(0)

    head_mask = (
        lax.broadcasted_iota(jnp.int32, (256, 128), 0) // 32
        == lax.broadcasted_iota(jnp.int32, (256, 128), 1) // 16
    )

    @pl.when(step == 0)
    def _():
        for k, ref in enumerate((own_ref, one_ref, two_ref, three_ref)):
            wk, wv, wo = ref[0:128], ref[128:256], ref[256:384]
            queries = ref[384:416].astype(F32)
            tiled = jnp.where(head_mask, jnp.concatenate([queries] * HEADS, axis=0), 0.0)
            block = tiled.T.astype(BF)
            both = mm(wk, block) * SCALE
            s_k[k] = wk
            s_qb[k] = block
            s_a[k] = both.astype(BF)
            s_a2[k] = (both * LOG2E).astype(BF)
            s_v[k] = wv
            s_vT[k] = wv.T
            s_out[k] = wo
            s_outT[k] = wo.T
        mats = mats_ref[...].astype(BF)
        for c in range(5):
            vecs[c] = jnp.broadcast_to(vec_ref[c : c + 1], (128, 128)).T
        corner = lax.broadcasted_iota(jnp.int32, (128, 16), 1)

        def beside(column):
            column = jnp.broadcast_to(column, (128, 16))
            high = column.astype(BF).astype(F32)
            return jnp.where(corner == 0, high, jnp.where(corner == 1, column - high, 0.0)).astype(BF)

        for c in range(7):
            where = 128 * c if c < 3 else 128 * (c + 1)
            block = mats[:, where : where + 128].astype(F32)
            gain, bias = (vecs[0], vecs[1]) if c < 3 else (vecs[2], vecs[3])
            scaled = (block * gain).astype(BF)
            shift = jnp.sum((block * bias).T, axis=1, keepdims=True)
            if c < 3:
                t_qkv[:, 128 * c : 128 * c + 128] = scaled
                t_qkvT[128 * c : 128 * c + 128, 0:128] = scaled.T
                t_qkvT[128 * c : 128 * c + 128, 128:144] = beside(shift)
            else:
                d = c - 3
                shift = shift + jnp.broadcast_to(vec_ref[5 + d : 6 + d], (128, 128)).T[:, 0:1]
                t_in[:, 128 * d : 128 * d + 128] = scaled
                t_inT[128 * d : 128 * d + 128, 0:128] = scaled.T
                t_inT[128 * d : 128 * d + 128, 128:144] = beside(shift)
        t_o[...] = mats[:, 384:512]
        t_oT[...] = mats[:, 384:512].T
        down = down_ref[...].astype(BF)
        t_dn[...] = down
        for c in range(4):
            t_dnT[:, 128 * c : 128 * c + 128] = down[128 * c : 128 * c + 128].T
        for ref in (a_qkv, a_o, a_in, a_dn, a_vec, a_a, a_v, a_out):
            ref[...] = jnp.zeros_like(ref)

    lane_block = lax.broadcasted_iota(jnp.int32, (1, 128), 1) // 32
    ones = jnp.ones((16, 128), BF)
    zero = jnp.zeros((16, 128), BF)
    c0 = math.sqrt(2.0 / math.pi)
    c1 = c0 * 0.044715
    LOW_M0, LOW_M1, LOW_ONE, LOW_2C0, LOW_6C1 = [
        jnp.bfloat16(value)
        for value in (-2.0 * LOG2E * c0, -2.0 * LOG2E * c1, 1.0, 2.0 * c0, 6.0 * c1)
    ]
    masks = [(lane_block == c).astype(BF) for c in range(4)]
    lane_head = lax.broadcasted_iota(jnp.int32, (1, 128), 1) // 16
    head_lanes = [(lane_head == h).astype(BF) for h in range(HEADS)]
    at_block = [lane_block == c for c in range(4)]
    kept = {name: [] for name in ("normed", "gradp", "mixed", "branch", "normed2", "inner", "cot", "active", "sums")}

    def flow(seqs):
        every = range(len(seqs))
        rels = [rel_ref[step * group + b] for b in seqs]
        lanes = [slice(128 * b, 128 * b + 128) for b in every]
        scores = [mm(rows_ref[b], s_a2[e]) for b, e in zip(seqs, rels)]
        rows_T = [rows_ref[b].T for b in seqs]
        value_T = [mm(s_vT[e], rows_T[i]).astype(BF) for i, e in enumerate(rels)]
        yield
        probs, probs_low = [], []
        for b in every:
            probs.append([])
            probs_low.append([])
            for s in range(STEPS):
                halves = []
                for u in range(2):
                    tile = scores[b][64 * s : 64 * s + 64, 128 * u : 128 * u + 128]
                    raised = jnp.exp2(tile - jnp.max(tile, axis=0, keepdims=True))
                    halves.append(raised * (1.0 / jnp.sum(raised, axis=0, keepdims=True)))
                probs[b].append(halves)
                probs_low[b].append([half.astype(BF) for half in halves])
        stem_values = [value_T[b].T for b in every]
        yield
        made = []
        gap = jnp.zeros((64, 128), BF)
        for b in every:
            made.append([])
            for t in range(2):
                made[b].append([])
                for u in range(2):
                    block = jnp.concatenate(
                        [
                            jnp.concatenate([probs_low[b][2 * t][u], gap], axis=1),
                            jnp.concatenate([gap, probs_low[b][2 * t + 1][u]], axis=1),
                        ],
                        axis=0,
                    )
                    made[b][t].append(
                        mm(value_T[b][64 * u : 64 * u + 64, 128 * t : 128 * t + 128], block)
                    )
        stem_mixed = []
        for b in every:
            rows = []
            for h in range(HEADS):
                u, c = divmod(h, 4)
                row = None
                for s in range(STEPS):
                    piece = made[b][s // 2][u][
                        16 * c : 16 * c + 16, 128 * (s % 2) : 128 * (s % 2) + 128
                    ]
                    turn = (s - c) % 4
                    if turn:
                        piece = pltpu.roll(piece, 32 * turn, 1)
                    row = piece if row is None else jnp.where(at_block[s], piece, row)
                rows.append(row)
            stem_mixed.append(jnp.concatenate(rows, axis=0).astype(BF))
        yield
        residual = [mm(s_outT[rels[b]], stem_mixed[b]) for b in every]
        yield

        def norm(values):
            units, inverses = [], []
            for value in values:
                centered = value - jnp.mean(value, axis=0, keepdims=True)
                inverse = lax.rsqrt(
                    jnp.mean(centered * centered, axis=0, keepdims=True) + NORM_EPSILON
                )
                units.append(centered * inverse)
                inverses.append(inverse)
            low = jnp.concatenate([unit.astype(BF) for unit in units], axis=1)
            return units, inverses, jnp.concatenate([low, jnp.ones((16, low.shape[1]), BF)], axis=0)

        def norm_back(gradient, unit, inverse):
            mean_one = jnp.mean(gradient, axis=0, keepdims=True)
            mean_two = jnp.mean(gradient * unit, axis=0, keepdims=True)
            return inverse * (gradient - mean_one - unit * mean_two)

        unit_one, inverse_one, normed = norm(residual)
        yield
        projected = mm(t_qkvT[...], normed)
        query_T = [(projected[:128, lanes[b]] * (LOG2E * SCALE)).astype(BF) for b in every]
        key_T = [projected[128:256, lanes[b]].astype(BF) for b in every]
        value_T = [projected[256:, lanes[b]].astype(BF) for b in every]
        keys = [key_T[b].T for b in every]
        values = [value_T[b].T for b in every]
        hide = []
        for b in seqs:
            base = (step * group + b) * STEPS
            marks = [seg_ref[base + s] for s in range(STEPS)]
            lane_marks = jnp.where(
                at_block[0],
                marks[0],
                jnp.where(at_block[1], marks[1], jnp.where(at_block[2], marks[2], marks[3])),
            )
            hide.append([jnp.where(lane_marks == marks[s], 0.0, HIDDEN_SCORE) for s in range(STEPS)])
        yield
        scores = [[mm(keys[b], head_pair(query_T[b], j)) for j in range(PAIRS)] for b in every]
        cot_list = [cot_ref[b].T for b in seqs]
        yield
        raised = []
        for b in every:
            raised.append([])
            for j in range(PAIRS):
                halves = []
                for u in range(2):
                    tile = scores[b][j][:, 128 * u : 128 * u + 128]
                    tile = jnp.concatenate(
                        [tile[32 * s : 32 * s + 32] + hide[b][s] for s in range(STEPS)], axis=0
                    )
                    halves.append(
                        jnp.exp2(tile - jnp.max(tile, axis=0, keepdims=True)).astype(BF)
                    )
                raised[b].append(jnp.concatenate(halves, axis=1))
        yield
        made = [
            [
                mm(jnp.concatenate([value_T[b][32 * j : 32 * j + 32], ones], axis=0), raised[b][j])
                for j in range(PAIRS)
            ]
            for b in every
        ]
        head_mixed, head_inverse, mixed_list = [], [], []
        for b in every:
            head_mixed.append([])
            head_inverse.append([])
            for h in range(HEADS):
                j, u = divmod(h, 2)
                here = slice(128 * u, 128 * u + 128)
                inverse = 1.0 / made[b][j][32:40, here]
                part = made[b][j][16 * u : 16 * u + 16, here]
                head_inverse[b].append(inverse)
                head_mixed[b].append(
                    jnp.concatenate([part[:8] * inverse, part[8:] * inverse], axis=0)
                )
            mixed_list.append(jnp.concatenate(head_mixed[b], axis=0).astype(BF))
        mixed = jnp.concatenate(mixed_list, axis=1)
        yield
        branch = mm(t_oT[...], mixed)
        hidden = [residual[b] + branch[:, lanes[b]] for b in every]
        yield
        unit_two, inverse_two, normed_two = norm(hidden)
        cot = jnp.concatenate(cot_list, axis=1)
        yield
        inner_all = mm(t_inT[...], normed_two)
        grad_all = mm(t_dn[...], cot)
        yield
        active_rows, grad_rows = [], []
        for r in range(0, FF, 16):
            active_cols, grad_cols = [], []
            for b in every:
                inner = inner_all[r : r + 16, lanes[b]].astype(BF)
                square = inner * inner
                bend = jnp.exp2(inner * (LOW_M0 + LOW_M1 * square))
                rise = pl.reciprocal(LOW_ONE + bend, approx=True)
                active = inner * rise
                slope = rise + (active - active * rise) * (LOW_2C0 + LOW_6C1 * square)
                active_cols.append(active)
                grad_cols.append(grad_all[r : r + 16, lanes[b]].astype(BF) * slope)
            active_rows.append(jnp.concatenate(active_cols, axis=1))
            grad_rows.append(jnp.concatenate(grad_cols, axis=1))
        active = jnp.concatenate(active_rows, axis=0)
        grad_inner = jnp.concatenate(grad_rows, axis=0)
        yield
        grad_all = mm(t_in[...], grad_inner)
        output_all = mm(t_dnT[...], active)
        turn_inner, turn_active = turn_all(grad_inner), turn_all(active)
        yield

        grad_hidden = []
        for b in every:
            grad_hidden.append(
                cot_list[b].astype(F32)
                + norm_back(grad_all[:, lanes[b]], unit_two[b], inverse_two[b])
            )
        grad_branch = jnp.concatenate([part.astype(BF) for part in grad_hidden], axis=1)
        yield
        grad_mixed = mm(t_o[...], grad_branch)
        sums = [jnp.zeros((128, 128), F32)] * 3
        for i, b in enumerate(seqs):
            output = hidden[i] + output_all[:, lanes[i]] + vecs[4]
            out_ref[b] = output.astype(BF).T
            sums = [
                sums[0] + cot_list[i].astype(F32),
                sums[1] + output,
                sums[2] + output * output,
            ]
        kept["sums"].append(sums)
        grad_T, drops = [], []
        for b in every:
            scaled = []
            drops.append([])
            for h in range(HEADS):
                inverse = head_inverse[b][h]
                part = grad_mixed[16 * h : 16 * h + 16, lanes[b]]
                part = jnp.concatenate([part[:8] * inverse, part[8:] * inverse], axis=0)
                scaled.append(part.astype(BF))
                drops[b].append(jnp.sum(part * head_mixed[b][h], axis=0, keepdims=True))
            grad_T.append(jnp.concatenate(scaled, axis=0))
        yield
        grad_probs = [[mm(values[b], head_pair(grad_T[b], j)) for j in range(PAIRS)] for b in every]
        grad_values = [
            [mm(pair_rows(grad_T[b], j), turn_pair(raised[b][j])) for j in range(PAIRS)] for b in every
        ]
        yield
        grad_scores = []
        for b in every:
            grad_scores.append([])
            for j in range(PAIRS):
                halves = []
                for u in range(2):
                    here = slice(128 * u, 128 * u + 128)
                    tile = grad_probs[b][j][:, here] - drops[b][2 * j + u]
                    halves.append(tile.astype(BF) * raised[b][j][:, here])
                grad_scores[b].append(jnp.concatenate(halves, axis=1))
        yield
        grad_queries = [
            [pair_pick(mm(key_T[b][32 * j : 32 * j + 32], grad_scores[b][j])) for j in range(PAIRS)]
            for b in every
        ]
        grad_keys = [
            [mm(pair_rows(query_T[b], j), turn_pair(grad_scores[b][j])) for j in range(PAIRS)] for b in every
        ]
        grad_list = []
        for b in every:
            grad_list.append(
                jnp.concatenate(
                    [
                        (jnp.concatenate(grad_queries[b], axis=0) * SCALE).astype(BF),
                        (jnp.concatenate(grad_keys[b], axis=0) * (1.0 / LOG2E)).astype(BF),
                        jnp.concatenate(grad_values[b], axis=0).astype(BF),
                    ],
                    axis=0,
                )
            )
        grad_projected = jnp.concatenate(grad_list, axis=1)
        yield
        grad_all = mm(t_qkv[...], grad_projected)
        for name, value in (
            ("normed", normed),
            ("gradp", turn_all(grad_projected)),
            ("mixed", mixed),
            ("branch", grad_branch),
            ("normed2", normed_two),
            ("inner", turn_inner),
            ("cot", cot),
            ("active", turn_active),
        ):
            kept[name].append(value)
        yield
        grad_tokens = [
            (grad_hidden[b] + norm_back(grad_all[:, lanes[b]], unit_one[b], inverse_one[b])).astype(BF)
            for b in every
        ]
        yield

        grad_mixed = [mm(s_out[rels[b]], grad_tokens[b]) for b in every]
        for b in every:
            a_out[rels[b]] += mm_nt(stem_mixed[b], grad_tokens[b])
        yield
        spread, tall = [], []
        for b in every:
            spread.append([])
            mixed_tok = grad_mixed[b].astype(BF).T
            tall.append(
                [
                    jnp.concatenate(
                        [mixed_tok[32 * s : 32 * s + 32] * head_lanes[h] for h in range(HEADS)],
                        axis=0,
                    )
                    for s in range(STEPS)
                ]
            )
            turned = [grad_mixed[b].astype(BF)] + [
                pltpu.roll(grad_mixed[b], 32 * k, 1).astype(BF) for k in range(1, 4)
            ]
            for s in range(STEPS):
                pieces = []
                for h in range(HEADS):
                    c = h % 4
                    piece = turned[(c - s) % 4][16 * h : 16 * h + 16] * masks[c]
                    pieces.append(
                        jnp.concatenate([piece, zero] if h < 4 else [zero, piece], axis=1)
                    )
                spread[b].append(jnp.concatenate(pieces, axis=0))
        yield
        grad_probs = [
            [mm(stem_values[b][64 * s : 64 * s + 64], spread[b][s]) for s in range(STEPS)]
            for b in every
        ]
        grad_values = [
            jnp.concatenate(
                [
                    mm(jnp.concatenate(probs_low[b][s], axis=1), tall[b][s]).astype(BF)
                    for s in range(STEPS)
                ],
                axis=0,
            )
            for b in every
        ]
        yield
        grad_scores = []
        for b in every:
            steps = []
            for s in range(STEPS):
                steps.append(
                    jnp.concatenate(
                        [
                            scores_back(probs[b][s][u], grad_probs[b][s][:, 128 * u : 128 * u + 128], 0)
                            for u in range(2)
                        ],
                        axis=1,
                    )
                )
            grad_scores.append(jnp.concatenate(steps, axis=0))
        yield
        for i, b in enumerate(seqs):
            e = rels[i]
            made = mm(s_a[e], turn_square(grad_scores[i])) + mm_nt(s_v[e], grad_values[i])
            rgrad_ref[b] = made.astype(BF).T
        yield
        for i, b in enumerate(seqs):
            e = rels[i]
            rows_T = rows_ref[b].T
            a_a[e] += mm(rows_T, grad_scores[i])
            a_v[e] += mm(rows_T, grad_values[i])

    part = 2
    flows = [flow(range(part * g, part * g + part)) for g in range(group // part)]
    live, wave = len(flows), 0
    while live:
        live = 0
        for g, one in enumerate(flows):
            if wave < LAG * g:
                live += 1
                continue
            try:
                next(one)
                live += 1
            except StopIteration:
                pass
        wave += 1

    def side(name):
        return jnp.concatenate(kept[name], axis=1)

    def stack(name):
        return jnp.concatenate(kept[name], axis=0)

    a_dn[...] += mm(side("cot"), stack("active"))
    a_in[...] += mm(side("normed2"), stack("inner"))
    a_o[...] += mm_nt(side("mixed"), side("branch"))
    a_qkv[...] += mm(side("normed"), stack("gradp"))
    for c in range(3):
        total = kept["sums"][0][c]
        for sums in kept["sums"][1:]:
            total = total + sums[c]
        a_vec[c] += total

    @pl.when(step == pl.num_programs(0) - 1)
    def _():
        me = pos_ref[0]

        def exact(left, right):
            high = left.astype(BF)
            return mm(high, right) + mm((left - high.astype(F32)).astype(BF), right)

        mats = mats_ref[...].astype(BF).astype(F32)
        blocks, gains, biases = [], [None, None], [None, None]
        for c in range(8):
            if c == 3:
                blocks.append(a_o[...])
                continue
            n = 0 if c < 3 else 1
            ref, where = (a_qkv, 128 * c) if c < 3 else (a_in, 128 * (c - 4))
            summed = ref[0:128, where : where + 128]
            ones_row = jnp.broadcast_to(ref[128:129, where : where + 128], (128, 128))
            weight = mats[:, 128 * c : 128 * c + 128]
            blocks.append(summed * vecs[2 * n] + ones_row * vecs[2 * n + 1])
            gain, bias = weight * summed, weight * ones_row
            gains[n] = gain if gains[n] is None else gains[n] + gain
            biases[n] = bias if biases[n] is None else biases[n] + bias
        blocks += [a_dn[:, 128 * c : 128 * c + 128].T for c in range(4)]
        count, per = 4, len(blocks) // 4

        def put(place, where, value):
            rows = value.shape[0]
            base = PIECE_ROWS * lax.div(place, 2)

            @pl.when(lax.rem(place, 2) == 0)
            def _():
                keep_ref[pl.ds(base + where, rows)] = value

            @pl.when(lax.rem(place, 2) == 1)
            def _():
                give_ref[pl.ds(base + where, rows)] = value.astype(BF)

        for j in range(count):
            place = jnp.bitwise_xor(me, j)
            for i in range(per):
                put(place, 128 * i, blocks[per * j + i])
        columns = [gains[0], biases[0], gains[1], biases[1], a_vec[0]]
        sums = [jnp.sum(column.T, axis=0, keepdims=True) for column in columns]
        sums += [a_in[128:129, 128 * c : 128 * c + 128] for c in range(4)]
        sums += [jnp.sum(a_vec[c].T, axis=0, keepdims=True) for c in (1, 2)]
        sums.append(jnp.zeros((5, 128), F32))
        sums = jnp.concatenate(sums, axis=0)
        high, low = split_sum(sums)
        sums_ref[...] = sums
        give_ref[2 * PIECE_ROWS : 2 * PIECE_ROWS + 16] = high
        give_ref[2 * PIECE_ROWS + 16 : 2 * PIECE_ROWS + 32] = low
        for k in range(count):
            grad = a_a[k] * SCALE
            grad_high = grad.astype(BF)
            grad_low = (grad - grad_high.astype(F32)).astype(BF)
            key_T = s_k[k].T
            spread = (mm(key_T, grad_high) + mm(key_T, grad_low)).T
            spread = jnp.where(head_mask, spread, 0.0)
            query = spread[0:32]
            for h in range(1, HEADS):
                query = query + spread[32 * h : 32 * h + 32]
            parts = [
                mm_nt(grad_high, s_qb[k]) + mm_nt(grad_low, s_qb[k]),
                a_v[k],
                a_out[k],
                query,
            ]
            base = PIECE_ROWS * (k // 2) + TRUNK_ROWS
            for i, value in enumerate(parts):
                here = slice(base + 128 * i, base + 128 * i + value.shape[0])
                if k % 2:
                    give_ref[here] = value.astype(BF)
                else:
                    keep_ref[here] = value


def split_sum(sums):
    high = sums.astype(BF)
    return high, (sums - high.astype(F32)).astype(BF)


def add_sums(sums_ref, got_ref, start, next_ref, give_ref, give_start):
    total = sums_ref[...] + (
        got_ref[start : start + 16].astype(F32) + got_ref[start + 16 : start + 32].astype(F32)
    )
    next_ref[...] = total
    if give_ref is not None:
        high, low = split_sum(total)
        give_ref[give_start : give_start + 16] = high
        give_ref[give_start + 16 : give_start + 32] = low


def core_kernel(keep_ref, got_ref, sums_ref, own_ref, give_ref, next_ref):
    own_ref[...] = keep_ref[0:PIECE_ROWS] + got_ref[0:PIECE_ROWS].astype(F32)
    give_ref[0:PIECE_ROWS] = (
        keep_ref[PIECE_ROWS : 2 * PIECE_ROWS] + got_ref[PIECE_ROWS : 2 * PIECE_ROWS].astype(F32)
    ).astype(BF)
    add_sums(sums_ref, got_ref, 2 * PIECE_ROWS, next_ref, give_ref, PIECE_ROWS)


def halve_kernel(pos_ref, keep_ref, got_ref, sums_ref, own_ref, give_ref, next_ref):
    odd = lax.rem(pos_ref[1], 2)
    trunk = keep_ref[0:TRUNK_ROWS] + got_ref[0:TRUNK_ROWS].astype(F32)
    stem = keep_ref[TRUNK_ROWS:] + got_ref[TRUNK_ROWS:PIECE_ROWS].astype(F32)
    rest = jnp.zeros((STEM_ROWS - TRUNK_ROWS, D), F32)
    trunk = jnp.concatenate([trunk, rest], axis=0)
    own_ref[...] = jnp.where(odd == 0, trunk, stem)
    give_ref[0:STEM_ROWS] = jnp.where(odd == 0, stem, trunk).astype(BF)
    add_sums(sums_ref, got_ref, PIECE_ROWS, next_ref, give_ref, STEM_ROWS)


def level_kernel(keep_ref, got_ref, sums_ref, own_ref, give_ref, next_ref):
    total = keep_ref[...] + got_ref[0:STEM_ROWS].astype(F32)
    own_ref[...] = total
    give_ref[0:STEM_ROWS] = total.astype(BF)
    add_sums(sums_ref, got_ref, STEM_ROWS, next_ref, give_ref, STEM_ROWS)


def last_kernel(keep_ref, got_ref, sums_ref, own_ref, next_ref):
    own_ref[...] = (keep_ref[...] + got_ref[0:STEM_ROWS].astype(F32)).astype(BF)
    add_sums(sums_ref, got_ref, STEM_ROWS, next_ref, None, 0)


def renew(weight, moment, average, gradient, step_rate):
    new_moment = MOMENTUM_DECAY * moment + gradient
    new_weight = weight - step_rate * (gradient + MOMENTUM_DECAY * new_moment)
    new_average = average + (new_weight - average) / (STEP + 1)
    return (new_moment, new_average, new_weight)


def put_new(outs, where, made):
    outs[0][where], outs[1][where], outs[2][where] = made
    if len(outs) > 3:
        outs[3][where] = made[2].astype(BF)


def renew_stem(token_total, pos_ref, own_ref, got_ref, sums_ref, *refs):
    stem_in, quer_in, vec_in = refs[0:3], refs[3:6], refs[6:9]
    stem_o, quer_o, vec_o, stats_o = refs[9:13], refs[13:17], refs[17:20], refs[20]
    rate = BASE_RATE / math.sqrt(token_total)
    odd = lax.rem(pos_ref[1], 2) == 1
    full = (slice(None), slice(None))
    for i in range(3):
        where = (slice(None), slice(128 * i, 128 * i + 128))
        rows = slice(128 * i, 128 * i + 128)
        grad = jnp.where(odd, own_ref[rows].astype(F32), got_ref[rows].astype(F32))
        put_new(stem_o, where, renew(*[ref[where] for ref in stem_in], grad, rate))
    grad = jnp.where(odd, own_ref[384:416].astype(F32), got_ref[384:416].astype(F32))
    put_new(quer_o, full, renew(*[ref[...] for ref in quer_in], grad, rate))
    put_new(vec_o, full, renew(*[ref[...] for ref in vec_in], sums_ref[0:9], rate))
    mean = sums_ref[9:10] / token_total
    stats_o[0:1] = mean
    stats_o[1:2] = sums_ref[10:11] / token_total - mean * mean


def renew_trunk(token_total, pos_ref, *refs):
    trunk_refs, mats_in, down_in = refs[0:4], refs[4:7], refs[7:10]
    mats_o, down_o, pieces = refs[10:14], refs[14:18], refs[18]
    rate = BASE_RATE / math.sqrt(token_total)
    for k, ref in enumerate(trunk_refs):
        pieces[jnp.bitwise_xor(pos_ref[0], k)] = ref[...].astype(F32)

    def block(i):
        return pieces[i // 3, 128 * (i % 3) : 128 * (i % 3) + 128]

    for i in range(8):
        where = (slice(None), slice(128 * i, 128 * i + 128))
        put_new(mats_o, where, renew(*[ref[where] for ref in mats_in], block(i), rate))
    for i in range(4):
        where = (slice(128 * i, 128 * i + 128), slice(None))
        put_new(down_o, where, renew(*[ref[where] for ref in down_in], block(8 + i), rate))


def vmem_call(kernel, outs, scratch=(), scalars=0):
    in_vmem = pl.BlockSpec(memory_space=pltpu.VMEM)

    def call(*args):
        return pl.pallas_call(
            kernel,
            out_shape=outs,
            in_specs=[pl.BlockSpec(memory_space=pltpu.SMEM)] * scalars
            + [in_vmem] * (len(args) - scalars),
            out_specs=jax.tree.map(lambda _: in_vmem, outs),
            scratch_shapes=list(scratch),
            compiler_params=pltpu.CompilerParams(vmem_limit_bytes=8 * 1024 * 1024),
        )(*args)

    return call


def run_main(rel, segments, pos, rows, cot, stems, mats, down, vectors, emb_count):
    seqs = rows.shape[0]
    group = 16
    grid = seqs // group

    def whole(shape):
        return pl.BlockSpec(shape, lambda i, *_: (0,) * len(shape))

    scratch = [
        ((4, 128, 128), BF),
        ((4, 128, 256), BF),
        ((4, 128, 256), BF),
        ((4, 128, 256), BF),
        ((4, 128, 128), BF),
        ((4, 128, 128), BF),
        ((4, 128, 128), BF),
        ((4, 128, 128), BF),
        ((384, 144), BF),
        ((128, 384), BF),
        ((128, 128), BF),
        ((128, 128), BF),
        ((128, 512), BF),
        ((512, 144), BF),
        ((512, 128), BF),
        ((128, 512), BF),
        ((5, 128, 128), F32),
        ((144, 384), F32),
        ((128, 128), F32),
        ((144, 512), F32),
        ((128, 512), F32),
        ((3, 128, 128), F32),
        ((4, 128, 256), F32),
        ((4, 128, 128), F32),
        ((4, 128, 128), F32),
    ]
    return pl.pallas_call(
        functools.partial(main_kernel, group),
        out_shape=(
            jax.ShapeDtypeStruct((seqs, TOK_SEQ, D), BF),
            jax.ShapeDtypeStruct((seqs, ROWS_SEQ, D), BF),
            jax.ShapeDtypeStruct((2 * PIECE_ROWS, D), F32),
            jax.ShapeDtypeStruct((2 * PIECE_ROWS + VEC_ROWS, D), BF),
            jax.ShapeDtypeStruct((16, D), F32),
        ),
        grid_spec=pltpu.PrefetchScalarGridSpec(
            num_scalar_prefetch=3,
            grid=(grid,),
            in_specs=[
                pl.BlockSpec((group, ROWS_SEQ, D), lambda i, *_: (i, 0, 0)),
                pl.BlockSpec((group, TOK_SEQ, D), lambda i, *_: (i, 0, 0)),
            ]
            + [whole((STEM_ROWS, D))] * 4
            + [whole((D, 1024)), whole((FF, D)), whole((9, D))],
            out_specs=(
                pl.BlockSpec((group, TOK_SEQ, D), lambda i, *_: (i, 0, 0)),
                pl.BlockSpec((group, ROWS_SEQ, D), lambda i, *_: (i, 0, 0)),
                whole((2 * PIECE_ROWS, D)),
                whole((2 * PIECE_ROWS + VEC_ROWS, D)),
                whole((16, D)),
            ),
            scratch_shapes=[pltpu.VMEM(shape, dtype) for shape, dtype in scratch],
        ),
        compiler_params=pltpu.CompilerParams(
            vmem_limit_bytes=VMEM_LIMIT, dimension_semantics=("arbitrary",)
        ),
    )(rel, segments, pos, rows, cot, *stems, mats, down, vectors)


def local(
    stem_rows,
    emb_ids,
    segments,
    cotangent,
    trunk_mats,
    mats_momentum,
    mats_average,
    trunk_down,
    down_momentum,
    down_average,
    trunk_vectors,
    vectors_momentum,
    vectors_average,
    stem_mats,
    stem_momentum,
    stem_average,
    stem_queries,
    queries_momentum,
    queries_average,
):
    seqs = stem_rows.shape[0]
    emb_count, dp_count = lax.axis_size("emb"), lax.axis_size("dp")
    emb_me, dp_me = lax.axis_index("emb"), lax.axis_index("dp")
    pos = jnp.stack([emb_me, dp_me]).astype(jnp.int32)
    rel = emb_ids[:, 0] ^ emb_me
    token_total = seqs * TOK_SEQ * dp_count * emb_count

    def swap(value, axis, count, mask):
        return lax.ppermute(value, axis, [(i, i ^ mask) for i in range(count)])

    def spread(value):
        far = swap(value, "emb", emb_count, 2)
        return [value, swap(value, "emb", emb_count, 1), far, swap(far, "emb", emb_count, 1)]

    low = stem_mats[0].astype(BF)
    own = jnp.concatenate(
        [low[:, :D], low[:, D : 2 * D], low[:, 2 * D :], stem_queries[0].astype(BF)], axis=0
    )
    stems = spread(own)

    output, rows_grad, keep, give, sums = run_main(
        rel,
        segments.reshape(-1),
        pos,
        stem_rows.reshape(seqs, ROWS_SEQ, D),
        cotangent,
        stems,
        trunk_mats,
        trunk_down,
        trunk_vectors,
        emb_count,
    )

    f32, bf16 = F32, BF

    def shape(rows, dtype):
        return jax.ShapeDtypeStruct((rows, D), dtype)

    got = swap(give, "emb", emb_count, 1)
    own, give, sums = vmem_call(
        core_kernel, (shape(PIECE_ROWS, f32), shape(PIECE_ROWS + VEC_ROWS, bf16), shape(16, f32))
    )(keep, got, sums)
    got = swap(give, "emb", emb_count, 2)
    half = (shape(STEM_ROWS, f32), shape(STEM_ROWS + VEC_ROWS, bf16), shape(16, f32))
    own, give, sums = vmem_call(halve_kernel, half, scalars=1)(pos, own, got, sums)
    got = swap(give, "dp", dp_count, 1)
    bits = [1 << i for i in range(1, dp_count.bit_length() - 1)]
    if len(bits) == 2:
        bits[1] = bits[0] | bits[1]
    for mask in bits:
        own, give, sums = vmem_call(level_kernel, half)(own, got, sums)
        got = swap(give, "dp", dp_count, mask)
    own, sums = vmem_call(last_kernel, (shape(STEM_ROWS, bf16), shape(16, f32)))(own, got, sums)
    other = swap(own, "dp", dp_count, 1)
    trunk = jnp.where(dp_me % 2 == 0, own[:TRUNK_ROWS], other[:TRUNK_ROWS])
    trunks = spread(trunk)

    def like(array, copy):
        made = [jax.ShapeDtypeStruct(array.shape, F32)] * 3
        return made + ([jax.ShapeDtypeStruct(array.shape, BF)] if copy else [])

    stem_made = vmem_call(
        functools.partial(renew_stem, token_total),
        like(stem_mats[0], True)
        + like(stem_queries[0], True)
        + like(trunk_vectors, False)
        + [jax.ShapeDtypeStruct((2, D), F32)],
        scalars=1,
    )(
        pos,
        own,
        other,
        sums,
        stem_mats[0],
        stem_momentum[0],
        stem_average[0],
        stem_queries[0],
        queries_momentum[0],
        queries_average[0],
        trunk_vectors,
        vectors_momentum,
        vectors_average,
    )
    trunk_made = vmem_call(
        functools.partial(renew_trunk, token_total),
        like(trunk_mats, True) + like(trunk_down, True),
        [pltpu.VMEM((emb_count, TRUNK_ROWS, D), F32)],
        scalars=1,
    )(
        pos,
        *trunks,
        trunk_mats,
        mats_momentum,
        mats_average,
        trunk_down,
        down_momentum,
        down_average,
    )
    stems_new = [part[None] for part in stem_made[:8]]
    return (
        output,
        rows_grad.reshape(stem_rows.shape),
        *trunk_made,
        *stem_made[8:11],
        *stems_new,
        stem_made[11],
    )


def solution(mesh):
    split = P(("dp", "emb"))
    stem = P("emb")
    in_specs = (split,) * 4 + (P(),) * 9 + (stem,) * 6
    out_specs = (split,) * 2 + (P(),) * 11 + (stem,) * 8 + (P(),)
    return jax.shard_map(local, mesh=mesh, in_specs=in_specs, out_specs=out_specs, check_vma=False)
```

```python
import functools
import math

import jax
import jax.numpy as jnp
from jax import lax
from jax.experimental import pallas as pl
from jax.experimental.pallas import tpu as pltpu
from jax.sharding import PartitionSpec as P

D = 128
FF = 512
HEADS = 8
HEAD_DIM = 16
QUERIES = 32
STEPS = 4
STEP = 4
TOK_SEQ = 128
ROWS_SEQ = 256
PAIRS = HEADS // 2

NORM_EPSILON = 1e-05
MOMENTUM_DECAY = 0.9
BASE_RATE = 0.1
HIDDEN_SCORE = -1e30
LAG = 1
SCALE = 1.0 / math.sqrt(HEAD_DIM)
LOG2E = math.log2(math.e)

TRUNK_ROWS = 384
STEM_ROWS = 416
VEC_ROWS = 32
PIECE_ROWS = TRUNK_ROWS + STEM_ROWS

BF = jnp.bfloat16
F32 = jnp.float32
VMEM_LIMIT = 44 * 1024 * 1024


def mm(a, b):
    return lax.dot_general(a, b, (((1,), (0,)), ((), ())), preferred_element_type=F32)


def mm_nt(a, b):
    return lax.dot_general(a, b, (((1,), (1,)), ((), ())), preferred_element_type=F32)


def scores_back(probs, grad, axis):
    product = probs * grad
    return (product - probs * jnp.sum(product, axis=axis, keepdims=True)).astype(BF)


def head_pair(source, j):
    pieces = []
    if j:
        pieces.append(jnp.zeros((32 * j, 256), BF))
    zero = jnp.zeros((16, 128), BF)
    one = source[32 * j : 32 * j + 16]
    two = source[32 * j + 16 : 32 * j + 32]
    pieces.append(jnp.concatenate([one, zero], axis=1))
    pieces.append(jnp.concatenate([zero, two], axis=1))
    if j < PAIRS - 1:
        pieces.append(jnp.zeros((128 - 32 * j - 32, 256), BF))
    return jnp.concatenate(pieces, axis=0)


def pair_rows(source, j):
    zero = jnp.zeros((16, 128), BF)
    one = source[32 * j : 32 * j + 16]
    two = source[32 * j + 16 : 32 * j + 32]
    return jnp.concatenate(
        [jnp.concatenate([one, zero], axis=1), jnp.concatenate([zero, two], axis=1)], axis=0
    )


def turn_pair(both):
    return jnp.concatenate([both[:, :128].T, both[:, 128:].T], axis=0)


def turn_all(wide):
    return jnp.concatenate(
        [turn_rows(wide[:, c : c + 128]) for c in range(0, wide.shape[1], 128)], axis=0
    )


def turn_rows(tall):
    return jnp.concatenate(
        [tall[i : i + 128].T for i in range(0, tall.shape[0], 128)], axis=1
    )


def pair_pick(both):
    return jnp.concatenate([both[:16, :128], both[16:, 128:]], axis=0)


def ready_kernel(
    mats_ref,
    down_ref,
    vec_ref,
    rel_ref,
    seg_ref,
    t_qkvT,
    t_qkv,
    t_o,
    t_oT,
    t_in,
    t_inT,
    t_dn,
    t_dnT,
    vecs,
    done_ref,
):
    done_ref[...] = jnp.zeros_like(done_ref)
    mats = mats_ref[...].astype(BF)
    for c in range(5):
        vecs[c] = jnp.broadcast_to(vec_ref[c : c + 1], (128, 128)).T
    corner = lax.broadcasted_iota(jnp.int32, (128, 16), 1)

    def beside(column):
        column = jnp.broadcast_to(column, (128, 16))
        high = column.astype(BF).astype(F32)
        return jnp.where(corner == 0, high, jnp.where(corner == 1, column - high, 0.0)).astype(BF)

    for c in range(7):
        where = 128 * c if c < 3 else 128 * (c + 1)
        block = mats[:, where : where + 128].astype(F32)
        gain, bias = (vecs[0], vecs[1]) if c < 3 else (vecs[2], vecs[3])
        scaled = (block * gain).astype(BF)
        shift = jnp.sum((block * bias).T, axis=1, keepdims=True)
        if c < 3:
            t_qkv[:, 128 * c : 128 * c + 128] = scaled
            t_qkvT[128 * c : 128 * c + 128, 0:128] = scaled.T
            t_qkvT[128 * c : 128 * c + 128, 128:144] = beside(shift)
        else:
            d = c - 3
            shift = shift + jnp.broadcast_to(vec_ref[5 + d : 6 + d], (128, 128)).T[:, 0:1]
            t_in[:, 128 * d : 128 * d + 128] = scaled
            t_inT[128 * d : 128 * d + 128, 0:128] = scaled.T
            t_inT[128 * d : 128 * d + 128, 128:144] = beside(shift)
    t_o[...] = mats[:, 384:512]
    t_oT[...] = mats[:, 384:512].T
    down = down_ref[...].astype(BF)
    t_dn[...] = down
    for c in range(4):
        t_dnT[:, 128 * c : 128 * c + 128] = down[128 * c : 128 * c + 128].T


def own_kernel(mats_ref, queries_ref, own_ref):
    for c in range(3):
        own_ref[128 * c : 128 * c + 128] = mats_ref[:, 128 * c : 128 * c + 128].astype(BF)
    own_ref[384:416] = queries_ref[...].astype(BF)


def main_kernel(
    group,
    rel_ref,
    seg_ref,
    rows_hbm,
    cot_hbm,
    own_ref,
    one_ref,
    two_ref,
    three_ref,
    mats_ref,
    t_qkvT,
    t_qkv,
    t_o,
    t_oT,
    t_in,
    t_inT,
    t_dn,
    t_dnT,
    vecs,
    out_hbm,
    late_hbm,
    back_ref,
    keep_ref,
    give_ref,
    sums_ref,
    s_k,
    s_qb,
    s_a2,
    s_vT,
    s_out,
    s_outT,
    a_qkv,
    a_o,
    a_in,
    a_dn,
    a_vec,
    a_a,
    a_v,
    a_out,
    pieces,
    rows_ref,
    cot_ref,
    out_ref,
    late_ref,
    sems,
):
    step = pl.program_id(0)
    steps = rows_ref.shape[0] // group

    def moves(g):
        here = pl.ds(g * group, group)
        ends = (
            (rows_hbm, rows_ref),
            (cot_hbm, cot_ref),
            (out_ref, out_hbm),
            (late_ref, late_hbm),
        )
        return [
            pltpu.make_async_copy(one.at[here], two.at[here], sems.at[i, g])
            for i, (one, two) in enumerate(ends)
        ]

    @pl.when(step == 0)
    def _():
        for g in range(steps):
            for move in moves(g)[:2]:
                move.start()


    head_mask = (
        lax.broadcasted_iota(jnp.int32, (256, 128), 0) // 32
        == lax.broadcasted_iota(jnp.int32, (256, 128), 1) // 16
    )

    @pl.when(step == 0)
    def _():
        for k, ref in enumerate((own_ref, one_ref, two_ref, three_ref)):
            wk, wv, wo = ref[0:128], ref[128:256], ref[256:384]
            queries = ref[384:416].astype(F32)
            tiled = jnp.where(head_mask, jnp.concatenate([queries] * HEADS, axis=0), 0.0)
            block = tiled.T.astype(BF)
            both = mm(wk, block) * SCALE
            s_k[k] = wk
            s_qb[k] = block
            back_ref[k, 0:256] = both.T.astype(BF)
            back_ref[k, 256:384] = wv.T
            s_a2[k] = (both * LOG2E).astype(BF)
            s_vT[k] = wv.T
            s_out[k] = wo
            s_outT[k] = wo.T
        for ref in (a_qkv, a_o, a_in, a_dn, a_vec, a_a, a_v, a_out):
            ref[...] = jnp.zeros_like(ref)

    for move in moves(step)[:2]:
        move.wait()
    first = step * group
    lane_block = lax.broadcasted_iota(jnp.int32, (1, 128), 1) // 32
    ones = jnp.ones((16, 128), BF)
    zero = jnp.zeros((16, 128), BF)
    c0 = math.sqrt(2.0 / math.pi)
    c1 = c0 * 0.044715
    LOW_M0, LOW_M1, LOW_ONE, LOW_2C0, LOW_6C1 = [
        jnp.bfloat16(value)
        for value in (-2.0 * LOG2E * c0, -2.0 * LOG2E * c1, 1.0, 2.0 * c0, 6.0 * c1)
    ]
    masks = [(lane_block == c).astype(BF) for c in range(4)]
    lane_head = lax.broadcasted_iota(jnp.int32, (1, 128), 1) // 16
    head_lanes = [(lane_head == h).astype(BF) for h in range(HEADS)]
    at_block = [lane_block == c for c in range(4)]
    kept = {name: [] for name in ("normed", "gradp", "mixed", "branch", "normed2", "inner", "cot", "active", "sums")}

    def flow(seqs):
        every = range(len(seqs))
        rels = [rel_ref[first + b] for b in seqs]
        lanes = [slice(128 * b, 128 * b + 128) for b in every]
        scores = [mm(rows_ref[first + b], s_a2[e]) for b, e in zip(seqs, rels)]
        rows_T = [rows_ref[first + b].T for b in seqs]
        value_T = [mm(s_vT[e], rows_T[i]).astype(BF) for i, e in enumerate(rels)]
        yield
        probs, probs_low = [], []
        for b in every:
            probs.append([])
            probs_low.append([])
            for s in range(STEPS):
                halves = []
                for u in range(2):
                    tile = scores[b][64 * s : 64 * s + 64, 128 * u : 128 * u + 128]
                    raised = jnp.exp2(tile - jnp.max(tile, axis=0, keepdims=True))
                    halves.append(raised * (1.0 / jnp.sum(raised, axis=0, keepdims=True)))
                probs[b].append(halves)
                probs_low[b].append([half.astype(BF) for half in halves])
        stem_values = [value_T[b].T for b in every]
        yield
        made = []
        gap = jnp.zeros((64, 128), BF)
        for b in every:
            made.append([])
            for t in range(2):
                made[b].append([])
                for u in range(2):
                    block = jnp.concatenate(
                        [
                            jnp.concatenate([probs_low[b][2 * t][u], gap], axis=1),
                            jnp.concatenate([gap, probs_low[b][2 * t + 1][u]], axis=1),
                        ],
                        axis=0,
                    )
                    made[b][t].append(
                        mm(value_T[b][64 * u : 64 * u + 64, 128 * t : 128 * t + 128], block)
                    )
        stem_mixed = []
        for b in every:
            rows = []
            for h in range(HEADS):
                u, c = divmod(h, 4)
                row = None
                for s in range(STEPS):
                    piece = made[b][s // 2][u][
                        16 * c : 16 * c + 16, 128 * (s % 2) : 128 * (s % 2) + 128
                    ]
                    turn = (s - c) % 4
                    if turn:
                        piece = pltpu.roll(piece, 32 * turn, 1)
                    row = piece if row is None else jnp.where(at_block[s], piece, row)
                rows.append(row)
            stem_mixed.append(jnp.concatenate(rows, axis=0).astype(BF))
        yield
        residual = [mm(s_outT[rels[b]], stem_mixed[b]) for b in every]
        yield

        def norm(values):
            units, inverses = [], []
            for value in values:
                centered = value - jnp.mean(value, axis=0, keepdims=True)
                inverse = lax.rsqrt(
                    jnp.mean(centered * centered, axis=0, keepdims=True) + NORM_EPSILON
                )
                units.append(centered * inverse)
                inverses.append(inverse)
            low = jnp.concatenate([unit.astype(BF) for unit in units], axis=1)
            return units, inverses, jnp.concatenate([low, jnp.ones((16, low.shape[1]), BF)], axis=0)

        def norm_back(gradient, unit, inverse):
            mean_one = jnp.mean(gradient, axis=0, keepdims=True)
            mean_two = jnp.mean(gradient * unit, axis=0, keepdims=True)
            return inverse * (gradient - mean_one - unit * mean_two)

        unit_one, inverse_one, normed = norm(residual)
        yield
        projected = mm(t_qkvT[...], normed)
        query_T = [(projected[:128, lanes[b]] * (LOG2E * SCALE)).astype(BF) for b in every]
        key_T = [projected[128:256, lanes[b]].astype(BF) for b in every]
        value_T = [projected[256:, lanes[b]].astype(BF) for b in every]
        keys = [key_T[b].T for b in every]
        values = [value_T[b].T for b in every]
        hide = []
        for b in seqs:
            marks = [seg_ref[(first + b) * STEPS + s] for s in range(STEPS)]
            lane_marks = jnp.where(
                at_block[0],
                marks[0],
                jnp.where(at_block[1], marks[1], jnp.where(at_block[2], marks[2], marks[3])),
            )
            hide.append([jnp.where(lane_marks == marks[s], 0.0, HIDDEN_SCORE) for s in range(STEPS)])
        yield
        scores = [[mm(keys[b], head_pair(query_T[b], j)) for j in range(PAIRS)] for b in every]
        cot_list = [cot_ref[first + b].T for b in seqs]
        yield
        raised = []
        for b in every:
            raised.append([])
            for j in range(PAIRS):
                halves = []
                for u in range(2):
                    tile = scores[b][j][:, 128 * u : 128 * u + 128]
                    tile = jnp.concatenate(
                        [tile[32 * s : 32 * s + 32] + hide[b][s] for s in range(STEPS)], axis=0
                    )
                    halves.append(
                        jnp.exp2(tile - jnp.max(tile, axis=0, keepdims=True)).astype(BF)
                    )
                raised[b].append(jnp.concatenate(halves, axis=1))
        yield
        made = [
            [
                mm(jnp.concatenate([value_T[b][32 * j : 32 * j + 32], ones], axis=0), raised[b][j])
                for j in range(PAIRS)
            ]
            for b in every
        ]
        head_mixed, head_inverse, mixed_list = [], [], []
        for b in every:
            head_mixed.append([])
            head_inverse.append([])
            for h in range(HEADS):
                j, u = divmod(h, 2)
                here = slice(128 * u, 128 * u + 128)
                inverse = 1.0 / made[b][j][32:40, here]
                part = made[b][j][16 * u : 16 * u + 16, here]
                head_inverse[b].append(inverse)
                head_mixed[b].append(
                    jnp.concatenate([part[:8] * inverse, part[8:] * inverse], axis=0)
                )
            mixed_list.append(jnp.concatenate(head_mixed[b], axis=0).astype(BF))
        mixed = jnp.concatenate(mixed_list, axis=1)
        yield
        branch = mm(t_oT[...], mixed)
        hidden = [residual[b] + branch[:, lanes[b]] for b in every]
        yield
        unit_two, inverse_two, normed_two = norm(hidden)
        cot = jnp.concatenate(cot_list, axis=1)
        yield
        inner_all = mm(t_inT[...], normed_two)
        grad_all = mm(t_dn[...], cot)
        yield
        active_rows, grad_rows = [], []
        for r in range(0, FF, 16):
            active_cols, grad_cols = [], []
            for b in every:
                inner = inner_all[r : r + 16, lanes[b]].astype(BF)
                square = inner * inner
                bend = jnp.exp2(inner * (LOW_M0 + LOW_M1 * square))
                rise = pl.reciprocal(LOW_ONE + bend, approx=True)
                active = inner * rise
                slope = rise + (active - active * rise) * (LOW_2C0 + LOW_6C1 * square)
                active_cols.append(active)
                grad_cols.append(grad_all[r : r + 16, lanes[b]].astype(BF) * slope)
            active_rows.append(jnp.concatenate(active_cols, axis=1))
            grad_rows.append(jnp.concatenate(grad_cols, axis=1))
        active = jnp.concatenate(active_rows, axis=0)
        grad_inner = jnp.concatenate(grad_rows, axis=0)
        yield
        grad_all = mm(t_in[...], grad_inner)
        output_all = mm(t_dnT[...], active)
        turn_inner, turn_active = turn_all(grad_inner), turn_all(active)
        yield

        grad_hidden = []
        for b in every:
            grad_hidden.append(
                cot_list[b].astype(F32)
                + norm_back(grad_all[:, lanes[b]], unit_two[b], inverse_two[b])
            )
        grad_branch = jnp.concatenate([part.astype(BF) for part in grad_hidden], axis=1)
        yield
        grad_mixed = mm(t_o[...], grad_branch)
        sums = [jnp.zeros((128, 128), F32)] * 3
        for i, b in enumerate(seqs):
            output = hidden[i] + output_all[:, lanes[i]] + vecs[4]
            out_ref[first + b] = output.astype(BF).T
            sums = [
                sums[0] + cot_list[i].astype(F32),
                sums[1] + output,
                sums[2] + output * output,
            ]
        kept["sums"].append(sums)
        grad_T, drops = [], []
        for b in every:
            scaled = []
            drops.append([])
            for h in range(HEADS):
                inverse = head_inverse[b][h]
                part = grad_mixed[16 * h : 16 * h + 16, lanes[b]]
                part = jnp.concatenate([part[:8] * inverse, part[8:] * inverse], axis=0)
                scaled.append(part.astype(BF))
                drops[b].append(jnp.sum(part * head_mixed[b][h], axis=0, keepdims=True))
            grad_T.append(jnp.concatenate(scaled, axis=0))
        yield
        grad_probs = [[mm(values[b], head_pair(grad_T[b], j)) for j in range(PAIRS)] for b in every]
        grad_values = [
            [mm(pair_rows(grad_T[b], j), turn_pair(raised[b][j])) for j in range(PAIRS)] for b in every
        ]
        yield
        grad_scores = []
        for b in every:
            grad_scores.append([])
            for j in range(PAIRS):
                halves = []
                for u in range(2):
                    here = slice(128 * u, 128 * u + 128)
                    tile = grad_probs[b][j][:, here] - drops[b][2 * j + u]
                    halves.append(tile.astype(BF) * raised[b][j][:, here])
                grad_scores[b].append(jnp.concatenate(halves, axis=1))
        yield
        grad_queries = [
            [pair_pick(mm(key_T[b][32 * j : 32 * j + 32], grad_scores[b][j])) for j in range(PAIRS)]
            for b in every
        ]
        grad_keys = [
            [mm(pair_rows(query_T[b], j), turn_pair(grad_scores[b][j])) for j in range(PAIRS)] for b in every
        ]
        grad_list = []
        for b in every:
            grad_list.append(
                jnp.concatenate(
                    [
                        (jnp.concatenate(grad_queries[b], axis=0) * SCALE).astype(BF),
                        (jnp.concatenate(grad_keys[b], axis=0) * (1.0 / LOG2E)).astype(BF),
                        jnp.concatenate(grad_values[b], axis=0).astype(BF),
                    ],
                    axis=0,
                )
            )
        grad_projected = jnp.concatenate(grad_list, axis=1)
        yield
        grad_all = mm(t_qkv[...], grad_projected)
        for name, value in (
            ("normed", normed),
            ("gradp", turn_all(grad_projected)),
            ("mixed", mixed),
            ("branch", grad_branch),
            ("normed2", normed_two),
            ("inner", turn_inner),
            ("cot", cot),
            ("active", turn_active),
        ):
            kept[name].append(value)
        yield
        grad_tokens = [
            (grad_hidden[b] + norm_back(grad_all[:, lanes[b]], unit_one[b], inverse_one[b])).astype(BF)
            for b in every
        ]
        yield

        grad_mixed = [mm(s_out[rels[b]], grad_tokens[b]) for b in every]
        for b in every:
            a_out[rels[b]] += mm_nt(stem_mixed[b], grad_tokens[b])
        yield
        spread, tall = [], []
        for b in every:
            spread.append([])
            mixed_tok = grad_mixed[b].astype(BF).T
            tall.append(
                [
                    jnp.concatenate(
                        [mixed_tok[32 * s : 32 * s + 32] * head_lanes[h] for h in range(HEADS)],
                        axis=0,
                    )
                    for s in range(STEPS)
                ]
            )
            turned = [grad_mixed[b].astype(BF)] + [
                pltpu.roll(grad_mixed[b], 32 * k, 1).astype(BF) for k in range(1, 4)
            ]
            for s in range(STEPS):
                pieces = []
                for h in range(HEADS):
                    c = h % 4
                    piece = turned[(c - s) % 4][16 * h : 16 * h + 16] * masks[c]
                    pieces.append(
                        jnp.concatenate([piece, zero] if h < 4 else [zero, piece], axis=1)
                    )
                spread[b].append(jnp.concatenate(pieces, axis=0))
        yield
        grad_probs = [
            [mm(stem_values[b][64 * s : 64 * s + 64], spread[b][s]) for s in range(STEPS)]
            for b in every
        ]
        grad_values = [
            jnp.concatenate(
                [
                    mm(jnp.concatenate(probs_low[b][s], axis=1), tall[b][s]).astype(BF)
                    for s in range(STEPS)
                ],
                axis=0,
            )
            for b in every
        ]
        yield
        grad_scores = []
        for b in every:
            steps = []
            for s in range(STEPS):
                steps.append(
                    jnp.concatenate(
                        [
                            scores_back(probs[b][s][u], grad_probs[b][s][:, 128 * u : 128 * u + 128], 0)
                            for u in range(2)
                        ],
                        axis=1,
                    )
                )
            grad_scores.append(jnp.concatenate(steps, axis=0))
        yield
        for i, b in enumerate(seqs):
            e = rels[i]
            late_ref[first + b, :, 0:256] = grad_scores[i]
            late_ref[first + b, :, 256:384] = grad_values[i]
            rows_T = rows_ref[first + b].T
            a_a[e] += mm(rows_T, grad_scores[i])
            a_v[e] += mm(rows_T, grad_values[i])

    part = 2
    flows = [flow(range(part * g, part * g + part)) for g in range(group // part)]
    live, wave = len(flows), 0
    while live:
        live = 0
        for g, one in enumerate(flows):
            if wave < LAG * g:
                live += 1
                continue
            try:
                next(one)
                live += 1
            except StopIteration:
                pass
        wave += 1

    for move in moves(step)[2:]:
        move.start()

    def side(name):
        return jnp.concatenate(kept[name], axis=1)

    def stack(name):
        return jnp.concatenate(kept[name], axis=0)

    a_dn[...] += mm(side("cot"), stack("active"))
    a_in[...] += mm(side("normed2"), stack("inner"))
    a_o[...] += mm_nt(side("mixed"), side("branch"))
    a_qkv[...] += mm(side("normed"), stack("gradp"))
    for c in range(3):
        total = kept["sums"][0][c]
        for sums in kept["sums"][1:]:
            total = total + sums[c]
        a_vec[c] += total

    @pl.when(step == pl.num_programs(0) - 1)
    def _():
        me = lax.axis_index("emb")

        def exact(left, right):
            high = left.astype(BF)
            return mm(high, right) + mm((left - high.astype(F32)).astype(BF), right)

        mats = mats_ref[...].astype(BF).astype(F32)
        blocks, gains, biases = [], [None, None], [None, None]
        for c in range(8):
            if c == 3:
                blocks.append(a_o[...])
                continue
            n = 0 if c < 3 else 1
            ref, where = (a_qkv, 128 * c) if c < 3 else (a_in, 128 * (c - 4))
            summed = ref[0:128, where : where + 128]
            ones_row = jnp.broadcast_to(ref[128:129, where : where + 128], (128, 128))
            weight = mats[:, 128 * c : 128 * c + 128]
            blocks.append(summed * vecs[2 * n] + ones_row * vecs[2 * n + 1])
            gain, bias = weight * summed, weight * ones_row
            gains[n] = gain if gains[n] is None else gains[n] + gain
            biases[n] = bias if biases[n] is None else biases[n] + bias
        blocks += [a_dn[:, 128 * c : 128 * c + 128].T for c in range(4)]
        count, per = 4, len(blocks) // 4

        for j in range(count):
            place = jnp.bitwise_xor(me, j)
            for i in range(per):
                pieces[place, 128 * i : 128 * i + 128] = blocks[per * j + i]
        for k in range(count):
            here = slice(PIECE_ROWS * (k // 2), PIECE_ROWS * (k // 2) + TRUNK_ROWS)
            if k % 2:
                give_ref[here] = pieces[k].astype(BF)
            else:
                keep_ref[here] = pieces[k]
        columns = [gains[0], biases[0], gains[1], biases[1], a_vec[0]]
        sums = [jnp.sum(column.T, axis=0, keepdims=True) for column in columns]
        sums += [a_in[128:129, 128 * c : 128 * c + 128] for c in range(4)]
        sums += [jnp.sum(a_vec[c].T, axis=0, keepdims=True) for c in (1, 2)]
        sums.append(jnp.zeros((5, 128), F32))
        sums = jnp.concatenate(sums, axis=0)
        high, low = split_sum(sums)
        sums_ref[...] = sums
        give_ref[2 * PIECE_ROWS : 2 * PIECE_ROWS + 16] = high
        give_ref[2 * PIECE_ROWS + 16 : 2 * PIECE_ROWS + 32] = low
        for k in range(count):
            grad = a_a[k] * SCALE
            grad_high = grad.astype(BF)
            grad_low = (grad - grad_high.astype(F32)).astype(BF)
            key_T = s_k[k].T
            spread = (mm(key_T, grad_high) + mm(key_T, grad_low)).T
            spread = jnp.where(head_mask, spread, 0.0)
            query = spread[0:32]
            for h in range(1, HEADS):
                query = query + spread[32 * h : 32 * h + 32]
            parts = [
                mm_nt(grad_high, s_qb[k]) + mm_nt(grad_low, s_qb[k]),
                a_v[k],
                a_out[k],
                query,
            ]
            base = PIECE_ROWS * (k // 2) + TRUNK_ROWS
            for i, value in enumerate(parts):
                here = slice(base + 128 * i, base + 128 * i + value.shape[0])
                if k % 2:
                    give_ref[here] = value.astype(BF)
                else:
                    keep_ref[here] = value
        for g in range(steps):
            for move in moves(g)[2:]:
                move.wait()


def rows_kernel(group, rel_ref, late_ref, back_ref, after_ref, out_ref, done_ref):
    step = pl.program_id(0)
    done_ref[...] = jnp.zeros_like(done_ref)
    for b in range(group):
        out_ref[b] = mm(late_ref[b], back_ref[rel_ref[step * group + b]]).astype(BF)


def run_rows(rel, late, back, after, group=8):
    seqs = late.shape[0]
    flops = 2 * seqs * ROWS_SEQ * 3 * D * D
    return pl.pallas_call(
        functools.partial(rows_kernel, group),
        out_shape=(
            jax.ShapeDtypeStruct((seqs, ROWS_SEQ, D), BF),
            jax.ShapeDtypeStruct((8, D), F32),
        ),
        grid_spec=pltpu.PrefetchScalarGridSpec(
            num_scalar_prefetch=1,
            grid=(seqs // group,),
            in_specs=[
                pl.BlockSpec((group, ROWS_SEQ, 3 * D), lambda i, *_: (i, 0, 0)),
                pl.BlockSpec(back.shape, lambda i, *_: (0, 0, 0)),
                pl.BlockSpec(memory_space=pl.ANY),
            ],
            out_specs=(
                pl.BlockSpec((group, ROWS_SEQ, D), lambda i, *_: (i, 0, 0)),
                pl.BlockSpec((8, D), lambda i, *_: (0, 0)),
            ),
        ),
        cost_estimate=pl.CostEstimate(flops=flops, bytes_accessed=16 * 1024 * 1024, transcendentals=0),
        compiler_params=pltpu.CompilerParams(
            vmem_limit_bytes=16 * 1024 * 1024, dimension_semantics=("arbitrary",)
        ),
    )(rel, late, back, after)


def split_sum(sums):
    high = sums.astype(BF)
    return high, (sums - high.astype(F32)).astype(BF)


def add_sums(sums_ref, got_ref, start, next_ref, give_ref, give_start):
    total = sums_ref[...] + (
        got_ref[start : start + 16].astype(F32) + got_ref[start + 16 : start + 32].astype(F32)
    )
    next_ref[...] = total
    if give_ref is not None:
        high, low = split_sum(total)
        give_ref[give_start : give_start + 16] = high
        give_ref[give_start + 16 : give_start + 32] = low


def core_kernel(keep_ref, got_ref, sums_ref, own_ref, give_ref, next_ref):
    own_ref[...] = keep_ref[0:PIECE_ROWS] + got_ref[0:PIECE_ROWS].astype(F32)
    give_ref[0:PIECE_ROWS] = (
        keep_ref[PIECE_ROWS : 2 * PIECE_ROWS] + got_ref[PIECE_ROWS : 2 * PIECE_ROWS].astype(F32)
    ).astype(BF)
    add_sums(sums_ref, got_ref, 2 * PIECE_ROWS, next_ref, give_ref, PIECE_ROWS)


def halve_kernel(keep_ref, got_ref, sums_ref, after_ref, own_ref, give_ref, next_ref):
    odd = lax.rem(lax.axis_index("dp"), 2)
    trunk = keep_ref[0:TRUNK_ROWS] + got_ref[0:TRUNK_ROWS].astype(F32)
    stem = keep_ref[TRUNK_ROWS:] + got_ref[TRUNK_ROWS:PIECE_ROWS].astype(F32)
    rest = jnp.zeros((STEM_ROWS - TRUNK_ROWS, D), F32)
    trunk = jnp.concatenate([trunk, rest], axis=0)
    own_ref[...] = jnp.where(odd == 0, trunk, stem)
    give_ref[0:STEM_ROWS] = jnp.where(odd == 0, stem, trunk).astype(BF)
    add_sums(sums_ref, got_ref, PIECE_ROWS, next_ref, give_ref, STEM_ROWS)


def level_kernel(keep_ref, got_ref, sums_ref, own_ref, give_ref, next_ref):
    total = keep_ref[...] + got_ref[0:STEM_ROWS].astype(F32)
    own_ref[...] = total
    give_ref[0:STEM_ROWS] = total.astype(BF)
    add_sums(sums_ref, got_ref, STEM_ROWS, next_ref, give_ref, STEM_ROWS)


def last_kernel(keep_ref, got_ref, sums_ref, own_ref, next_ref):
    own_ref[...] = (keep_ref[...] + got_ref[0:STEM_ROWS].astype(F32)).astype(BF)
    add_sums(sums_ref, got_ref, STEM_ROWS, next_ref, None, 0)


def renew(weight, moment, average, gradient, step_rate):
    new_moment = MOMENTUM_DECAY * moment + gradient
    new_weight = weight - step_rate * (gradient + MOMENTUM_DECAY * new_moment)
    new_average = average + (new_weight - average) / (STEP + 1)
    return (new_moment, new_average, new_weight)


def put_new(outs, where, made):
    outs[0][where], outs[1][where], outs[2][where] = made
    if len(outs) > 3:
        outs[3][where] = made[2].astype(BF)


def renew_stem(token_total, own_ref, got_ref, sums_ref, *refs):
    stem_in, quer_in, vec_in = refs[0:3], refs[3:6], refs[6:9]
    stem_o, quer_o, vec_o, stats_o = refs[9:13], refs[13:17], refs[17:20], refs[20]
    refs[21][...] = jnp.zeros_like(refs[21])
    rate = BASE_RATE / math.sqrt(token_total)
    odd = lax.rem(lax.axis_index("dp"), 2) == 1
    full = (slice(None), slice(None))
    for i in range(3):
        where = (slice(None), slice(128 * i, 128 * i + 128))
        rows = slice(128 * i, 128 * i + 128)
        grad = jnp.where(odd, own_ref[rows].astype(F32), got_ref[rows].astype(F32))
        put_new(stem_o, where, renew(*[ref[where] for ref in stem_in], grad, rate))
    grad = jnp.where(odd, own_ref[384:416].astype(F32), got_ref[384:416].astype(F32))
    put_new(quer_o, full, renew(*[ref[...] for ref in quer_in], grad, rate))
    put_new(vec_o, full, renew(*[ref[...] for ref in vec_in], sums_ref[0:9], rate))
    mean = sums_ref[9:10] / token_total
    stats_o[0:1] = mean
    stats_o[1:2] = sums_ref[10:11] / token_total - mean * mean


def pass_kernel(in_ref, after_ref, out_ref):
    out_ref[...] = in_ref[...]


def renew_trunk(token_total, *refs):
    trunk_refs, mats_in, down_in = refs[0:4], refs[4:7], refs[7:10]
    mats_o, down_o, pieces = refs[10:14], refs[14:18], refs[18]
    rate = BASE_RATE / math.sqrt(token_total)
    for k, ref in enumerate(trunk_refs):
        pieces[jnp.bitwise_xor(lax.axis_index("emb"), k)] = ref[...].astype(F32)

    def block(i):
        return pieces[i // 3, 128 * (i % 3) : 128 * (i % 3) + 128]

    for i in range(8):
        where = (slice(None), slice(128 * i, 128 * i + 128))
        put_new(mats_o, where, renew(*[ref[where] for ref in mats_in], block(i), rate))
    for i in range(4):
        where = (slice(128 * i, 128 * i + 128), slice(None))
        put_new(down_o, where, renew(*[ref[where] for ref in down_in], block(8 + i), rate))


def vmem_call(kernel, outs, scratch=(), scalars=0, cost=None, after=0):
    in_vmem = pl.BlockSpec(memory_space=pltpu.VMEM)

    def call(*args):
        return pl.pallas_call(
            kernel,
            out_shape=outs,
            in_specs=[pl.BlockSpec(memory_space=pltpu.SMEM)] * scalars
            + [in_vmem] * (len(args) - scalars - after)
            + [pl.BlockSpec(memory_space=pl.ANY)] * after,
            out_specs=jax.tree.map(lambda _: in_vmem, outs),
            scratch_shapes=list(scratch),
            cost_estimate=cost,
            compiler_params=pltpu.CompilerParams(vmem_limit_bytes=8 * 1024 * 1024),
        )(*args)

    return call


def in_hbm(value):
    return pltpu.with_memory_space_constraint(value, pltpu.HBM)


def run_ready(mats, down, vectors, rel, segments):
    shapes = [
        ((384, 144), BF),
        ((128, 384), BF),
        ((128, 128), BF),
        ((128, 128), BF),
        ((128, 512), BF),
        ((512, 144), BF),
        ((512, 128), BF),
        ((128, 512), BF),
        ((5, 128, 128), F32),
        ((8, 128), F32),
    ]
    return vmem_call(
        ready_kernel,
        [jax.ShapeDtypeStruct(*shape) for shape in shapes],
        cost=pl.CostEstimate(flops=0, bytes_accessed=8 * 1024 * 1024, transcendentals=0),
        after=2,
    )(in_hbm(mats), in_hbm(down), in_hbm(vectors), rel, segments)


def run_main(rel, segments, rows, cot, stems, mats, ready, emb_count):
    seqs = rows.shape[0]
    group = 16
    steps = seqs // group

    def whole(shape, mode=None):
        return pl.BlockSpec(shape, lambda i, *_: (0,) * len(shape), pipeline_mode=mode)

    scratch = [
        ((4, 128, 128), BF),
        ((4, 128, 256), BF),
        ((4, 128, 256), BF),
        ((4, 128, 128), BF),
        ((4, 128, 128), BF),
        ((4, 128, 128), BF),
        ((144, 384), F32),
        ((128, 128), F32),
        ((144, 512), F32),
        ((128, 512), F32),
        ((3, 128, 128), F32),
        ((4, 128, 256), F32),
        ((4, 128, 128), F32),
        ((4, 128, 128), F32),
        ((4, TRUNK_ROWS, D), F32),
        ((seqs, ROWS_SEQ, D), BF),
        ((seqs, TOK_SEQ, D), BF),
        ((seqs, TOK_SEQ, D), BF),
        ((seqs, ROWS_SEQ, 3 * D), BF),
    ]
    anywhere = pl.BlockSpec(memory_space=pl.ANY)
    return pl.pallas_call(
        functools.partial(main_kernel, group),
        out_shape=(
            jax.ShapeDtypeStruct((seqs, TOK_SEQ, D), BF),
            jax.ShapeDtypeStruct((seqs, ROWS_SEQ, 3 * D), BF),
            jax.ShapeDtypeStruct((emb_count, 3 * D, D), BF),
            jax.ShapeDtypeStruct((2 * PIECE_ROWS, D), F32),
            jax.ShapeDtypeStruct((2 * PIECE_ROWS + VEC_ROWS, D), BF),
            jax.ShapeDtypeStruct((16, D), F32),
        ),
        grid_spec=pltpu.PrefetchScalarGridSpec(
            num_scalar_prefetch=2,
            grid=(steps,),
            in_specs=[anywhere, anywhere]
            + [whole((STEM_ROWS, D))] * 4
            + [whole((D, 1024))]
            + [whole(value.shape, pl.Buffered(1)) for value in ready],
            out_specs=(
                anywhere,
                anywhere,
                whole((emb_count, 3 * D, D)),
                whole((2 * PIECE_ROWS, D)),
                whole((2 * PIECE_ROWS + VEC_ROWS, D)),
                whole((16, D)),
            ),
            scratch_shapes=[pltpu.VMEM(shape, dtype) for shape, dtype in scratch]
            + [pltpu.SemaphoreType.DMA((4, steps))],
        ),
        compiler_params=pltpu.CompilerParams(
            vmem_limit_bytes=VMEM_LIMIT, dimension_semantics=("arbitrary",)
        ),
    )(rel, segments, in_hbm(rows), in_hbm(cot), *stems, in_hbm(mats), *ready)


def local(
    stem_rows,
    emb_ids,
    segments,
    cotangent,
    trunk_mats,
    mats_momentum,
    mats_average,
    trunk_down,
    down_momentum,
    down_average,
    trunk_vectors,
    vectors_momentum,
    vectors_average,
    stem_mats,
    stem_momentum,
    stem_average,
    stem_queries,
    queries_momentum,
    queries_average,
):
    seqs = stem_rows.shape[0]
    emb_count, dp_count = lax.axis_size("emb"), lax.axis_size("dp")
    rel = emb_ids[:, 0] ^ lax.axis_index("emb")
    token_total = seqs * TOK_SEQ * dp_count * emb_count

    def swap(value, axis, count, mask):
        return lax.ppermute(value, axis, [(i, i ^ mask) for i in range(count)])

    own = vmem_call(own_kernel, jax.ShapeDtypeStruct((STEM_ROWS, D), BF))(
        in_hbm(stem_mats[0]), in_hbm(stem_queries[0])
    )
    segments = segments.reshape(-1)
    *ready, ready_done = run_ready(trunk_mats, trunk_down, trunk_vectors, rel, segments)
    near, far = swap(own, "emb", emb_count, 1), swap(own, "emb", emb_count, 2)
    far = vmem_call(pass_kernel, jax.ShapeDtypeStruct(far.shape, BF), after=1)(far, ready_done)
    stems = [own, near, far, swap(far, "emb", emb_count, 1)]

    output, late, back, keep, give, sums = run_main(
        rel,
        segments,
        stem_rows.reshape(seqs, ROWS_SEQ, D),
        cotangent,
        stems,
        trunk_mats,
        ready,
        emb_count,
    )

    f32, bf16 = F32, BF

    def shape(rows, dtype):
        return jax.ShapeDtypeStruct((rows, D), dtype)

    got = swap(give, "emb", emb_count, 1)
    own, give, sums = vmem_call(
        core_kernel, (shape(PIECE_ROWS, f32), shape(PIECE_ROWS + VEC_ROWS, bf16), shape(16, f32))
    )(keep, got, sums)
    got = swap(give, "emb", emb_count, 2)
    rows_grad, rows_done = run_rows(rel, late, back, give)
    half = (shape(STEM_ROWS, f32), shape(STEM_ROWS + VEC_ROWS, bf16), shape(16, f32))
    own, give, sums = vmem_call(halve_kernel, half, after=1)(
        own, got, sums, rows_done
    )
    got = swap(give, "dp", dp_count, 1)
    bits = [1 << i for i in range(1, dp_count.bit_length() - 1)]
    if len(bits) == 2:
        bits[1] = bits[0] | bits[1]
    for mask in bits:
        own, give, sums = vmem_call(level_kernel, half)(own, got, sums)
        got = swap(give, "dp", dp_count, mask)
    own, sums = vmem_call(last_kernel, (shape(STEM_ROWS, bf16), shape(16, f32)))(own, got, sums)
    other = swap(own, "dp", dp_count, 1)
    trunk = jnp.where(lax.axis_index("dp") % 2 == 0, own[:TRUNK_ROWS], other[:TRUNK_ROWS])
    far = swap(trunk, "emb", emb_count, 2)
    near = swap(trunk, "emb", emb_count, 1)

    def like(array, copy):
        made = [jax.ShapeDtypeStruct(array.shape, F32)] * 3
        return made + ([jax.ShapeDtypeStruct(array.shape, BF)] if copy else [])

    stem_made = vmem_call(
        functools.partial(renew_stem, token_total),
        like(stem_mats[0], True)
        + like(stem_queries[0], True)
        + like(trunk_vectors, False)
        + [jax.ShapeDtypeStruct((2, D), F32), jax.ShapeDtypeStruct((8, D), F32)],
        cost=pl.CostEstimate(flops=0, bytes_accessed=6 * 1024 * 1024, transcendentals=0),
    )(
        own,
        other,
        sums,
        stem_mats[0],
        stem_momentum[0],
        stem_average[0],
        stem_queries[0],
        queries_momentum[0],
        queries_average[0],
        trunk_vectors,
        vectors_momentum,
        vectors_average,
    )
    far = vmem_call(pass_kernel, jax.ShapeDtypeStruct(far.shape, far.dtype), after=1)(
        far, stem_made[12]
    )
    trunks = [trunk, near, far, swap(far, "emb", emb_count, 1)]
    trunk_made = vmem_call(
        functools.partial(renew_trunk, token_total),
        like(trunk_mats, True) + like(trunk_down, True),
        [pltpu.VMEM((emb_count, TRUNK_ROWS, D), F32)],
    )(
        *trunks,
        trunk_mats,
        mats_momentum,
        mats_average,
        trunk_down,
        down_momentum,
        down_average,
    )
    stems_new = [part[None] for part in stem_made[:8]]
    return (
        output,
        rows_grad.reshape(stem_rows.shape),
        *trunk_made,
        *stem_made[8:11],
        *stems_new,
        stem_made[11],
    )


def solution(mesh):
    split = P(("dp", "emb"))
    stem = P("emb")
    in_specs = (split,) * 4 + (P(),) * 9 + (stem,) * 6
    out_specs = (split,) * 2 + (P(),) * 11 + (stem,) * 8 + (P(),)
    return jax.shard_map(local, mesh=mesh, in_specs=in_specs, out_specs=out_specs, check_vma=False)
```

```python
import functools
import math

import jax
import jax.numpy as jnp
from jax import lax
from jax.experimental import pallas as pl
from jax.experimental.pallas import tpu as pltpu
from jax.sharding import PartitionSpec as P

D = 128
FF = 512
HEADS = 8
HEAD_DIM = 16
QUERIES = 32
STEPS = 4
STEP = 4
TOK_SEQ = 128
ROWS_SEQ = 256
PAIRS = HEADS // 2

NORM_EPSILON = 1e-05
MOMENTUM_DECAY = 0.9
BASE_RATE = 0.1
HIDDEN_SCORE = -1e30
LAG = 1
SCALE = 1.0 / math.sqrt(HEAD_DIM)
LOG2E = math.log2(math.e)

TRUNK_ROWS = 384
STEM_ROWS = 416
VEC_ROWS = 32
PIECE_ROWS = TRUNK_ROWS + STEM_ROWS

BF = jnp.bfloat16
F32 = jnp.float32
VMEM_LIMIT = 44 * 1024 * 1024


def mm(a, b):
    return lax.dot_general(a, b, (((1,), (0,)), ((), ())), preferred_element_type=F32)


def mm_nt(a, b):
    return lax.dot_general(a, b, (((1,), (1,)), ((), ())), preferred_element_type=F32)


def scores_back(probs, grad, axis):
    product = probs * grad
    return (product - probs * jnp.sum(product, axis=axis, keepdims=True)).astype(BF)


def head_pair(source, j):
    pieces = []
    if j:
        pieces.append(jnp.zeros((32 * j, 256), BF))
    zero = jnp.zeros((16, 128), BF)
    one = source[32 * j : 32 * j + 16]
    two = source[32 * j + 16 : 32 * j + 32]
    pieces.append(jnp.concatenate([one, zero], axis=1))
    pieces.append(jnp.concatenate([zero, two], axis=1))
    if j < PAIRS - 1:
        pieces.append(jnp.zeros((128 - 32 * j - 32, 256), BF))
    return jnp.concatenate(pieces, axis=0)


def pair_rows(source, j):
    zero = jnp.zeros((16, 128), BF)
    one = source[32 * j : 32 * j + 16]
    two = source[32 * j + 16 : 32 * j + 32]
    return jnp.concatenate(
        [jnp.concatenate([one, zero], axis=1), jnp.concatenate([zero, two], axis=1)], axis=0
    )


def turn_pair(both):
    return jnp.concatenate([both[:, :128].T, both[:, 128:].T], axis=0)


def turn_all(wide):
    return jnp.concatenate(
        [turn_rows(wide[:, c : c + 128]) for c in range(0, wide.shape[1], 128)], axis=0
    )


def turn_rows(tall):
    return jnp.concatenate(
        [tall[i : i + 128].T for i in range(0, tall.shape[0], 128)], axis=1
    )


def aslant(one, two):
    gap = jnp.zeros_like(one)
    return jnp.concatenate(
        [jnp.concatenate([one, gap], axis=1), jnp.concatenate([gap, two], axis=1)], axis=0
    )


def pair_pick(both):
    return jnp.concatenate([both[:16, :128], both[16:, 128:]], axis=0)


def query_block(ref):
    head_mask = (
        lax.broadcasted_iota(jnp.int32, (256, 128), 0) // 32
        == lax.broadcasted_iota(jnp.int32, (256, 128), 1) // 16
    )
    queries = ref[384:416].astype(F32)
    return jnp.where(head_mask, jnp.concatenate([queries] * HEADS, axis=0), 0.0).T.astype(BF)


def ready_kernel(
    mats_ref,
    down_ref,
    vec_ref,
    rel_ref,
    seg_ref,
    t_qkvT,
    t_qkv,
    t_o,
    t_oT,
    t_in,
    t_inT,
    t_dn,
    t_dnT,
    vecs,
    done_ref,
):
    done_ref[...] = jnp.zeros_like(done_ref)
    mats = mats_ref[...].astype(BF)
    for c in range(5):
        vecs[c] = jnp.broadcast_to(vec_ref[c : c + 1], (128, 128)).T
    corner = lax.broadcasted_iota(jnp.int32, (128, 16), 1)

    def beside(column):
        column = jnp.broadcast_to(column, (128, 16))
        high = column.astype(BF).astype(F32)
        return jnp.where(corner == 0, high, jnp.where(corner == 1, column - high, 0.0)).astype(BF)

    for c in range(7):
        where = 128 * c if c < 3 else 128 * (c + 1)
        block = mats[:, where : where + 128].astype(F32)
        gain, bias = (vecs[0], vecs[1]) if c < 3 else (vecs[2], vecs[3])
        scaled = (block * gain).astype(BF)
        shift = jnp.sum((block * bias).T, axis=1, keepdims=True)
        if c < 3:
            t_qkv[:, 128 * c : 128 * c + 128] = scaled
            t_qkvT[128 * c : 128 * c + 128, 0:128] = scaled.T
            t_qkvT[128 * c : 128 * c + 128, 128:144] = beside(shift)
        else:
            d = c - 3
            shift = shift + jnp.broadcast_to(vec_ref[5 + d : 6 + d], (128, 128)).T[:, 0:1]
            t_in[:, 128 * d : 128 * d + 128] = scaled
            t_inT[128 * d : 128 * d + 128, 0:128] = scaled.T
            t_inT[128 * d : 128 * d + 128, 128:144] = beside(shift)
    t_o[...] = mats[:, 384:512]
    t_oT[...] = mats[:, 384:512].T
    down = down_ref[...].astype(BF)
    t_dn[...] = down
    for c in range(4):
        t_dnT[:, 128 * c : 128 * c + 128] = down[128 * c : 128 * c + 128].T


def own_kernel(mats_ref, queries_ref, own_ref):
    for c in range(3):
        own_ref[128 * c : 128 * c + 128] = mats_ref[:, 128 * c : 128 * c + 128].astype(BF)
    own_ref[384:416] = queries_ref[...].astype(BF)


def main_kernel(
    group,
    rel_ref,
    seg_ref,
    rows_hbm,
    cot_hbm,
    own_ref,
    one_ref,
    two_ref,
    three_ref,
    mats_any,
    t_qkvT_any,
    t_qkv_any,
    t_o_any,
    t_oT_any,
    t_in_any,
    t_inT_any,
    t_dn_any,
    t_dnT_any,
    vecs_any,
    out_hbm,
    late_hbm,
    keep_ref,
    give_ref,
    sums_ref,
    s_a2,
    s_vT,
    s_out,
    s_outT,
    a_qkv,
    a_o,
    a_in,
    a_dn,
    a_vec,
    a_a,
    a_v,
    a_out,
    pieces,
    rows_ref,
    cot_ref,
    out_ref,
    late_ref,
    mats_ref,
    t_qkvT,
    t_qkv,
    t_o,
    t_oT,
    t_in,
    t_inT,
    t_dn,
    t_dnT,
    vecs,
    sems,
    more_sems,
):
    step = pl.program_id(0)
    ends = (
        (mats_any, mats_ref),
        (t_qkvT_any, t_qkvT),
        (t_qkv_any, t_qkv),
        (t_o_any, t_o),
        (t_oT_any, t_oT),
        (t_in_any, t_in),
        (t_inT_any, t_inT),
        (t_dn_any, t_dn),
        (t_dnT_any, t_dnT),
        (vecs_any, vecs),
    )
    weights = [
        pltpu.make_async_copy(one, two, more_sems.at[i]) for i, (one, two) in enumerate(ends)
    ]
    steps = rows_ref.shape[0] // group

    def moves(g):
        here = pl.ds(g * group, group)
        ends = (
            (rows_hbm, rows_ref),
            (cot_hbm, cot_ref),
            (out_ref, out_hbm),
            (late_ref, late_hbm),
        )
        return [
            pltpu.make_async_copy(one.at[here], two.at[here], sems.at[i, g])
            for i, (one, two) in enumerate(ends)
        ]

    @pl.when(step == 0)
    def _():
        for move in moves(0)[:2] + weights[1:]:
            move.start()
        for g in range(1, steps):
            for move in moves(g)[:2]:
                move.start()
        weights[0].start()


    head_mask = (
        lax.broadcasted_iota(jnp.int32, (256, 128), 0) // 32
        == lax.broadcasted_iota(jnp.int32, (256, 128), 1) // 16
    )

    @pl.when(step == 0)
    def _():
        for k, ref in enumerate((own_ref, one_ref, two_ref, three_ref)):
            wk, wv, wo = ref[0:128], ref[128:256], ref[256:384]
            s_a2[k] = (mm(wk, query_block(ref)) * (SCALE * LOG2E)).astype(BF)
            s_vT[k] = wv.T
            s_out[k] = wo
            s_outT[k] = wo.T
        for ref in (a_qkv, a_o, a_in, a_dn, a_vec, a_a, a_v, a_out):
            ref[...] = jnp.zeros_like(ref)
        for move in weights[1:]:
            move.wait()

    for move in moves(step)[:2]:
        move.wait()
    first = step * group
    lane_block = lax.broadcasted_iota(jnp.int32, (1, 128), 1) // 32
    ones = jnp.ones((16, 128), BF)
    zero = jnp.zeros((16, 128), BF)
    c0 = math.sqrt(2.0 / math.pi)
    c1 = c0 * 0.044715
    LOW_M0, LOW_M1, LOW_ONE, LOW_2C0, LOW_6C1 = [
        jnp.bfloat16(value)
        for value in (-2.0 * LOG2E * c0, -2.0 * LOG2E * c1, 1.0, 2.0 * c0, 6.0 * c1)
    ]
    masks = [(lane_block == c).astype(BF) for c in range(4)]
    lane_head = lax.broadcasted_iota(jnp.int32, (1, 128), 1) // 16
    head_lanes = [(lane_head == h).astype(BF) for h in range(HEADS)]
    at_block = [lane_block == c for c in range(4)]
    kept = {name: [] for name in ("normed", "gradp", "mixed", "branch", "normed2", "inner", "cot", "active", "sums")}

    def flow(seqs):
        every = range(len(seqs))
        rels = [rel_ref[first + b] for b in seqs]
        lanes = [slice(128 * b, 128 * b + 128) for b in every]
        scores = [mm(rows_ref[first + b], s_a2[e]) for b, e in zip(seqs, rels)]
        rows_T = [rows_ref[first + b].T for b in seqs]
        value_T = [mm(s_vT[e], rows_T[i]).astype(BF) for i, e in enumerate(rels)]
        yield
        probs, probs_low = [], []
        for b in every:
            probs.append([])
            probs_low.append([])
            for s in range(STEPS):
                halves = []
                for u in range(2):
                    tile = scores[b][64 * s : 64 * s + 64, 128 * u : 128 * u + 128]
                    raised = jnp.exp2(tile - jnp.max(tile, axis=0, keepdims=True))
                    halves.append(raised * (1.0 / jnp.sum(raised, axis=0, keepdims=True)))
                probs[b].append(halves)
                probs_low[b].append([half.astype(BF) for half in halves])
        stem_values = [value_T[b].T for b in every]
        yield
        made = []
        gap = jnp.zeros((64, 128), BF)
        for b in every:
            made.append([])
            for t in range(2):
                made[b].append([])
                for u in range(2):
                    block = jnp.concatenate(
                        [
                            jnp.concatenate([probs_low[b][2 * t][u], gap], axis=1),
                            jnp.concatenate([gap, probs_low[b][2 * t + 1][u]], axis=1),
                        ],
                        axis=0,
                    )
                    made[b][t].append(
                        mm(value_T[b][64 * u : 64 * u + 64, 128 * t : 128 * t + 128], block)
                    )
        stem_mixed = []
        for b in every:
            rows = []
            for h in range(HEADS):
                u, c = divmod(h, 4)
                row = None
                for s in range(STEPS):
                    piece = made[b][s // 2][u][
                        16 * c : 16 * c + 16, 128 * (s % 2) : 128 * (s % 2) + 128
                    ]
                    turn = (s - c) % 4
                    if turn:
                        piece = pltpu.roll(piece, 32 * turn, 1)
                    row = piece if row is None else jnp.where(at_block[s], piece, row)
                rows.append(row)
            stem_mixed.append(jnp.concatenate(rows, axis=0).astype(BF))
        yield
        both = mm(
            jnp.concatenate([s_outT[e] for e in rels], axis=1), aslant(*stem_mixed)
        )
        residual = [both[:, lanes[b]] for b in every]
        yield

        def norm(values):
            units, inverses = [], []
            for value in values:
                centered = value - jnp.mean(value, axis=0, keepdims=True)
                inverse = lax.rsqrt(
                    jnp.mean(centered * centered, axis=0, keepdims=True) + NORM_EPSILON
                )
                units.append(centered * inverse)
                inverses.append(inverse)
            low = jnp.concatenate([unit.astype(BF) for unit in units], axis=1)
            return units, inverses, jnp.concatenate([low, jnp.ones((16, low.shape[1]), BF)], axis=0)

        def norm_back(gradient, unit, inverse):
            mean_one = jnp.mean(gradient, axis=0, keepdims=True)
            mean_two = jnp.mean(gradient * unit, axis=0, keepdims=True)
            return inverse * (gradient - mean_one - unit * mean_two)

        unit_one, inverse_one, normed = norm(residual)
        yield
        projected = mm(t_qkvT[...], normed)
        query_T = [(projected[:128, lanes[b]] * (LOG2E * SCALE)).astype(BF) for b in every]
        key_T = [projected[128:256, lanes[b]].astype(BF) for b in every]
        value_T = [projected[256:, lanes[b]].astype(BF) for b in every]
        keys = [key_T[b].T for b in every]
        values = [value_T[b].T for b in every]
        hide = []
        for b in seqs:
            marks = [seg_ref[(first + b) * STEPS + s] for s in range(STEPS)]
            lane_marks = jnp.where(
                at_block[0],
                marks[0],
                jnp.where(at_block[1], marks[1], jnp.where(at_block[2], marks[2], marks[3])),
            )
            hide.append([jnp.where(lane_marks == marks[s], 0.0, HIDDEN_SCORE) for s in range(STEPS)])
        yield
        scores = [[mm(keys[b], head_pair(query_T[b], j)) for j in range(PAIRS)] for b in every]
        cot_list = [cot_ref[first + b].T for b in seqs]
        yield
        raised = []
        for b in every:
            raised.append([])
            for j in range(PAIRS):
                halves = []
                for u in range(2):
                    tile = scores[b][j][:, 128 * u : 128 * u + 128]
                    tile = jnp.concatenate(
                        [tile[32 * s : 32 * s + 32] + hide[b][s] for s in range(STEPS)], axis=0
                    )
                    halves.append(
                        jnp.exp2(tile - jnp.max(tile, axis=0, keepdims=True)).astype(BF)
                    )
                raised[b].append(jnp.concatenate(halves, axis=1))
        yield
        made = [
            [
                mm(jnp.concatenate([value_T[b][32 * j : 32 * j + 32], ones], axis=0), raised[b][j])
                for j in range(PAIRS)
            ]
            for b in every
        ]
        head_mixed, head_inverse, mixed_list = [], [], []
        for b in every:
            head_mixed.append([])
            head_inverse.append([])
            for h in range(HEADS):
                j, u = divmod(h, 2)
                here = slice(128 * u, 128 * u + 128)
                inverse = 1.0 / made[b][j][32:40, here]
                part = made[b][j][16 * u : 16 * u + 16, here]
                head_inverse[b].append(inverse)
                head_mixed[b].append(
                    jnp.concatenate([part[:8] * inverse, part[8:] * inverse], axis=0)
                )
            mixed_list.append(jnp.concatenate(head_mixed[b], axis=0).astype(BF))
        mixed = jnp.concatenate(mixed_list, axis=1)
        yield
        branch = mm(t_oT[...], mixed)
        hidden = [residual[b] + branch[:, lanes[b]] for b in every]
        yield
        unit_two, inverse_two, normed_two = norm(hidden)
        cot = jnp.concatenate(cot_list, axis=1)
        yield
        inner_all = mm(t_inT[...], normed_two)
        grad_all = mm(t_dn[...], cot)
        yield
        active_rows, grad_rows = [], []
        for r in range(0, FF, 16):
            active_cols, grad_cols = [], []
            for b in every:
                inner = inner_all[r : r + 16, lanes[b]].astype(BF)
                square = inner * inner
                bend = jnp.exp2(inner * (LOW_M0 + LOW_M1 * square))
                rise = pl.reciprocal(LOW_ONE + bend, approx=True)
                active = inner * rise
                slope = rise + (active - active * rise) * (LOW_2C0 + LOW_6C1 * square)
                active_cols.append(active)
                grad_cols.append(grad_all[r : r + 16, lanes[b]].astype(BF) * slope)
            active_rows.append(jnp.concatenate(active_cols, axis=1))
            grad_rows.append(jnp.concatenate(grad_cols, axis=1))
        active = jnp.concatenate(active_rows, axis=0)
        grad_inner = jnp.concatenate(grad_rows, axis=0)
        yield
        grad_all = mm(t_in[...], grad_inner)
        output_all = mm(t_dnT[...], active)
        turn_inner, turn_active = turn_all(grad_inner), turn_all(active)
        yield

        grad_hidden = []
        for b in every:
            grad_hidden.append(
                cot_list[b].astype(F32)
                + norm_back(grad_all[:, lanes[b]], unit_two[b], inverse_two[b])
            )
        grad_branch = jnp.concatenate([part.astype(BF) for part in grad_hidden], axis=1)
        yield
        grad_mixed = mm(t_o[...], grad_branch)
        sums = [jnp.zeros((128, 128), F32)] * 3
        for i, b in enumerate(seqs):
            output = hidden[i] + output_all[:, lanes[i]] + vecs[4]
            out_ref[first + b] = output.astype(BF).T
            sums = [
                sums[0] + cot_list[i].astype(F32),
                sums[1] + output,
                sums[2] + output * output,
            ]
        kept["sums"].append(sums)
        grad_T, drops = [], []
        for b in every:
            scaled = []
            drops.append([])
            for h in range(HEADS):
                inverse = head_inverse[b][h]
                part = grad_mixed[16 * h : 16 * h + 16, lanes[b]]
                part = jnp.concatenate([part[:8] * inverse, part[8:] * inverse], axis=0)
                scaled.append(part.astype(BF))
                drops[b].append(jnp.sum(part * head_mixed[b][h], axis=0, keepdims=True))
            grad_T.append(jnp.concatenate(scaled, axis=0))
        yield
        grad_probs = [[mm(values[b], head_pair(grad_T[b], j)) for j in range(PAIRS)] for b in every]
        grad_values = [
            [mm(pair_rows(grad_T[b], j), turn_pair(raised[b][j])) for j in range(PAIRS)] for b in every
        ]
        yield
        grad_scores = []
        for b in every:
            grad_scores.append([])
            for j in range(PAIRS):
                halves = []
                for u in range(2):
                    here = slice(128 * u, 128 * u + 128)
                    tile = grad_probs[b][j][:, here] - drops[b][2 * j + u]
                    halves.append(tile.astype(BF) * raised[b][j][:, here])
                grad_scores[b].append(jnp.concatenate(halves, axis=1))
        yield
        grad_queries = [
            [pair_pick(mm(key_T[b][32 * j : 32 * j + 32], grad_scores[b][j])) for j in range(PAIRS)]
            for b in every
        ]
        grad_keys = [
            [mm(pair_rows(query_T[b], j), turn_pair(grad_scores[b][j])) for j in range(PAIRS)] for b in every
        ]
        grad_list = []
        for b in every:
            grad_list.append(
                jnp.concatenate(
                    [
                        (jnp.concatenate(grad_queries[b], axis=0) * SCALE).astype(BF),
                        (jnp.concatenate(grad_keys[b], axis=0) * (1.0 / LOG2E)).astype(BF),
                        jnp.concatenate(grad_values[b], axis=0).astype(BF),
                    ],
                    axis=0,
                )
            )
        grad_projected = jnp.concatenate(grad_list, axis=1)
        yield
        grad_all = mm(t_qkv[...], grad_projected)
        for name, value in (
            ("normed", normed),
            ("gradp", turn_all(grad_projected)),
            ("mixed", mixed),
            ("branch", grad_branch),
            ("normed2", normed_two),
            ("inner", turn_inner),
            ("cot", cot),
            ("active", turn_active),
        ):
            kept[name].append(value)
        yield
        grad_tokens = [
            (grad_hidden[b] + norm_back(grad_all[:, lanes[b]], unit_one[b], inverse_one[b])).astype(BF)
            for b in every
        ]
        yield

        both = mm(jnp.concatenate([s_out[e] for e in rels], axis=1), aslant(*grad_tokens))
        grad_mixed = [both[:, lanes[b]] for b in every]
        both = mm(
            jnp.concatenate(stem_mixed, axis=1), aslant(*[grad.T for grad in grad_tokens])
        )
        for b in every:
            a_out[rels[b]] += both[:, lanes[b]]
        yield
        spread, tall = [], []
        for b in every:
            spread.append([])
            mixed_tok = grad_mixed[b].astype(BF).T
            tall.append(
                [
                    jnp.concatenate(
                        [mixed_tok[32 * s : 32 * s + 32] * head_lanes[h] for h in range(HEADS)],
                        axis=0,
                    )
                    for s in range(STEPS)
                ]
            )
            turned = [grad_mixed[b].astype(BF)] + [
                pltpu.roll(grad_mixed[b], 32 * k, 1).astype(BF) for k in range(1, 4)
            ]
            for s in range(STEPS):
                pieces = []
                for h in range(HEADS):
                    c = h % 4
                    piece = turned[(c - s) % 4][16 * h : 16 * h + 16] * masks[c]
                    pieces.append(
                        jnp.concatenate([piece, zero] if h < 4 else [zero, piece], axis=1)
                    )
                spread[b].append(jnp.concatenate(pieces, axis=0))
        yield
        grad_probs = [
            [mm(stem_values[b][64 * s : 64 * s + 64], spread[b][s]) for s in range(STEPS)]
            for b in every
        ]
        grad_values = [
            jnp.concatenate(
                [
                    mm(jnp.concatenate(probs_low[b][s], axis=1), tall[b][s]).astype(BF)
                    for s in range(STEPS)
                ],
                axis=0,
            )
            for b in every
        ]
        yield
        grad_scores = []
        for b in every:
            steps = []
            for s in range(STEPS):
                steps.append(
                    jnp.concatenate(
                        [
                            scores_back(probs[b][s][u], grad_probs[b][s][:, 128 * u : 128 * u + 128], 0)
                            for u in range(2)
                        ],
                        axis=1,
                    )
                )
            grad_scores.append(jnp.concatenate(steps, axis=0))
        yield
        for i, b in enumerate(seqs):
            e = rels[i]
            late_ref[first + b, :, 0:256] = grad_scores[i]
            late_ref[first + b, :, 256:384] = grad_values[i]
            rows_T = rows_ref[first + b].T
            a_a[e] += mm(rows_T, grad_scores[i])
            a_v[e] += mm(rows_T, grad_values[i])

    part = 2
    flows = [flow(range(part * g, part * g + part)) for g in range(group // part)]
    live, wave = len(flows), 0
    while live:
        live = 0
        for g, one in enumerate(flows):
            if wave < LAG * g:
                live += 1
                continue
            try:
                next(one)
                live += 1
            except StopIteration:
                pass
        wave += 1

    for move in moves(step)[2:]:
        move.start()

    def side(name):
        return jnp.concatenate(kept[name], axis=1)

    def stack(name):
        return jnp.concatenate(kept[name], axis=0)

    a_dn[...] += mm(side("cot"), stack("active"))
    a_in[...] += mm(side("normed2"), stack("inner"))
    a_o[...] += mm_nt(side("mixed"), side("branch"))
    a_qkv[...] += mm(side("normed"), stack("gradp"))
    for c in range(3):
        total = kept["sums"][0][c]
        for sums in kept["sums"][1:]:
            total = total + sums[c]
        a_vec[c] += total

    @pl.when(step == pl.num_programs(0) - 1)
    def _():
        me = lax.axis_index("emb")
        weights[0].wait()

        def exact(left, right):
            high = left.astype(BF)
            return mm(high, right) + mm((left - high.astype(F32)).astype(BF), right)

        mats = mats_ref[...].astype(BF).astype(F32)
        blocks, gains, biases = [], [None, None], [None, None]
        for c in range(8):
            if c == 3:
                blocks.append(a_o[...])
                continue
            n = 0 if c < 3 else 1
            ref, where = (a_qkv, 128 * c) if c < 3 else (a_in, 128 * (c - 4))
            summed = ref[0:128, where : where + 128]
            ones_row = jnp.broadcast_to(ref[128:129, where : where + 128], (128, 128))
            weight = mats[:, 128 * c : 128 * c + 128]
            blocks.append(summed * vecs[2 * n] + ones_row * vecs[2 * n + 1])
            gain, bias = weight * summed, weight * ones_row
            gains[n] = gain if gains[n] is None else gains[n] + gain
            biases[n] = bias if biases[n] is None else biases[n] + bias
        blocks += [a_dn[:, 128 * c : 128 * c + 128].T for c in range(4)]
        count, per = 4, len(blocks) // 4

        for j in range(count):
            place = jnp.bitwise_xor(me, j)
            for i in range(per):
                pieces[place, 128 * i : 128 * i + 128] = blocks[per * j + i]
        for k in range(count):
            here = slice(PIECE_ROWS * (k // 2), PIECE_ROWS * (k // 2) + TRUNK_ROWS)
            if k % 2:
                give_ref[here] = pieces[k].astype(BF)
            else:
                keep_ref[here] = pieces[k]
        columns = [gains[0], biases[0], gains[1], biases[1], a_vec[0]]
        sums = [jnp.sum(column.T, axis=0, keepdims=True) for column in columns]
        sums += [a_in[128:129, 128 * c : 128 * c + 128] for c in range(4)]
        sums += [jnp.sum(a_vec[c].T, axis=0, keepdims=True) for c in (1, 2)]
        sums.append(jnp.zeros((5, 128), F32))
        sums = jnp.concatenate(sums, axis=0)
        high, low = split_sum(sums)
        sums_ref[...] = sums
        give_ref[2 * PIECE_ROWS : 2 * PIECE_ROWS + 16] = high
        give_ref[2 * PIECE_ROWS + 16 : 2 * PIECE_ROWS + 32] = low
        for k, ref in enumerate((own_ref, one_ref, two_ref, three_ref)):
            block = query_block(ref)
            grad = a_a[k] * SCALE
            grad_high = grad.astype(BF)
            grad_low = (grad - grad_high.astype(F32)).astype(BF)
            key_T = ref[0:128].T
            spread = (mm(key_T, grad_high) + mm(key_T, grad_low)).T
            spread = jnp.where(head_mask, spread, 0.0)
            query = spread[0:32]
            for h in range(1, HEADS):
                query = query + spread[32 * h : 32 * h + 32]
            parts = [
                mm_nt(grad_high, block) + mm_nt(grad_low, block),
                a_v[k],
                a_out[k],
                query,
            ]
            base = PIECE_ROWS * (k // 2) + TRUNK_ROWS
            for i, value in enumerate(parts):
                here = slice(base + 128 * i, base + 128 * i + value.shape[0])
                if k % 2:
                    give_ref[here] = value.astype(BF)
                else:
                    keep_ref[here] = value
        for g in range(steps):
            for move in moves(g)[2:]:
                move.wait()


def rows_kernel(group, count, rel_ref, late_ref, *refs):
    stems, (after_ref, out_ref, done_ref, back_ref) = refs[:count], refs[count:]
    step = pl.program_id(0)

    @pl.when(step == 0)
    def _():
        for k, ref in enumerate(stems):
            both = mm(ref[0:128], query_block(ref)) * SCALE
            back_ref[k, 0:256] = both.T.astype(BF)
            back_ref[k, 256:384] = ref[128:256].T

    done_ref[...] = jnp.zeros_like(done_ref)
    for b in range(group):
        out_ref[b] = mm(late_ref[b], back_ref[rel_ref[step * group + b]]).astype(BF)


def run_rows(rel, late, stems, after, group=8):
    seqs = late.shape[0]
    flops = 2 * seqs * ROWS_SEQ * 3 * D * D
    return pl.pallas_call(
        functools.partial(rows_kernel, group, len(stems)),
        out_shape=(
            jax.ShapeDtypeStruct((seqs, ROWS_SEQ, D), BF),
            jax.ShapeDtypeStruct((8, D), F32),
        ),
        grid_spec=pltpu.PrefetchScalarGridSpec(
            num_scalar_prefetch=1,
            grid=(seqs // group,),
            in_specs=[
                pl.BlockSpec((group, ROWS_SEQ, 3 * D), lambda i, *_: (i, 0, 0)),
            ]
            + [pl.BlockSpec(stem.shape, lambda i, *_: (0, 0)) for stem in stems]
            + [pl.BlockSpec(memory_space=pl.ANY)],
            scratch_shapes=[pltpu.VMEM((len(stems), 3 * D, D), BF)],
            out_specs=(
                pl.BlockSpec((group, ROWS_SEQ, D), lambda i, *_: (i, 0, 0)),
                pl.BlockSpec((8, D), lambda i, *_: (0, 0)),
            ),
        ),
        cost_estimate=pl.CostEstimate(flops=flops, bytes_accessed=16 * 1024 * 1024, transcendentals=0),
        compiler_params=pltpu.CompilerParams(
            vmem_limit_bytes=16 * 1024 * 1024, dimension_semantics=("arbitrary",)
        ),
    )(rel, late, *stems, after)


def split_sum(sums):
    high = sums.astype(BF)
    return high, (sums - high.astype(F32)).astype(BF)


def add_sums(sums_ref, got_ref, start, next_ref, give_ref, give_start):
    total = sums_ref[...] + (
        got_ref[start : start + 16].astype(F32) + got_ref[start + 16 : start + 32].astype(F32)
    )
    next_ref[...] = total
    if give_ref is not None:
        high, low = split_sum(total)
        give_ref[give_start : give_start + 16] = high
        give_ref[give_start + 16 : give_start + 32] = low


def core_kernel(keep_ref, got_ref, sums_ref, own_ref, give_ref, next_ref):
    own_ref[...] = keep_ref[0:PIECE_ROWS] + got_ref[0:PIECE_ROWS].astype(F32)
    give_ref[0:PIECE_ROWS] = (
        keep_ref[PIECE_ROWS : 2 * PIECE_ROWS] + got_ref[PIECE_ROWS : 2 * PIECE_ROWS].astype(F32)
    ).astype(BF)
    add_sums(sums_ref, got_ref, 2 * PIECE_ROWS, next_ref, give_ref, PIECE_ROWS)


def halve_kernel(keep_ref, got_ref, sums_ref, after_ref, own_ref, give_ref, next_ref):
    odd = lax.rem(lax.axis_index("dp"), 2)
    trunk = keep_ref[0:TRUNK_ROWS] + got_ref[0:TRUNK_ROWS].astype(F32)
    stem = keep_ref[TRUNK_ROWS:] + got_ref[TRUNK_ROWS:PIECE_ROWS].astype(F32)
    rest = jnp.zeros((STEM_ROWS - TRUNK_ROWS, D), F32)
    trunk = jnp.concatenate([trunk, rest], axis=0)
    own_ref[...] = jnp.where(odd == 0, trunk, stem)
    give_ref[0:STEM_ROWS] = jnp.where(odd == 0, stem, trunk).astype(BF)
    add_sums(sums_ref, got_ref, PIECE_ROWS, next_ref, give_ref, STEM_ROWS)


def level_kernel(keep_ref, got_ref, sums_ref, own_ref, give_ref, next_ref):
    total = keep_ref[...] + got_ref[0:STEM_ROWS].astype(F32)
    own_ref[...] = total
    give_ref[0:STEM_ROWS] = total.astype(BF)
    add_sums(sums_ref, got_ref, STEM_ROWS, next_ref, give_ref, STEM_ROWS)


def last_kernel(keep_ref, got_ref, sums_ref, own_ref, next_ref):
    own_ref[...] = (keep_ref[...] + got_ref[0:STEM_ROWS].astype(F32)).astype(BF)
    add_sums(sums_ref, got_ref, STEM_ROWS, next_ref, None, 0)


def renew(weight, moment, average, gradient, step_rate):
    new_moment = MOMENTUM_DECAY * moment + gradient
    new_weight = weight - step_rate * (gradient + MOMENTUM_DECAY * new_moment)
    new_average = average + (new_weight - average) / (STEP + 1)
    return (new_moment, new_average, new_weight)


def put_new(outs, where, made):
    outs[0][where], outs[1][where], outs[2][where] = made
    if len(outs) > 3:
        outs[3][where] = made[2].astype(BF)


def renew_stem(token_total, own_ref, got_ref, sums_ref, *refs):
    stem_in, quer_in, vec_in = refs[0:3], refs[3:6], refs[6:9]
    stem_o, quer_o, vec_o, stats_o = refs[9:13], refs[13:17], refs[17:20], refs[20]
    refs[21][...] = jnp.zeros_like(refs[21])
    rate = BASE_RATE / math.sqrt(token_total)
    odd = lax.rem(lax.axis_index("dp"), 2) == 1
    full = (slice(None), slice(None))
    for i in range(3):
        where = (slice(None), slice(128 * i, 128 * i + 128))
        rows = slice(128 * i, 128 * i + 128)
        grad = jnp.where(odd, own_ref[rows].astype(F32), got_ref[rows].astype(F32))
        put_new(stem_o, where, renew(*[ref[where] for ref in stem_in], grad, rate))
    grad = jnp.where(odd, own_ref[384:416].astype(F32), got_ref[384:416].astype(F32))
    put_new(quer_o, full, renew(*[ref[...] for ref in quer_in], grad, rate))
    put_new(vec_o, full, renew(*[ref[...] for ref in vec_in], sums_ref[0:9], rate))
    mean = sums_ref[9:10] / token_total
    stats_o[0:1] = mean
    stats_o[1:2] = sums_ref[10:11] / token_total - mean * mean


def pass_kernel(in_ref, after_ref, out_ref):
    out_ref[...] = in_ref[...]


def renew_trunk(token_total, *refs):
    trunk_refs, mats_in, down_in = refs[0:4], refs[4:7], refs[7:10]
    mats_o, down_o, pieces = refs[10:14], refs[14:18], refs[18]
    rate = BASE_RATE / math.sqrt(token_total)
    for k, ref in enumerate(trunk_refs):
        pieces[jnp.bitwise_xor(lax.axis_index("emb"), k)] = ref[...].astype(F32)

    def block(i):
        return pieces[i // 3, 128 * (i % 3) : 128 * (i % 3) + 128]

    for i in range(8):
        where = (slice(None), slice(128 * i, 128 * i + 128))
        put_new(mats_o, where, renew(*[ref[where] for ref in mats_in], block(i), rate))
    for i in range(4):
        where = (slice(128 * i, 128 * i + 128), slice(None))
        put_new(down_o, where, renew(*[ref[where] for ref in down_in], block(8 + i), rate))


def vmem_call(kernel, outs, scratch=(), scalars=0, cost=None, after=0):
    in_vmem = pl.BlockSpec(memory_space=pltpu.VMEM)

    def call(*args):
        return pl.pallas_call(
            kernel,
            out_shape=outs,
            in_specs=[pl.BlockSpec(memory_space=pltpu.SMEM)] * scalars
            + [in_vmem] * (len(args) - scalars - after)
            + [pl.BlockSpec(memory_space=pl.ANY)] * after,
            out_specs=jax.tree.map(lambda _: in_vmem, outs),
            scratch_shapes=list(scratch),
            cost_estimate=cost,
            compiler_params=pltpu.CompilerParams(vmem_limit_bytes=8 * 1024 * 1024),
        )(*args)

    return call


def in_hbm(value):
    return pltpu.with_memory_space_constraint(value, pltpu.HBM)


def run_ready(mats, down, vectors, rel, segments):
    shapes = [
        ((384, 144), BF),
        ((128, 384), BF),
        ((128, 128), BF),
        ((128, 128), BF),
        ((128, 512), BF),
        ((512, 144), BF),
        ((512, 128), BF),
        ((128, 512), BF),
        ((5, 128, 128), F32),
        ((8, 128), F32),
    ]
    return vmem_call(
        ready_kernel,
        [jax.ShapeDtypeStruct(*shape) for shape in shapes],
        cost=pl.CostEstimate(flops=0, bytes_accessed=8 * 1024 * 1024, transcendentals=0),
        after=2,
    )(in_hbm(mats), in_hbm(down), in_hbm(vectors), rel, segments)


def run_main(rel, segments, rows, cot, stems, mats, ready, emb_count):
    seqs = rows.shape[0]
    group = 16
    steps = seqs // group

    def whole(shape):
        return pl.BlockSpec(shape, lambda i, *_: (0,) * len(shape))

    scratch = [
        ((4, 128, 256), BF),
        ((4, 128, 128), BF),
        ((4, 128, 128), BF),
        ((4, 128, 128), BF),
        ((144, 384), F32),
        ((128, 128), F32),
        ((144, 512), F32),
        ((128, 512), F32),
        ((3, 128, 128), F32),
        ((4, 128, 256), F32),
        ((4, 128, 128), F32),
        ((4, 128, 128), F32),
        ((4, TRUNK_ROWS, D), F32),
        ((seqs, ROWS_SEQ, D), BF),
        ((seqs, TOK_SEQ, D), BF),
        ((seqs, TOK_SEQ, D), BF),
        ((seqs, ROWS_SEQ, 3 * D), BF),
    ]
    anywhere = pl.BlockSpec(memory_space=pl.ANY)
    return pl.pallas_call(
        functools.partial(main_kernel, group),
        out_shape=(
            jax.ShapeDtypeStruct((seqs, TOK_SEQ, D), BF),
            jax.ShapeDtypeStruct((seqs, ROWS_SEQ, 3 * D), BF),
            jax.ShapeDtypeStruct((2 * PIECE_ROWS, D), F32),
            jax.ShapeDtypeStruct((2 * PIECE_ROWS + VEC_ROWS, D), BF),
            jax.ShapeDtypeStruct((16, D), F32),
        ),
        grid_spec=pltpu.PrefetchScalarGridSpec(
            num_scalar_prefetch=2,
            grid=(steps,),
            in_specs=[anywhere, anywhere]
            + [whole((STEM_ROWS, D))] * 4
            + [anywhere] * (1 + len(ready)),
            out_specs=(
                anywhere,
                anywhere,
                whole((2 * PIECE_ROWS, D)),
                whole((2 * PIECE_ROWS + VEC_ROWS, D)),
                whole((16, D)),
            ),
            scratch_shapes=[pltpu.VMEM(shape, dtype) for shape, dtype in scratch]
            + [pltpu.VMEM(mats.shape, F32)]
            + [pltpu.VMEM(value.shape, value.dtype) for value in ready]
            + [pltpu.SemaphoreType.DMA((4, steps)), pltpu.SemaphoreType.DMA((1 + len(ready),))],
        ),
        compiler_params=pltpu.CompilerParams(
            vmem_limit_bytes=VMEM_LIMIT, dimension_semantics=("arbitrary",)
        ),
    )(rel, segments, in_hbm(rows), in_hbm(cot), *stems, in_hbm(mats), *ready)


def local(
    stem_rows,
    emb_ids,
    segments,
    cotangent,
    trunk_mats,
    mats_momentum,
    mats_average,
    trunk_down,
    down_momentum,
    down_average,
    trunk_vectors,
    vectors_momentum,
    vectors_average,
    stem_mats,
    stem_momentum,
    stem_average,
    stem_queries,
    queries_momentum,
    queries_average,
):
    seqs = stem_rows.shape[0]
    emb_count, dp_count = lax.axis_size("emb"), lax.axis_size("dp")
    rel = emb_ids[:, 0] ^ lax.axis_index("emb")
    token_total = seqs * TOK_SEQ * dp_count * emb_count

    def swap(value, axis, count, mask):
        return lax.ppermute(value, axis, [(i, i ^ mask) for i in range(count)])

    own = vmem_call(own_kernel, jax.ShapeDtypeStruct((STEM_ROWS, D), BF))(
        in_hbm(stem_mats[0]), in_hbm(stem_queries[0])
    )
    segments = segments.reshape(-1)
    *ready, ready_done = run_ready(trunk_mats, trunk_down, trunk_vectors, rel, segments)
    near, far = swap(own, "emb", emb_count, 1), swap(own, "emb", emb_count, 2)
    far = vmem_call(pass_kernel, jax.ShapeDtypeStruct(far.shape, BF), after=1)(far, ready_done)
    stems = [own, near, far, swap(far, "emb", emb_count, 1)]

    output, late, keep, give, sums = run_main(
        rel,
        segments,
        stem_rows.reshape(seqs, ROWS_SEQ, D),
        cotangent,
        stems,
        trunk_mats,
        ready,
        emb_count,
    )

    f32, bf16 = F32, BF

    def shape(rows, dtype):
        return jax.ShapeDtypeStruct((rows, D), dtype)

    got = swap(give, "emb", emb_count, 1)
    own, give, sums = vmem_call(
        core_kernel, (shape(PIECE_ROWS, f32), shape(PIECE_ROWS + VEC_ROWS, bf16), shape(16, f32))
    )(keep, got, sums)
    got = swap(give, "emb", emb_count, 2)
    rows_grad, rows_done = run_rows(rel, late, stems, give)
    half = (shape(STEM_ROWS, f32), shape(STEM_ROWS + VEC_ROWS, bf16), shape(16, f32))
    own, give, sums = vmem_call(halve_kernel, half, after=1)(
        own, got, sums, rows_done
    )
    got = swap(give, "dp", dp_count, 1)
    bits = [1 << i for i in range(1, dp_count.bit_length() - 1)]
    if len(bits) == 2:
        bits[1] = bits[0] | bits[1]
    for mask in bits:
        own, give, sums = vmem_call(level_kernel, half)(own, got, sums)
        got = swap(give, "dp", dp_count, mask)
    own, sums = vmem_call(last_kernel, (shape(STEM_ROWS, bf16), shape(16, f32)))(own, got, sums)
    other = swap(own, "dp", dp_count, 1)
    trunk = jnp.where(lax.axis_index("dp") % 2 == 0, own[:TRUNK_ROWS], other[:TRUNK_ROWS])
    far = swap(trunk, "emb", emb_count, 2)
    near = swap(trunk, "emb", emb_count, 1)

    def like(array, copy):
        made = [jax.ShapeDtypeStruct(array.shape, F32)] * 3
        return made + ([jax.ShapeDtypeStruct(array.shape, BF)] if copy else [])

    stem_made = vmem_call(
        functools.partial(renew_stem, token_total),
        like(stem_mats[0], True)
        + like(stem_queries[0], True)
        + like(trunk_vectors, False)
        + [jax.ShapeDtypeStruct((2, D), F32), jax.ShapeDtypeStruct((8, D), F32)],
        cost=pl.CostEstimate(flops=0, bytes_accessed=6 * 1024 * 1024, transcendentals=0),
    )(
        own,
        other,
        sums,
        stem_mats[0],
        stem_momentum[0],
        stem_average[0],
        stem_queries[0],
        queries_momentum[0],
        queries_average[0],
        trunk_vectors,
        vectors_momentum,
        vectors_average,
    )
    far = vmem_call(pass_kernel, jax.ShapeDtypeStruct(far.shape, far.dtype), after=1)(
        far, stem_made[12]
    )
    trunks = [trunk, near, far, swap(far, "emb", emb_count, 1)]
    trunk_made = vmem_call(
        functools.partial(renew_trunk, token_total),
        like(trunk_mats, True) + like(trunk_down, True),
        [pltpu.VMEM((emb_count, TRUNK_ROWS, D), F32)],
    )(
        *trunks,
        trunk_mats,
        mats_momentum,
        mats_average,
        trunk_down,
        down_momentum,
        down_average,
    )
    stems_new = [part[None] for part in stem_made[:8]]
    return (
        output,
        rows_grad.reshape(stem_rows.shape),
        *trunk_made,
        *stem_made[8:11],
        *stems_new,
        stem_made[11],
    )


def solution(mesh):
    split = P(("dp", "emb"))
    stem = P("emb")
    in_specs = (split,) * 4 + (P(),) * 9 + (stem,) * 6
    out_specs = (split,) * 2 + (P(),) * 11 + (stem,) * 8 + (P(),)
    return jax.shard_map(local, mesh=mesh, in_specs=in_specs, out_specs=out_specs, check_vma=False)
```

```python
import functools
import math

import jax
import jax.numpy as jnp
from jax import lax
from jax.experimental import pallas as pl
from jax.experimental.pallas import tpu as pltpu
from jax.sharding import PartitionSpec as P

D = 128
FF = 512
HEADS = 8
HEAD_DIM = 16
QUERIES = 32
STEPS = 4
STEP = 4
TOK_SEQ = 128
ROWS_SEQ = 256
PAIRS = HEADS // 2

NORM_EPSILON = 1e-05
MOMENTUM_DECAY = 0.9
BASE_RATE = 0.1
HIDDEN_SCORE = -1e30
LAG = 1
FLUSH = 4
SCALE = 1.0 / math.sqrt(HEAD_DIM)
LOG2E = math.log2(math.e)

TRUNK_ROWS = 384
STEM_ROWS = 416
VEC_ROWS = 32
PIECE_ROWS = TRUNK_ROWS + STEM_ROWS

BF = jnp.bfloat16
F32 = jnp.float32
VMEM_LIMIT = 44 * 1024 * 1024


def mm(a, b):
    return lax.dot_general(a, b, (((1,), (0,)), ((), ())), preferred_element_type=F32)


def mm_nt(a, b):
    return lax.dot_general(a, b, (((1,), (1,)), ((), ())), preferred_element_type=F32)


def scores_back(probs, low, grad, axis):
    drop = jnp.sum(probs * grad, axis=axis, keepdims=True)
    return (grad - drop).astype(BF) * low


def head_pair(source, j):
    pieces = []
    if j:
        pieces.append(jnp.zeros((32 * j, 256), BF))
    zero = jnp.zeros((16, 128), BF)
    one = source[32 * j : 32 * j + 16]
    two = source[32 * j + 16 : 32 * j + 32]
    pieces.append(jnp.concatenate([one, zero], axis=1))
    pieces.append(jnp.concatenate([zero, two], axis=1))
    if j < PAIRS - 1:
        pieces.append(jnp.zeros((128 - 32 * j - 32, 256), BF))
    return jnp.concatenate(pieces, axis=0)


def pair_rows(source, j):
    zero = jnp.zeros((16, 128), BF)
    one = source[32 * j : 32 * j + 16]
    two = source[32 * j + 16 : 32 * j + 32]
    return jnp.concatenate(
        [jnp.concatenate([one, zero], axis=1), jnp.concatenate([zero, two], axis=1)], axis=0
    )


def turn_pair(both):
    return jnp.concatenate([both[:, :128].T, both[:, 128:].T], axis=0)


def turn_all(wide):
    return jnp.concatenate(
        [turn_rows(wide[:, c : c + 128]) for c in range(0, wide.shape[1], 128)], axis=0
    )


def turn_rows(tall):
    return jnp.concatenate(
        [tall[i : i + 128].T for i in range(0, tall.shape[0], 128)], axis=1
    )


def aslant(one, two):
    gap = jnp.zeros_like(one)
    return jnp.concatenate(
        [jnp.concatenate([one, gap], axis=1), jnp.concatenate([gap, two], axis=1)], axis=0
    )


def pair_pick(both):
    return jnp.concatenate([both[:16, :128], both[16:, 128:]], axis=0)


def query_block(ref):
    head_mask = (
        lax.broadcasted_iota(jnp.int32, (256, 128), 0) // 32
        == lax.broadcasted_iota(jnp.int32, (256, 128), 1) // 16
    )
    queries = ref[384:416].astype(F32)
    return jnp.where(head_mask, jnp.concatenate([queries] * HEADS, axis=0), 0.0).T.astype(BF)


def ready_kernel(
    mats_ref,
    down_ref,
    vec_ref,
    rel_ref,
    seg_ref,
    t_qkvT,
    t_qkv,
    t_o,
    t_oT,
    t_in,
    t_inT,
    t_dn,
    t_dnT,
    vecs,
    done_ref,
):
    done_ref[...] = jnp.zeros_like(done_ref)
    mats = mats_ref[...].astype(BF)
    for c in range(5):
        vecs[c] = jnp.broadcast_to(vec_ref[c : c + 1], (128, 128)).T
    corner = lax.broadcasted_iota(jnp.int32, (128, 16), 1)

    def beside(column):
        column = jnp.broadcast_to(column, (128, 16))
        high = column.astype(BF).astype(F32)
        return jnp.where(corner == 0, high, jnp.where(corner == 1, column - high, 0.0)).astype(BF)

    for c in range(7):
        where = 128 * c if c < 3 else 128 * (c + 1)
        block = mats[:, where : where + 128].astype(F32)
        gain, bias = (vecs[0], vecs[1]) if c < 3 else (vecs[2], vecs[3])
        scaled = (block * gain).astype(BF)
        shift = jnp.sum((block * bias).T, axis=1, keepdims=True)
        if c < 3:
            t_qkv[:, 128 * c : 128 * c + 128] = scaled
            t_qkvT[128 * c : 128 * c + 128, 0:128] = scaled.T
            t_qkvT[128 * c : 128 * c + 128, 128:144] = beside(shift)
        else:
            d = c - 3
            shift = shift + jnp.broadcast_to(vec_ref[5 + d : 6 + d], (128, 128)).T[:, 0:1]
            t_in[:, 128 * d : 128 * d + 128] = scaled
            t_inT[128 * d : 128 * d + 128, 0:128] = scaled.T
            t_inT[128 * d : 128 * d + 128, 128:144] = beside(shift)
    t_o[...] = mats[:, 384:512]
    t_oT[...] = mats[:, 384:512].T
    down = down_ref[...].astype(BF)
    t_dn[...] = down
    for c in range(4):
        t_dnT[:, 128 * c : 128 * c + 128] = down[128 * c : 128 * c + 128].T


def own_kernel(mats_ref, queries_ref, own_ref):
    for c in range(3):
        own_ref[128 * c : 128 * c + 128] = mats_ref[:, 128 * c : 128 * c + 128].astype(BF)
    own_ref[384:416] = queries_ref[...].astype(BF)


def main_kernel(
    group,
    rel_ref,
    seg_ref,
    rows_hbm,
    cot_hbm,
    own_ref,
    one_ref,
    two_ref,
    three_ref,
    mats_any,
    t_qkvT_any,
    t_qkv_any,
    t_o_any,
    t_oT_any,
    t_in_any,
    t_inT_any,
    t_dn_any,
    t_dnT_any,
    vecs_any,
    out_hbm,
    late_hbm,
    keep_ref,
    give_ref,
    sums_ref,
    s_a2,
    s_vT,
    s_out,
    s_outT,
    a_qkv,
    a_o,
    a_in,
    a_dn,
    a_vec,
    a_a,
    a_v,
    a_out,
    pieces,
    rows_ref,
    cot_ref,
    out_ref,
    late_ref,
    mats_ref,
    t_qkvT,
    t_qkv,
    t_o,
    t_oT,
    t_in,
    t_inT,
    t_dn,
    t_dnT,
    vecs,
    sems,
    more_sems,
):
    step = pl.program_id(0)
    ends = (
        (mats_any, mats_ref),
        (t_qkvT_any, t_qkvT),
        (t_qkv_any, t_qkv),
        (t_o_any, t_o),
        (t_oT_any, t_oT),
        (t_in_any, t_in),
        (t_inT_any, t_inT),
        (t_dn_any, t_dn),
        (t_dnT_any, t_dnT),
        (vecs_any, vecs),
    )
    weights = [
        pltpu.make_async_copy(one, two, more_sems.at[i]) for i, (one, two) in enumerate(ends)
    ]
    steps = rows_ref.shape[0] // group

    def moves(g):
        here = pl.ds(g * group, group)
        ends = (
            (rows_hbm, rows_ref),
            (cot_hbm, cot_ref),
            (out_ref, out_hbm),
            (late_ref, late_hbm),
        )
        return [
            pltpu.make_async_copy(one.at[here], two.at[here], sems.at[i, g])
            for i, (one, two) in enumerate(ends)
        ]

    @pl.when(step == 0)
    def _():
        for move in moves(0)[:2] + weights[1:]:
            move.start()
        for g in range(1, steps):
            for move in moves(g)[:2]:
                move.start()
        weights[0].start()


    head_mask = (
        lax.broadcasted_iota(jnp.int32, (256, 128), 0) // 32
        == lax.broadcasted_iota(jnp.int32, (256, 128), 1) // 16
    )

    @pl.when(step == 0)
    def _():
        for k, ref in enumerate((own_ref, one_ref, two_ref, three_ref)):
            wk, wv, wo = ref[0:128], ref[128:256], ref[256:384]
            s_a2[k] = (mm(wk, query_block(ref)) * (SCALE * LOG2E)).astype(BF)
            s_vT[k] = wv.T
            s_out[k] = wo
            s_outT[k] = wo.T
        for ref in (a_qkv, a_o, a_in, a_dn, a_vec, a_a, a_v, a_out):
            ref[...] = jnp.zeros_like(ref)
        for move in weights[1:]:
            move.wait()

    for move in moves(step)[:2]:
        move.wait()
    first = step * group
    lane_block = lax.broadcasted_iota(jnp.int32, (1, 128), 1) // 32
    ones = jnp.ones((16, 128), BF)
    zero = jnp.zeros((16, 128), BF)
    c0 = math.sqrt(2.0 / math.pi)
    c1 = c0 * 0.044715
    LOW_M0, LOW_M1, LOW_ONE, LOW_2C0, LOW_6C1 = [
        jnp.bfloat16(value)
        for value in (-2.0 * LOG2E * c0, -2.0 * LOG2E * c1, 1.0, 2.0 * c0, 6.0 * c1)
    ]
    masks = [(lane_block == c).astype(BF) for c in range(4)]
    lane_head = lax.broadcasted_iota(jnp.int32, (1, 128), 1) // 16
    head_lanes = [(lane_head == h).astype(BF) for h in range(HEADS)]
    at_block = [lane_block == c for c in range(4)]
    kept = {name: [] for name in ("normed", "gradp", "mixed", "branch", "normed2", "inner", "cot", "active", "sums")}

    def flow(seqs):
        every = range(len(seqs))
        rels = [rel_ref[first + b] for b in seqs]
        lanes = [slice(128 * b, 128 * b + 128) for b in every]
        scores = [mm(rows_ref[first + b], s_a2[e]) for b, e in zip(seqs, rels)]
        rows_T = [rows_ref[first + b].T for b in seqs]
        value_T = [mm(s_vT[e], rows_T[i]).astype(BF) for i, e in enumerate(rels)]
        yield
        probs, probs_low = [], []
        for b in every:
            probs.append([])
            probs_low.append([])
            for s in range(STEPS):
                halves = []
                for u in range(2):
                    tile = scores[b][64 * s : 64 * s + 64, 128 * u : 128 * u + 128]
                    raised = jnp.exp2(tile - jnp.max(tile, axis=0, keepdims=True))
                    halves.append(raised * (1.0 / jnp.sum(raised, axis=0, keepdims=True)))
                probs[b].append(halves)
                probs_low[b].append([half.astype(BF) for half in halves])
        stem_values = [value_T[b].T for b in every]
        yield
        made = []
        gap = jnp.zeros((64, 128), BF)
        for b in every:
            made.append([])
            for t in range(2):
                made[b].append([])
                for u in range(2):
                    block = jnp.concatenate(
                        [
                            jnp.concatenate([probs_low[b][2 * t][u], gap], axis=1),
                            jnp.concatenate([gap, probs_low[b][2 * t + 1][u]], axis=1),
                        ],
                        axis=0,
                    )
                    made[b][t].append(
                        mm(value_T[b][64 * u : 64 * u + 64, 128 * t : 128 * t + 128], block)
                    )
        stem_mixed = []
        for b in every:
            rows = []
            for h in range(HEADS):
                u, c = divmod(h, 4)
                row = None
                for s in range(STEPS):
                    piece = made[b][s // 2][u][
                        16 * c : 16 * c + 16, 128 * (s % 2) : 128 * (s % 2) + 128
                    ]
                    turn = (s - c) % 4
                    if turn:
                        piece = pltpu.roll(piece, 32 * turn, 1)
                    row = piece if row is None else jnp.where(at_block[s], piece, row)
                rows.append(row)
            stem_mixed.append(jnp.concatenate(rows, axis=0).astype(BF))
        yield
        both = mm(
            jnp.concatenate([s_outT[e] for e in rels], axis=1), aslant(*stem_mixed)
        )
        residual = [both[:, lanes[b]] for b in every]
        yield

        def norm(values):
            units, inverses = [], []
            for value in values:
                centered = value - jnp.mean(value, axis=0, keepdims=True)
                inverse = lax.rsqrt(
                    jnp.mean(centered * centered, axis=0, keepdims=True) + NORM_EPSILON
                )
                units.append(centered * inverse)
                inverses.append(inverse)
            low = jnp.concatenate([unit.astype(BF) for unit in units], axis=1)
            return units, inverses, jnp.concatenate([low, jnp.ones((16, low.shape[1]), BF)], axis=0)

        def norm_back(gradient, unit, inverse):
            mean_one = jnp.mean(gradient, axis=0, keepdims=True)
            mean_two = jnp.mean(gradient * unit, axis=0, keepdims=True)
            return inverse * (gradient - mean_one - unit * mean_two)

        unit_one, inverse_one, normed = norm(residual)
        yield
        projected = mm(t_qkvT[...], normed)
        query_T = [(projected[:128, lanes[b]] * (LOG2E * SCALE)).astype(BF) for b in every]
        key_T = [projected[128:256, lanes[b]].astype(BF) for b in every]
        value_T = [projected[256:, lanes[b]].astype(BF) for b in every]
        keys = [key_T[b].T for b in every]
        values = [value_T[b].T for b in every]
        hide = []
        for b in seqs:
            marks = [seg_ref[(first + b) * STEPS + s] for s in range(STEPS)]
            lane_marks = jnp.where(
                at_block[0],
                marks[0],
                jnp.where(at_block[1], marks[1], jnp.where(at_block[2], marks[2], marks[3])),
            )
            hide.append([jnp.where(lane_marks == marks[s], 0.0, HIDDEN_SCORE) for s in range(STEPS)])
        yield
        scores = [[mm(keys[b], head_pair(query_T[b], j)) for j in range(PAIRS)] for b in every]
        cot_list = [cot_ref[first + b].T for b in seqs]
        yield
        raised = []
        for b in every:
            raised.append([])
            for j in range(PAIRS):
                halves = []
                for u in range(2):
                    tile = scores[b][j][:, 128 * u : 128 * u + 128]
                    tile = jnp.concatenate(
                        [tile[32 * s : 32 * s + 32] + hide[b][s] for s in range(STEPS)], axis=0
                    )
                    halves.append(
                        jnp.exp2(tile - jnp.max(tile, axis=0, keepdims=True)).astype(BF)
                    )
                raised[b].append(jnp.concatenate(halves, axis=1))
        yield
        made = [
            [
                mm(jnp.concatenate([value_T[b][32 * j : 32 * j + 32], ones], axis=0), raised[b][j])
                for j in range(PAIRS)
            ]
            for b in every
        ]
        head_mixed, head_inverse, mixed_list = [], [], []
        for b in every:
            head_mixed.append([])
            head_inverse.append([])
            for h in range(HEADS):
                j, u = divmod(h, 2)
                here = slice(128 * u, 128 * u + 128)
                inverse = 1.0 / made[b][j][32:40, here]
                part = made[b][j][16 * u : 16 * u + 16, here]
                head_inverse[b].append(inverse)
                head_mixed[b].append(
                    jnp.concatenate([part[:8] * inverse, part[8:] * inverse], axis=0)
                )
            mixed_list.append(jnp.concatenate(head_mixed[b], axis=0).astype(BF))
        mixed = jnp.concatenate(mixed_list, axis=1)
        yield
        branch = mm(t_oT[...], mixed)
        hidden = [residual[b] + branch[:, lanes[b]] for b in every]
        yield
        unit_two, inverse_two, normed_two = norm(hidden)
        cot = jnp.concatenate(cot_list, axis=1)
        yield
        inner_all = mm(t_inT[...], normed_two)
        grad_all = mm(t_dn[...], cot)
        yield
        active_rows, grad_rows = [], []
        for r in range(0, FF, 16):
            active_cols, grad_cols = [], []
            for b in every:
                inner = inner_all[r : r + 16, lanes[b]].astype(BF)
                square = inner * inner
                bend = jnp.exp2(inner * (LOW_M0 + LOW_M1 * square))
                rise = pl.reciprocal(LOW_ONE + bend, approx=True)
                active = inner * rise
                slope = rise + (active - active * rise) * (LOW_2C0 + LOW_6C1 * square)
                active_cols.append(active)
                grad_cols.append(grad_all[r : r + 16, lanes[b]].astype(BF) * slope)
            active_rows.append(jnp.concatenate(active_cols, axis=1))
            grad_rows.append(jnp.concatenate(grad_cols, axis=1))
        active = jnp.concatenate(active_rows, axis=0)
        grad_inner = jnp.concatenate(grad_rows, axis=0)
        yield
        grad_all = mm(t_in[...], grad_inner)
        output_all = mm(t_dnT[...], active)
        for name, value in (
            ("normed2", normed_two),
            ("inner", turn_all(grad_inner)),
            ("cot", cot),
            ("active", turn_all(active)),
        ):
            kept[name].append(value)
        yield

        grad_hidden = []
        for b in every:
            grad_hidden.append(
                cot_list[b].astype(F32)
                + norm_back(grad_all[:, lanes[b]], unit_two[b], inverse_two[b])
            )
        grad_branch = jnp.concatenate([part.astype(BF) for part in grad_hidden], axis=1)
        yield
        grad_mixed = mm(t_o[...], grad_branch)
        sums = [jnp.zeros((128, 128), F32)] * 3
        for i, b in enumerate(seqs):
            output = hidden[i] + output_all[:, lanes[i]] + vecs[4]
            out_ref[first + b] = output.astype(BF).T
            sums = [
                sums[0] + cot_list[i].astype(F32),
                sums[1] + output,
                sums[2] + output * output,
            ]
        kept["sums"].append(sums)
        grad_T, drops = [], []
        for b in every:
            scaled = []
            drops.append([])
            for h in range(HEADS):
                inverse = head_inverse[b][h]
                part = grad_mixed[16 * h : 16 * h + 16, lanes[b]]
                part = jnp.concatenate([part[:8] * inverse, part[8:] * inverse], axis=0)
                scaled.append(part.astype(BF))
                drops[b].append(jnp.sum(part * head_mixed[b][h], axis=0, keepdims=True))
            grad_T.append(jnp.concatenate(scaled, axis=0))
        yield
        grad_probs = [[mm(values[b], head_pair(grad_T[b], j)) for j in range(PAIRS)] for b in every]
        grad_values = [
            [mm(pair_rows(grad_T[b], j), turn_pair(raised[b][j])) for j in range(PAIRS)] for b in every
        ]
        yield
        grad_scores = []
        for b in every:
            grad_scores.append([])
            for j in range(PAIRS):
                halves = []
                for u in range(2):
                    here = slice(128 * u, 128 * u + 128)
                    tile = grad_probs[b][j][:, here] - drops[b][2 * j + u]
                    halves.append(tile.astype(BF) * raised[b][j][:, here])
                grad_scores[b].append(jnp.concatenate(halves, axis=1))
        yield
        grad_queries = [
            [pair_pick(mm(key_T[b][32 * j : 32 * j + 32], grad_scores[b][j])) for j in range(PAIRS)]
            for b in every
        ]
        grad_keys = [
            [mm(pair_rows(query_T[b], j), turn_pair(grad_scores[b][j])) for j in range(PAIRS)] for b in every
        ]
        grad_list = []
        for b in every:
            grad_list.append(
                jnp.concatenate(
                    [
                        (jnp.concatenate(grad_queries[b], axis=0) * SCALE).astype(BF),
                        (jnp.concatenate(grad_keys[b], axis=0) * (1.0 / LOG2E)).astype(BF),
                        jnp.concatenate(grad_values[b], axis=0).astype(BF),
                    ],
                    axis=0,
                )
            )
        grad_projected = jnp.concatenate(grad_list, axis=1)
        yield
        grad_all = mm(t_qkv[...], grad_projected)
        for name, value in (
            ("normed", normed),
            ("gradp", turn_all(grad_projected)),
            ("mixed", mixed),
            ("branch", grad_branch),
        ):
            kept[name].append(value)
        yield
        grad_tokens = [
            (grad_hidden[b] + norm_back(grad_all[:, lanes[b]], unit_one[b], inverse_one[b])).astype(BF)
            for b in every
        ]
        yield

        both = mm(jnp.concatenate([s_out[e] for e in rels], axis=1), aslant(*grad_tokens))
        grad_mixed = [both[:, lanes[b]] for b in every]
        both = mm(
            jnp.concatenate(stem_mixed, axis=1), aslant(*[grad.T for grad in grad_tokens])
        )
        for b in every:
            a_out[rels[b]] += both[:, lanes[b]]
        yield
        spread, tall = [], []
        for b in every:
            spread.append([])
            mixed_tok = grad_mixed[b].astype(BF).T
            tall.append(
                [
                    jnp.concatenate(
                        [mixed_tok[32 * s : 32 * s + 32] * head_lanes[h] for h in range(HEADS)],
                        axis=0,
                    )
                    for s in range(STEPS)
                ]
            )
            turned = [grad_mixed[b].astype(BF)] + [
                pltpu.roll(grad_mixed[b], 32 * k, 1).astype(BF) for k in range(1, 4)
            ]
            for s in range(STEPS):
                pieces = []
                for h in range(HEADS):
                    c = h % 4
                    piece = turned[(c - s) % 4][16 * h : 16 * h + 16] * masks[c]
                    pieces.append(
                        jnp.concatenate([piece, zero] if h < 4 else [zero, piece], axis=1)
                    )
                spread[b].append(jnp.concatenate(pieces, axis=0))
        yield
        grad_probs = [
            [mm(stem_values[b][64 * s : 64 * s + 64], spread[b][s]) for s in range(STEPS)]
            for b in every
        ]
        grad_values = [
            jnp.concatenate(
                [
                    mm(jnp.concatenate(probs_low[b][s], axis=1), tall[b][s]).astype(BF)
                    for s in range(STEPS)
                ],
                axis=0,
            )
            for b in every
        ]
        yield
        grad_scores = []
        for b in every:
            steps = []
            for s in range(STEPS):
                steps.append(
                    jnp.concatenate(
                        [
                            scores_back(probs[b][s][u], probs_low[b][s][u], grad_probs[b][s][:, 128 * u : 128 * u + 128], 0)
                            for u in range(2)
                        ],
                        axis=1,
                    )
                )
            grad_scores.append(jnp.concatenate(steps, axis=0))
        yield
        for i, b in enumerate(seqs):
            e = rels[i]
            late_ref[first + b, :, 0:256] = grad_scores[i]
            late_ref[first + b, :, 256:384] = grad_values[i]
            rows_T = rows_ref[first + b].T
            a_a[e] += mm(rows_T, grad_scores[i])
            a_v[e] += mm(rows_T, grad_values[i])

    def side(name):
        return jnp.concatenate(kept[name], axis=1)

    def stack(name):
        return jnp.concatenate(kept[name], axis=0)

    def flush(least):
        if len(kept["active"]) >= least:
            a_dn[...] += mm(side("cot"), stack("active"))
            a_in[...] += mm(side("normed2"), stack("inner"))
            for name in ("cot", "active", "normed2", "inner"):
                kept[name].clear()
        if len(kept["gradp"]) >= least:
            a_o[...] += mm_nt(side("mixed"), side("branch"))
            a_qkv[...] += mm(side("normed"), stack("gradp"))
            for name in ("mixed", "branch", "normed", "gradp"):
                kept[name].clear()

    part = 2
    flows = [flow(range(part * g, part * g + part)) for g in range(group // part)]
    live, wave = len(flows), 0
    while live:
        live = 0
        for g, one in enumerate(flows):
            if wave < LAG * g:
                live += 1
                continue
            try:
                next(one)
                live += 1
            except StopIteration:
                pass
        wave += 1
        flush(FLUSH)

    for move in moves(step)[2:]:
        move.start()

    for c in range(3):
        total = kept["sums"][0][c]
        for sums in kept["sums"][1:]:
            total = total + sums[c]
        a_vec[c] += total

    @pl.when(step == pl.num_programs(0) - 1)
    def _():
        me = lax.axis_index("emb")
        weights[0].wait()

        def exact(left, right):
            high = left.astype(BF)
            return mm(high, right) + mm((left - high.astype(F32)).astype(BF), right)

        mats = mats_ref[...].astype(BF).astype(F32)
        blocks, gains, biases = [], [None, None], [None, None]
        for c in range(8):
            if c == 3:
                blocks.append(a_o[...])
                continue
            n = 0 if c < 3 else 1
            ref, where = (a_qkv, 128 * c) if c < 3 else (a_in, 128 * (c - 4))
            summed = ref[0:128, where : where + 128]
            ones_row = jnp.broadcast_to(ref[128:129, where : where + 128], (128, 128))
            weight = mats[:, 128 * c : 128 * c + 128]
            blocks.append(summed * vecs[2 * n] + ones_row * vecs[2 * n + 1])
            gain, bias = weight * summed, weight * ones_row
            gains[n] = gain if gains[n] is None else gains[n] + gain
            biases[n] = bias if biases[n] is None else biases[n] + bias
        blocks += [a_dn[:, 128 * c : 128 * c + 128].T for c in range(4)]
        count, per = 4, len(blocks) // 4

        for j in range(count):
            place = jnp.bitwise_xor(me, j)
            for i in range(per):
                pieces[place, 128 * i : 128 * i + 128] = blocks[per * j + i]
        for k in range(count):
            here = slice(PIECE_ROWS * (k // 2), PIECE_ROWS * (k // 2) + TRUNK_ROWS)
            if k % 2:
                give_ref[here] = pieces[k].astype(BF)
            else:
                keep_ref[here] = pieces[k]
        columns = [gains[0], biases[0], gains[1], biases[1], a_vec[0]]
        sums = [jnp.sum(column.T, axis=0, keepdims=True) for column in columns]
        sums += [a_in[128:129, 128 * c : 128 * c + 128] for c in range(4)]
        sums += [jnp.sum(a_vec[c].T, axis=0, keepdims=True) for c in (1, 2)]
        sums.append(jnp.zeros((5, 128), F32))
        sums = jnp.concatenate(sums, axis=0)
        high, low = split_sum(sums)
        sums_ref[...] = sums
        give_ref[2 * PIECE_ROWS : 2 * PIECE_ROWS + 16] = high
        give_ref[2 * PIECE_ROWS + 16 : 2 * PIECE_ROWS + 32] = low
        for k, ref in enumerate((own_ref, one_ref, two_ref, three_ref)):
            block = query_block(ref)
            grad = a_a[k] * SCALE
            grad_high = grad.astype(BF)
            grad_low = (grad - grad_high.astype(F32)).astype(BF)
            key_T = ref[0:128].T
            spread = (mm(key_T, grad_high) + mm(key_T, grad_low)).T
            spread = jnp.where(head_mask, spread, 0.0)
            query = spread[0:32]
            for h in range(1, HEADS):
                query = query + spread[32 * h : 32 * h + 32]
            parts = [
                mm_nt(grad_high, block) + mm_nt(grad_low, block),
                a_v[k],
                a_out[k],
                query,
            ]
            base = PIECE_ROWS * (k // 2) + TRUNK_ROWS
            for i, value in enumerate(parts):
                here = slice(base + 128 * i, base + 128 * i + value.shape[0])
                if k % 2:
                    give_ref[here] = value.astype(BF)
                else:
                    keep_ref[here] = value
        for g in range(steps):
            for move in moves(g)[2:]:
                move.wait()


def rows_kernel(group, count, rel_ref, late_ref, *refs):
    stems, (after_ref, out_ref, done_ref, back_ref) = refs[:count], refs[count:]
    step = pl.program_id(0)

    @pl.when(step == 0)
    def _():
        for k, ref in enumerate(stems):
            both = mm(ref[0:128], query_block(ref)) * SCALE
            back_ref[k, 0:256] = both.T.astype(BF)
            back_ref[k, 256:384] = ref[128:256].T

    done_ref[...] = jnp.zeros_like(done_ref)
    for b in range(group):
        out_ref[b] = mm(late_ref[b], back_ref[rel_ref[step * group + b]]).astype(BF)


def run_rows(rel, late, stems, after, group=8):
    seqs = late.shape[0]
    flops = 2 * seqs * ROWS_SEQ * 3 * D * D
    return pl.pallas_call(
        functools.partial(rows_kernel, group, len(stems)),
        out_shape=(
            jax.ShapeDtypeStruct((seqs, ROWS_SEQ, D), BF),
            jax.ShapeDtypeStruct((8, D), F32),
        ),
        grid_spec=pltpu.PrefetchScalarGridSpec(
            num_scalar_prefetch=1,
            grid=(seqs // group,),
            in_specs=[
                pl.BlockSpec((group, ROWS_SEQ, 3 * D), lambda i, *_: (i, 0, 0)),
            ]
            + [pl.BlockSpec(stem.shape, lambda i, *_: (0, 0)) for stem in stems]
            + [pl.BlockSpec(memory_space=pl.ANY)],
            scratch_shapes=[pltpu.VMEM((len(stems), 3 * D, D), BF)],
            out_specs=(
                pl.BlockSpec((group, ROWS_SEQ, D), lambda i, *_: (i, 0, 0)),
                pl.BlockSpec((8, D), lambda i, *_: (0, 0)),
            ),
        ),
        cost_estimate=pl.CostEstimate(flops=flops, bytes_accessed=16 * 1024 * 1024, transcendentals=0),
        compiler_params=pltpu.CompilerParams(
            vmem_limit_bytes=16 * 1024 * 1024, dimension_semantics=("arbitrary",)
        ),
    )(rel, late, *stems, after)


def split_sum(sums):
    high = sums.astype(BF)
    return high, (sums - high.astype(F32)).astype(BF)


def add_sums(sums_ref, got_ref, start, next_ref, give_ref, give_start):
    total = sums_ref[...] + (
        got_ref[start : start + 16].astype(F32) + got_ref[start + 16 : start + 32].astype(F32)
    )
    next_ref[...] = total
    if give_ref is not None:
        high, low = split_sum(total)
        give_ref[give_start : give_start + 16] = high
        give_ref[give_start + 16 : give_start + 32] = low


def core_kernel(keep_ref, got_ref, sums_ref, own_ref, give_ref, next_ref):
    own_ref[...] = keep_ref[0:PIECE_ROWS] + got_ref[0:PIECE_ROWS].astype(F32)
    give_ref[0:PIECE_ROWS] = (
        keep_ref[PIECE_ROWS : 2 * PIECE_ROWS] + got_ref[PIECE_ROWS : 2 * PIECE_ROWS].astype(F32)
    ).astype(BF)
    add_sums(sums_ref, got_ref, 2 * PIECE_ROWS, next_ref, give_ref, PIECE_ROWS)


def halve_kernel(keep_ref, got_ref, sums_ref, after_ref, own_ref, give_ref, next_ref):
    odd = lax.rem(lax.axis_index("dp"), 2)
    trunk = keep_ref[0:TRUNK_ROWS] + got_ref[0:TRUNK_ROWS].astype(F32)
    stem = keep_ref[TRUNK_ROWS:] + got_ref[TRUNK_ROWS:PIECE_ROWS].astype(F32)
    rest = jnp.zeros((STEM_ROWS - TRUNK_ROWS, D), F32)
    trunk = jnp.concatenate([trunk, rest], axis=0)
    own_ref[...] = jnp.where(odd == 0, trunk, stem)
    give_ref[0:STEM_ROWS] = jnp.where(odd == 0, stem, trunk).astype(BF)
    add_sums(sums_ref, got_ref, PIECE_ROWS, next_ref, give_ref, STEM_ROWS)


def level_kernel(keep_ref, got_ref, sums_ref, own_ref, give_ref, next_ref):
    total = keep_ref[...] + got_ref[0:STEM_ROWS].astype(F32)
    own_ref[...] = total
    give_ref[0:STEM_ROWS] = total.astype(BF)
    add_sums(sums_ref, got_ref, STEM_ROWS, next_ref, give_ref, STEM_ROWS)


def last_kernel(keep_ref, got_ref, sums_ref, own_ref, next_ref):
    own_ref[...] = (keep_ref[...] + got_ref[0:STEM_ROWS].astype(F32)).astype(BF)
    add_sums(sums_ref, got_ref, STEM_ROWS, next_ref, None, 0)


def renew(weight, moment, average, gradient, step_rate):
    new_moment = MOMENTUM_DECAY * moment + gradient
    new_weight = weight - step_rate * (gradient + MOMENTUM_DECAY * new_moment)
    new_average = average + (new_weight - average) / (STEP + 1)
    return (new_moment, new_average, new_weight)


def put_new(outs, where, made):
    outs[0][where], outs[1][where], outs[2][where] = made
    if len(outs) > 3:
        outs[3][where] = made[2].astype(BF)


def renew_stem(token_total, own_ref, got_ref, sums_ref, *refs):
    stem_in, quer_in, vec_in = refs[0:3], refs[3:6], refs[6:9]
    stem_o, quer_o, vec_o, stats_o = refs[9:13], refs[13:17], refs[17:20], refs[20]
    refs[21][...] = jnp.zeros_like(refs[21])
    rate = BASE_RATE / math.sqrt(token_total)
    odd = lax.rem(lax.axis_index("dp"), 2) == 1
    full = (slice(None), slice(None))
    for i in range(3):
        where = (slice(None), slice(128 * i, 128 * i + 128))
        rows = slice(128 * i, 128 * i + 128)
        grad = jnp.where(odd, own_ref[rows].astype(F32), got_ref[rows].astype(F32))
        put_new(stem_o, where, renew(*[ref[where] for ref in stem_in], grad, rate))
    grad = jnp.where(odd, own_ref[384:416].astype(F32), got_ref[384:416].astype(F32))
    put_new(quer_o, full, renew(*[ref[...] for ref in quer_in], grad, rate))
    put_new(vec_o, full, renew(*[ref[...] for ref in vec_in], sums_ref[0:9], rate))
    mean = sums_ref[9:10] / token_total
    stats_o[0:1] = mean
    stats_o[1:2] = sums_ref[10:11] / token_total - mean * mean


def pass_kernel(in_ref, after_ref, out_ref):
    out_ref[...] = in_ref[...]


def renew_trunk(token_total, *refs):
    trunk_refs, mats_in, down_in = refs[0:4], refs[4:7], refs[7:10]
    mats_o, down_o, pieces = refs[10:14], refs[14:18], refs[18]
    rate = BASE_RATE / math.sqrt(token_total)
    for k, ref in enumerate(trunk_refs):
        pieces[jnp.bitwise_xor(lax.axis_index("emb"), k)] = ref[...].astype(F32)

    def block(i):
        return pieces[i // 3, 128 * (i % 3) : 128 * (i % 3) + 128]

    for i in range(8):
        where = (slice(None), slice(128 * i, 128 * i + 128))
        put_new(mats_o, where, renew(*[ref[where] for ref in mats_in], block(i), rate))
    for i in range(4):
        where = (slice(128 * i, 128 * i + 128), slice(None))
        put_new(down_o, where, renew(*[ref[where] for ref in down_in], block(8 + i), rate))


def vmem_call(kernel, outs, scratch=(), scalars=0, cost=None, after=0):
    in_vmem = pl.BlockSpec(memory_space=pltpu.VMEM)

    def call(*args):
        return pl.pallas_call(
            kernel,
            out_shape=outs,
            in_specs=[pl.BlockSpec(memory_space=pltpu.SMEM)] * scalars
            + [in_vmem] * (len(args) - scalars - after)
            + [pl.BlockSpec(memory_space=pl.ANY)] * after,
            out_specs=jax.tree.map(lambda _: in_vmem, outs),
            scratch_shapes=list(scratch),
            cost_estimate=cost,
            compiler_params=pltpu.CompilerParams(vmem_limit_bytes=8 * 1024 * 1024),
        )(*args)

    return call


def in_hbm(value):
    return pltpu.with_memory_space_constraint(value, pltpu.HBM)


def run_ready(mats, down, vectors, rel, segments):
    shapes = [
        ((384, 144), BF),
        ((128, 384), BF),
        ((128, 128), BF),
        ((128, 128), BF),
        ((128, 512), BF),
        ((512, 144), BF),
        ((512, 128), BF),
        ((128, 512), BF),
        ((5, 128, 128), F32),
        ((8, 128), F32),
    ]
    return vmem_call(
        ready_kernel,
        [jax.ShapeDtypeStruct(*shape) for shape in shapes],
        cost=pl.CostEstimate(flops=0, bytes_accessed=8 * 1024 * 1024, transcendentals=0),
        after=2,
    )(in_hbm(mats), in_hbm(down), in_hbm(vectors), rel, segments)


def run_main(rel, segments, rows, cot, stems, mats, ready, emb_count):
    seqs = rows.shape[0]
    group = 16
    steps = seqs // group

    def whole(shape):
        return pl.BlockSpec(shape, lambda i, *_: (0,) * len(shape))

    scratch = [
        ((4, 128, 256), BF),
        ((4, 128, 128), BF),
        ((4, 128, 128), BF),
        ((4, 128, 128), BF),
        ((144, 384), F32),
        ((128, 128), F32),
        ((144, 512), F32),
        ((128, 512), F32),
        ((3, 128, 128), F32),
        ((4, 128, 256), F32),
        ((4, 128, 128), F32),
        ((4, 128, 128), F32),
        ((4, TRUNK_ROWS, D), F32),
        ((seqs, ROWS_SEQ, D), BF),
        ((seqs, TOK_SEQ, D), BF),
        ((seqs, TOK_SEQ, D), BF),
        ((seqs, ROWS_SEQ, 3 * D), BF),
    ]
    anywhere = pl.BlockSpec(memory_space=pl.ANY)
    return pl.pallas_call(
        functools.partial(main_kernel, group),
        out_shape=(
            jax.ShapeDtypeStruct((seqs, TOK_SEQ, D), BF),
            jax.ShapeDtypeStruct((seqs, ROWS_SEQ, 3 * D), BF),
            jax.ShapeDtypeStruct((2 * PIECE_ROWS, D), F32),
            jax.ShapeDtypeStruct((2 * PIECE_ROWS + VEC_ROWS, D), BF),
            jax.ShapeDtypeStruct((16, D), F32),
        ),
        grid_spec=pltpu.PrefetchScalarGridSpec(
            num_scalar_prefetch=2,
            grid=(steps,),
            in_specs=[anywhere, anywhere]
            + [whole((STEM_ROWS, D))] * 4
            + [anywhere] * (1 + len(ready)),
            out_specs=(
                anywhere,
                anywhere,
                whole((2 * PIECE_ROWS, D)),
                whole((2 * PIECE_ROWS + VEC_ROWS, D)),
                whole((16, D)),
            ),
            scratch_shapes=[pltpu.VMEM(shape, dtype) for shape, dtype in scratch]
            + [pltpu.VMEM(mats.shape, F32)]
            + [pltpu.VMEM(value.shape, value.dtype) for value in ready]
            + [pltpu.SemaphoreType.DMA((4, steps)), pltpu.SemaphoreType.DMA((1 + len(ready),))],
        ),
        compiler_params=pltpu.CompilerParams(
            vmem_limit_bytes=VMEM_LIMIT, dimension_semantics=("arbitrary",)
        ),
    )(rel, segments, in_hbm(rows), in_hbm(cot), *stems, in_hbm(mats), *ready)


def local(
    stem_rows,
    emb_ids,
    segments,
    cotangent,
    trunk_mats,
    mats_momentum,
    mats_average,
    trunk_down,
    down_momentum,
    down_average,
    trunk_vectors,
    vectors_momentum,
    vectors_average,
    stem_mats,
    stem_momentum,
    stem_average,
    stem_queries,
    queries_momentum,
    queries_average,
):
    seqs = stem_rows.shape[0]
    emb_count, dp_count = lax.axis_size("emb"), lax.axis_size("dp")
    rel = emb_ids[:, 0] ^ lax.axis_index("emb")
    token_total = seqs * TOK_SEQ * dp_count * emb_count

    def swap(value, axis, count, mask):
        return lax.ppermute(value, axis, [(i, i ^ mask) for i in range(count)])

    own = vmem_call(own_kernel, jax.ShapeDtypeStruct((STEM_ROWS, D), BF))(
        in_hbm(stem_mats[0]), in_hbm(stem_queries[0])
    )
    segments = segments.reshape(-1)
    *ready, ready_done = run_ready(trunk_mats, trunk_down, trunk_vectors, rel, segments)
    near, far = swap(own, "emb", emb_count, 1), swap(own, "emb", emb_count, 2)
    far = vmem_call(pass_kernel, jax.ShapeDtypeStruct(far.shape, BF), after=1)(far, ready_done)
    stems = [own, near, far, swap(far, "emb", emb_count, 1)]

    output, late, keep, give, sums = run_main(
        rel,
        segments,
        stem_rows.reshape(seqs, ROWS_SEQ, D),
        cotangent,
        stems,
        trunk_mats,
        ready,
        emb_count,
    )

    f32, bf16 = F32, BF

    def shape(rows, dtype):
        return jax.ShapeDtypeStruct((rows, D), dtype)

    got = swap(give, "emb", emb_count, 1)
    own, give, sums = vmem_call(
        core_kernel, (shape(PIECE_ROWS, f32), shape(PIECE_ROWS + VEC_ROWS, bf16), shape(16, f32))
    )(keep, got, sums)
    got = swap(give, "emb", emb_count, 2)
    rows_grad, rows_done = run_rows(rel, late, stems, give)
    half = (shape(STEM_ROWS, f32), shape(STEM_ROWS + VEC_ROWS, bf16), shape(16, f32))
    own, give, sums = vmem_call(halve_kernel, half, after=1)(
        own, got, sums, rows_done
    )
    got = swap(give, "dp", dp_count, 1)
    bits = [1 << i for i in range(1, dp_count.bit_length() - 1)]
    if len(bits) == 2:
        bits[1] = bits[0] | bits[1]
    for mask in bits:
        own, give, sums = vmem_call(level_kernel, half)(own, got, sums)
        got = swap(give, "dp", dp_count, mask)
    own, sums = vmem_call(last_kernel, (shape(STEM_ROWS, bf16), shape(16, f32)))(own, got, sums)
    other = swap(own, "dp", dp_count, 1)
    trunk = jnp.where(lax.axis_index("dp") % 2 == 0, own[:TRUNK_ROWS], other[:TRUNK_ROWS])
    far = swap(trunk, "emb", emb_count, 2)
    near = swap(trunk, "emb", emb_count, 1)

    def like(array, copy):
        made = [jax.ShapeDtypeStruct(array.shape, F32)] * 3
        return made + ([jax.ShapeDtypeStruct(array.shape, BF)] if copy else [])

    stem_made = vmem_call(
        functools.partial(renew_stem, token_total),
        like(stem_mats[0], True)
        + like(stem_queries[0], True)
        + like(trunk_vectors, False)
        + [jax.ShapeDtypeStruct((2, D), F32), jax.ShapeDtypeStruct((8, D), F32)],
        cost=pl.CostEstimate(flops=0, bytes_accessed=6 * 1024 * 1024, transcendentals=0),
    )(
        own,
        other,
        sums,
        stem_mats[0],
        stem_momentum[0],
        stem_average[0],
        stem_queries[0],
        queries_momentum[0],
        queries_average[0],
        trunk_vectors,
        vectors_momentum,
        vectors_average,
    )
    far = vmem_call(pass_kernel, jax.ShapeDtypeStruct(far.shape, far.dtype), after=1)(
        far, stem_made[12]
    )
    trunks = [trunk, near, far, swap(far, "emb", emb_count, 1)]
    trunk_made = vmem_call(
        functools.partial(renew_trunk, token_total),
        like(trunk_mats, True) + like(trunk_down, True),
        [pltpu.VMEM((emb_count, TRUNK_ROWS, D), F32)],
    )(
        *trunks,
        trunk_mats,
        mats_momentum,
        mats_average,
        trunk_down,
        down_momentum,
        down_average,
    )
    stems_new = [part[None] for part in stem_made[:8]]
    return (
        output,
        rows_grad.reshape(stem_rows.shape),
        *trunk_made,
        *stem_made[8:11],
        *stems_new,
        stem_made[11],
    )


def solution(mesh):
    split = P(("dp", "emb"))
    stem = P("emb")
    in_specs = (split,) * 4 + (P(),) * 9 + (stem,) * 6
    out_specs = (split,) * 2 + (P(),) * 11 + (stem,) * 8 + (P(),)
    return jax.shard_map(local, mesh=mesh, in_specs=in_specs, out_specs=out_specs, check_vma=False)
```
